256 devices in a mesh: seq: 128 (over y, x, z), head: 2 (over core).
Axes of the slice: x: 4, y: 4, z: 8, core: 2. Of those that a mesh axis runs over, the one named last changes fastest.
Arguments:
- queries: bfloat16 [16384, 1024], P('seq', 'head'), as said below
- keys: bfloat16 [16384, 1024], P('seq', 'head'), as said below
- values: bfloat16 [16384, 1024], P('seq', 'head'), may hold values from -6 to 6
- grad_y: bfloat16 [16384, 2048], P('seq', 'head'), may hold values from -6 to 6
- out_weight: bfloat16 [1024, 2048], P('head'), may hold values from -0.125 to 0.125
- bar_start: int32 [1024], P('seq'), may hold values from 0 to 16382, as said below
- related: int32 [1024, 8], P('seq'), may hold values from -1 to 1022, as said below
- bar_summary_token: int32 [1024], P('seq'), may hold values from 0 to 16383, as said below
Outputs:
- grad_queries: bfloat16 [16384, 1024], P('seq', 'head')
- grad_keys: bfloat16 [16384, 1024], P('seq', 'head')
- values_gradient: bfloat16 [16384, 1024], P('seq', 'head')
The draws below stay inside these ranges and needn't reach their ends.
Inputs may be any that keep to these rules, and one draw needn't show every extreme that they name: `bar_start`: bar 8 * i starts at token i * 128, so each shard of 128 tokens holds 8 whole bars; starts rise and are even, every bar has 2 tokens or more, and the last bar of each shard has exactly 2. `related`: entry j of bar b's list is b - o_j or -1, with o = 1, 2, 4, 8, 12, 16, 24, 32; it is -1 wherever b - o_j < 0, and entry 0 is b - 1 for every b >= 1. `bar_summary_token`: a token of bar c; bar 0 is summarized by token 0 and the last bar by token 16383. `queries`: real-valued, of order one. `keys`: real-valued, of order one.
All inputs are finite; a program needn't handle non-finite values.
Results may differ from the reference program's by a relative error of at most 0.0083.
Values may be sent and summed in bfloat16 or wider, within the bound.
No kernel may reach another device: no remote copies, remote signals or barrier semaphores. Data moves between devices by JAX's collectives and lax.ppermute only.
A program may use at most 64 MiB of HBM per device.

```python
import jax
import jax.numpy as jnp
from jax import lax

D = 2048
HEADS = 8
HD = 128
OFFSETS = 8
BAR_DEV = 8
TOKENS_PER_PART = 128
REACH = 4
TOKENS = 16384
BARS = 1024
FEATURE_TOTAL = 1024
N_SEQ = 128


def bar_layout(key):
    key = jax.random.fold_in(key, 100)
    device_keys = jax.random.split(key, N_SEQ)

    def one_shard(shard_key):
        picks = jax.random.permutation(shard_key, TOKENS_PER_PART // 2 - 2)[:BAR_DEV - 2] + 1
        last = jnp.full((1,), TOKENS_PER_PART // 2 - 1, jnp.int32)
        inner = jnp.concatenate([jnp.sort(picks).astype(jnp.int32), last])
        return jnp.concatenate([jnp.zeros((1,), jnp.int32), inner * 2])
    starts = jax.vmap(one_shard)(device_keys) + (jnp.arange(N_SEQ, dtype=jnp.int32) * TOKENS_PER_PART)[:, None]
    return starts.reshape(-1).astype(jnp.int32)


def draw_bar_start(key, part):
    return bar_layout(key)


def draw_bar_summary_token(key, part):
    starts = bar_layout(key)
    key = jax.random.fold_in(key, 2)
    ends = jnp.concatenate([starts[1:], jnp.full((1,), TOKENS, jnp.int32)])
    slots = (starts + jax.random.randint(key, (BARS,), 0, ends - starts)).astype(jnp.int32)
    return slots.at[0].set(0).at[BARS - 1].set(TOKENS - 1).astype(jnp.int32)


def draw_related(key, part):
    key = jax.random.fold_in(key, 3)
    offsets = jnp.array([1, 2, 4, 8, 12, 16, 24, 32], jnp.int32)
    earlier = jnp.arange(BARS, dtype=jnp.int32)[:, None] - offsets[None, :]
    keep = jax.random.randint(key, (BARS, OFFSETS), 0, 4) > 0
    keep = keep.at[:, 0].set(True)
    return jnp.where(keep & (earlier >= 0), earlier, -1).astype(jnp.int32)


def draw_queries(key, part):
    key = jax.random.fold_in(key, 4)
    drawn = jnp.clip(jax.random.normal(key, (TOKENS, FEATURE_TOTAL), jnp.float32), -6.0, 6.0)
    return drawn.astype(jnp.bfloat16)


def draw_keys(key, part):
    key = jax.random.fold_in(key, 5)
    drawn = jnp.clip(jax.random.normal(key, (TOKENS, FEATURE_TOTAL), jnp.float32), -6.0, 6.0)
    return drawn.astype(jnp.bfloat16)


def block_levels(own_key, shape, cuts, low, largest):
    factor_of, own = 1.0, jax.random.fold_in(own_key, 6)
    for dim, blocks in cuts:
        steps = jnp.exp(jax.random.uniform(jax.random.fold_in(own, dim), (blocks,), jnp.float32, low / len(cuts), largest / len(cuts)))
        factor_of = factor_of * jnp.repeat(steps, shape[dim] // blocks).reshape([-1 if axis == dim else 1 for axis in range(len(shape))])
    return factor_of


def scatter_about(rng, shape, spread, bound, cuts=(), held_as=jnp.bfloat16):
    level = block_levels(rng, shape, cuts, -0.22, 0.18) if cuts else 1.0
    values = jax.random.normal(rng, shape, jnp.float32) * spread * level
    return jnp.minimum(jnp.maximum(values, -bound), bound).astype(held_as)


def setup_inputs(seed: int = 0) -> dict:
    key_of = jax.random.split(jax.random.key(seed), 9)
    return {
        "queries": draw_queries(jax.random.fold_in(key_of[8], 71), 0),
        "keys": draw_keys(jax.random.fold_in(key_of[8], 71), 0),
        "values": scatter_about(key_of[2], (TOKENS, FEATURE_TOTAL), 1.0, 6.0, ((0, 128), (1, 2))),
        "grad_y": scatter_about(key_of[3], (TOKENS, D), 1.0, 6.0, ((0, 128), (1, 2))),
        "out_weight": scatter_about(key_of[4], (FEATURE_TOTAL, D), D ** -0.5, 0.125, ((0, 2),)),
        "bar_start": draw_bar_start(jax.random.fold_in(key_of[8], 71), 0),
        "related": draw_related(jax.random.fold_in(key_of[8], 71), 0),
        "bar_summary_token": draw_bar_summary_token(jax.random.fold_in(key_of[8], 71), 0),
    }


def attend_block(query_rows, key_rows, value_rows, grad_rows, allowed):
    score_scale = HD ** -0.5
    scores = score_scale * jnp.einsum("thd,khd->htk", query_rows, key_rows)
    top = jnp.max(jnp.where(allowed[None], scores, -jnp.inf), axis=-1, keepdims=True)
    weights = jnp.where(allowed[None], jnp.exp(scores - top), 0.0)
    probs = weights / jnp.sum(weights, axis=-1, keepdims=True)
    probs_low = lax.optimization_barrier(probs.astype(jnp.bfloat16)).astype(jnp.float32)
    attended = jnp.einsum("htk,khd->thd", probs_low, value_rows)
    delta = jnp.transpose(jnp.sum(grad_rows * attended, axis=-1))[:, :, None]
    dprobs = jnp.einsum("thd,khd->htk", grad_rows, value_rows)
    dscores = probs * (dprobs - delta)
    dscores_low = lax.optimization_barrier(dscores.astype(jnp.bfloat16)).astype(jnp.float32)
    query_gradient = score_scale * jnp.einsum("htk,khd->thd", dscores_low, key_rows)
    grad_k = score_scale * jnp.einsum("htk,thd->khd", dscores_low, query_rows)
    value_gradient = jnp.einsum("htk,thd->khd", probs_low, grad_rows)
    return query_gradient, grad_k, value_gradient


def reference(queries, keys, values, grad_y, out_weight, bar_start, related, bar_summary_token):
    grad_out = jnp.dot(grad_y, out_weight.T, preferred_element_type=jnp.float32).astype(jnp.bfloat16)
    marks = jnp.zeros((TOKENS,), jnp.int32).at[bar_start].add(1)
    bar_of = (jnp.cumsum(marks) - 1).astype(jnp.int32)
    window_margin = REACH * TOKENS_PER_PART
    local_window = (REACH + 1) * TOKENS_PER_PART
    key_pad = jnp.concatenate([jnp.zeros((window_margin, FEATURE_TOTAL), jnp.bfloat16), keys], axis=0)
    value_pad = jnp.concatenate([jnp.zeros((window_margin, FEATURE_TOTAL), jnp.bfloat16), values], axis=0)
    bar_pad = jnp.concatenate([jnp.full((window_margin,), -2, jnp.int32), bar_of])
    sum_keys = keys[bar_summary_token]
    sum_values = values[bar_summary_token]
    all_bars = jnp.arange(BARS, dtype=jnp.int32)
    rel_all = jnp.any(related[:, :, None] == all_bars[None, None, :], axis=1)
    coarse_bar = (all_bars[None, :] < all_bars[:, None]) & jnp.logical_not(rel_all)

    def as_heads(rows):
        return rows.astype(jnp.float32).reshape(rows.shape[0], HEADS, HD)

    def block(loop_carry, index):
        key_gradient_running, value_gradient_running, summed_key_running, summed_value_running = loop_carry
        start = (index * TOKENS_PER_PART).astype(jnp.int32)
        query_rows = lax.dynamic_slice_in_dim(queries, start, TOKENS_PER_PART, 0)
        grad_rows = lax.dynamic_slice_in_dim(grad_out, start, TOKENS_PER_PART, 0)
        win_keys = lax.dynamic_slice_in_dim(key_pad, start, local_window, 0)
        win_values = lax.dynamic_slice_in_dim(value_pad, start, local_window, 0)
        query_bar = lax.dynamic_slice_in_dim(bar_of, start, TOKENS_PER_PART, 0)
        key_bar = lax.dynamic_slice_in_dim(bar_pad, start, local_window, 0)
        query_pos = start + jnp.arange(TOKENS_PER_PART, dtype=jnp.int32)
        key_pos = start - window_margin + jnp.arange(local_window, dtype=jnp.int32)
        rel_rows = related[query_bar]
        fine = ((key_bar[None, :] == query_bar[:, None]) & (key_pos[None, :] <= query_pos[:, None])) | jnp.any(rel_rows[:, :, None] == key_bar[None, None, :], axis=1)
        coarse = coarse_bar[query_bar]
        allowed = jnp.concatenate([fine, coarse], axis=1)
        key_rows = jnp.concatenate([win_keys, sum_keys], axis=0)
        value_rows = jnp.concatenate([win_values, sum_values], axis=0)
        query_gradient, grad_k, value_gradient = attend_block(as_heads(query_rows), as_heads(key_rows), as_heads(value_rows), as_heads(grad_rows), allowed)
        grad_k = grad_k.reshape(-1, FEATURE_TOTAL)
        value_gradient = value_gradient.reshape(-1, FEATURE_TOTAL)
        key_gradient_running = lax.dynamic_update_slice_in_dim(key_gradient_running, lax.dynamic_slice_in_dim(key_gradient_running, start, local_window, 0) + grad_k[:local_window], start, 0)
        value_gradient_running = lax.dynamic_update_slice_in_dim(value_gradient_running, lax.dynamic_slice_in_dim(value_gradient_running, start, local_window, 0) + value_gradient[:local_window], start, 0)
        summed_key_running = summed_key_running + grad_k[local_window:]
        summed_value_running = summed_value_running + value_gradient[local_window:]
        return (key_gradient_running, value_gradient_running, summed_key_running, summed_value_running), query_gradient.reshape(TOKENS_PER_PART, FEATURE_TOTAL).astype(jnp.bfloat16)

    init = (jnp.zeros((TOKENS + window_margin, FEATURE_TOTAL), jnp.float32), jnp.zeros((TOKENS + window_margin, FEATURE_TOTAL), jnp.float32), jnp.zeros((BARS, FEATURE_TOTAL), jnp.float32), jnp.zeros((BARS, FEATURE_TOTAL), jnp.float32))
    final_result, grad_blocks = lax.scan(block, init, jnp.arange(TOKENS // TOKENS_PER_PART, dtype=jnp.int32))
    key_gradient_running, value_gradient_running, summed_key_running, summed_value_running = final_result
    grad_keys = key_gradient_running[window_margin:].at[bar_summary_token].add(summed_key_running)
    values_gradient = value_gradient_running[window_margin:].at[bar_summary_token].add(summed_value_running)
    return grad_blocks.reshape(TOKENS, FEATURE_TOTAL), grad_keys.astype(jnp.bfloat16), values_gradient.astype(jnp.bfloat16)
```

```python
import math

import jax
import jax.numpy as jnp
from jax import lax
from jax.experimental import pallas as pl
from jax.experimental.pallas import tpu as pltpu
from jax.sharding import PartitionSpec as P

HD = 128
REACH = 4
TOK = 128
BARS_HERE = 8
HEADS_HERE = 4
FEAT = HD * HEADS_HERE
META = 16
NZ = 8
NXY = 16
N_SEQ = NZ * NXY
WINDOW = (REACH + 1) * TOK
BARS = N_SEQ * BARS_HERE
KEYS_ALL = WINDOW + BARS
SCALE = HD ** (-0.5)
EXP_SCALE = SCALE * math.log2(math.e)

Z_GROUPS = [[j * NZ + z for z in range(NZ)] for j in range(NXY)]
XY_GROUPS = [[j * NZ + z for j in range(NXY)] for z in range(NZ)]

VMEM_LIMIT = 50 * 2**20
SMEM = pltpu.SMEM
VMEM = pltpu.VMEM


def shift(block, distance):
    route = [(i, i + distance) for i in range(N_SEQ) if 0 <= i + distance < N_SEQ]
    return lax.ppermute(block, "seq", route)


def local_bar(starts, positions):
    count = jnp.zeros_like(positions)
    for b in range(1, BARS_HERE):
        count = count + (positions >= starts[b]).astype(jnp.int32)
    return count


def pack_kernel(starts, slots, keys, values, payload, sums):
    base = starts[0]
    payload[0:TOK, :] = keys[...]
    payload[TOK : 2 * TOK, :] = values[...]
    lane = lax.broadcasted_iota(jnp.int32, (META, TOK), 1)
    row = lax.broadcasted_iota(jnp.int32, (META, TOK), 0)
    payload[2 * TOK :, :] = jnp.zeros((META, FEAT), jnp.bfloat16)
    payload[2 * TOK :, 0:TOK] = (
        local_bar(starts, lane + base).astype(jnp.float32).astype(jnp.bfloat16)
    )
    slot = jnp.full((META, TOK), -1, jnp.int32)
    for b in range(BARS_HERE):
        slot = jnp.where(row == b, slots[b] - base, slot)
    pick = (lane == slot).astype(jnp.float32).astype(jnp.bfloat16)
    key_rows = jnp.dot(pick, keys[...], preferred_element_type=jnp.float32)
    value_rows = jnp.dot(pick, values[...], preferred_element_type=jnp.float32)
    for h in range(HEADS_HERE):
        cols = slice(h * HD, (h + 1) * HD)
        sums[:, 2 * h * HD : (2 * h + 1) * HD] = key_rows[0:BARS_HERE, cols].astype(jnp.bfloat16)
        sums[:, (2 * h + 1) * HD : (2 * h + 2) * HD] = value_rows[0:BARS_HERE, cols].astype(
            jnp.bfloat16
        )


def attend_kernel(
    starts, related, queries, grad_out, own, back1, back2, back3, back4, sums,
    grad_queries, own_grad, halo_grad, sum_grad, bias,
):
    blocks = [back4, back3, back2, back1, own]
    nt = (((1,), (1,)), ((), ()))

    @pl.when(pl.program_id(0) == 0)
    def _():
        base = starts[0]
        rank = lax.shift_right_logical(base, 7)
        lane = lax.broadcasted_iota(jnp.int32, (8, TOK), 1)
        token_local = local_bar(starts, lane + base)
        token_bar = rank * BARS_HERE + token_local
        rel = []
        for j in range(8):
            entry = jnp.full((8, TOK), -1, jnp.int32)
            for b in range(BARS_HERE):
                entry = jnp.where(token_local == b, related[b, j], entry)
            rel.append(entry[0:1])
        token_bar = token_bar[0:1]
        for place in range(REACH + 1):
            offset = REACH - place
            meta = blocks[place][2 * TOK : 2 * TOK + META, :].astype(jnp.float32)
            key_local = jnp.transpose(jnp.broadcast_to(meta[0:1], (TOK, TOK))).astype(jnp.int32)
            owner = rank - offset
            key_bar = jnp.where(owner >= 0, owner * BARS_HERE + key_local, -2)
            seen = key_bar == rel[0]
            for j in range(1, 8):
                seen = seen | (key_bar == rel[j])
            if offset == 0:
                key_row = lax.broadcasted_iota(jnp.int32, (TOK, TOK), 0)
                token_col = lax.broadcasted_iota(jnp.int32, (TOK, TOK), 1)
                seen = seen | ((key_bar == token_bar) & (key_row <= token_col))
            bias[place * TOK : (place + 1) * TOK, :] = jnp.where(seen, 0.0, -jnp.inf)
        for part in range(BARS // TOK):
            bar = lax.broadcasted_iota(jnp.int32, (TOK, TOK), 0) + part * TOK
            hidden = bar >= token_bar
            for j in range(8):
                hidden = hidden | (bar == rel[j])
            low = WINDOW + part * TOK
            bias[low : low + TOK, :] = jnp.where(hidden, -jnp.inf, 0.0)

    query = queries[...]
    grad = grad_out[...]
    key_blocks = [block[0:TOK, :] for block in blocks] + [sums[:, 0:HD]]
    value_blocks = [block[TOK : 2 * TOK, :] for block in blocks] + [sums[:, HD : 2 * HD]]
    keys = jnp.concatenate(key_blocks, axis=0)
    values = jnp.concatenate(value_blocks, axis=0)
    scores = lax.dot_general(keys, query, nt, preferred_element_type=jnp.float32) + bias[...]
    top = jnp.max(scores, axis=0, keepdims=True)
    weights = jnp.exp2((scores - top) * EXP_SCALE)
    probs = weights * (1.0 / jnp.sum(weights, axis=0, keepdims=True))
    probs_low = probs.astype(jnp.bfloat16)
    dprobs = lax.dot_general(values, grad, nt, preferred_element_type=jnp.float32)
    delta = jnp.sum(probs_low.astype(jnp.float32) * dprobs, axis=0, keepdims=True)
    dscores = (probs * (dprobs - delta)).astype(jnp.bfloat16)
    grad_queries[...] = (
        SCALE
        * lax.dot_general(
            dscores, keys, (((0,), (0,)), ((), ())), preferred_element_type=jnp.float32
        )
    ).astype(jnp.bfloat16)
    dkeys = SCALE * jnp.dot(dscores, query, preferred_element_type=jnp.float32)
    dvalues = jnp.dot(probs_low, grad, preferred_element_type=jnp.float32)
    for place in range(REACH):
        rows = slice(place * TOK, (place + 1) * TOK)
        halo_grad[place, 0:TOK, :] = dkeys[rows].astype(jnp.bfloat16)
        halo_grad[place, TOK : 2 * TOK, :] = dvalues[rows].astype(jnp.bfloat16)
    own_grad[0:TOK, :] = dkeys[REACH * TOK : WINDOW]
    own_grad[TOK : 2 * TOK, :] = dvalues[REACH * TOK : WINDOW]
    sum_grad[:, 0:HD] = dkeys[WINDOW:].astype(jnp.bfloat16)
    sum_grad[:, HD : 2 * HD] = dvalues[WINDOW:].astype(jnp.bfloat16)


def finish_kernel(starts, slots, own_grad, arrived, parts, grad_keys, grad_values):
    base = starts[0]
    total = parts[0].astype(jnp.float32)
    for i in range(1, NZ):
        total = total + parts[i].astype(jnp.float32)
    row = lax.broadcasted_iota(jnp.int32, (TOK, HD), 0)
    for h in range(HEADS_HERE):
        cols = slice(h * HD, (h + 1) * HD)
        for kind, out in ((0, grad_keys), (1, grad_values)):
            rows = slice(kind * TOK, (kind + 1) * TOK)
            low = (2 * h + kind) * HD
            grad = own_grad[rows, cols] + arrived[rows, cols].astype(jnp.float32)
            for b in range(BARS_HERE):
                grad = grad + jnp.where(
                    row == slots[b] - base, total[b : b + 1, low : low + HD], 0.0
                )
            out[:, cols] = grad.astype(jnp.bfloat16)


def whole(space):
    return pl.BlockSpec(memory_space=space)


def shards(queries, keys, values, grad_y, out_weight, bar_start, related, bar_summary_token):
    bf16 = jnp.bfloat16
    payload, sums = pl.pallas_call(
        pack_kernel,
        out_shape=(
            jax.ShapeDtypeStruct((2 * TOK + META, FEAT), bf16),
            jax.ShapeDtypeStruct((BARS_HERE, 2 * FEAT), bf16),
        ),
        in_specs=[whole(SMEM), whole(SMEM), whole(VMEM), whole(VMEM)],
        out_specs=(whole(VMEM), whole(VMEM)),
    )(bar_start, bar_summary_token, keys, values)

    grad_out = lax.dot_general(
        lax.all_gather(grad_y, "head", axis=1, tiled=True),
        out_weight,
        (((1,), (1,)), ((), ())),
        preferred_element_type=jnp.float32,
    ).astype(bf16)

    back = [payload]
    for _ in range(REACH):
        back.append(shift(back[-1], 1))

    row_sums = lax.all_to_all(
        jnp.broadcast_to(sums[None], (NZ,) + sums.shape), "seq", 0, 0, axis_index_groups=Z_GROUPS
    )
    row_sums = row_sums.reshape(NZ * BARS_HERE, 2 * FEAT)
    all_sums = lax.all_to_all(
        jnp.broadcast_to(row_sums[None], (NXY,) + row_sums.shape),
        "seq",
        0,
        0,
        axis_index_groups=XY_GROUPS,
    ).reshape(BARS, 2 * FEAT)

    window = pl.BlockSpec((2 * TOK + META, HD), lambda h: (0, h))
    heads = pl.BlockSpec((TOK, HD), lambda h: (0, h))
    pairs = pl.BlockSpec((BARS, 2 * HD), lambda h: (0, h))
    grad_queries, own_grad, halo_grad, sum_grad = pl.pallas_call(
        attend_kernel,
        grid=(HEADS_HERE,),
        out_shape=(
            jax.ShapeDtypeStruct((TOK, FEAT), bf16),
            jax.ShapeDtypeStruct((2 * TOK, FEAT), jnp.float32),
            jax.ShapeDtypeStruct((REACH, 2 * TOK, FEAT), bf16),
            jax.ShapeDtypeStruct((BARS, 2 * FEAT), bf16),
        ),
        in_specs=[whole(SMEM), whole(SMEM), heads, heads] + [window] * 5 + [pairs],
        out_specs=(
            heads,
            pl.BlockSpec((2 * TOK, HD), lambda h: (0, h)),
            pl.BlockSpec((REACH, 2 * TOK, HD), lambda h: (0, 0, h)),
            pairs,
        ),
        scratch_shapes=[pltpu.VMEM((KEYS_ALL, TOK), jnp.float32)],
        compiler_params=pltpu.CompilerParams(vmem_limit_bytes=VMEM_LIMIT),
    )(bar_start, related, queries, grad_out, *back, all_sums)

    moving = shift(halo_grad[0], -1)
    for place in range(1, REACH):
        moving = (moving.astype(jnp.float32) + halo_grad[place].astype(jnp.float32)).astype(bf16)
        moving = shift(moving, -1)

    parts = lax.all_to_all(
        sum_grad.reshape(NXY, NZ * BARS_HERE, 2 * FEAT),
        "seq",
        0,
        0,
        axis_index_groups=XY_GROUPS,
    )
    row_grad = jnp.sum(parts.astype(jnp.float32), axis=0).astype(bf16)
    parts = lax.all_to_all(
        row_grad.reshape(NZ, BARS_HERE, 2 * FEAT), "seq", 0, 0, axis_index_groups=Z_GROUPS
    )

    grad_keys, grad_values = pl.pallas_call(
        finish_kernel,
        out_shape=(
            jax.ShapeDtypeStruct((TOK, FEAT), bf16),
            jax.ShapeDtypeStruct((TOK, FEAT), bf16),
        ),
        in_specs=[whole(SMEM), whole(SMEM), whole(VMEM), whole(VMEM), whole(VMEM)],
        out_specs=(whole(VMEM), whole(VMEM)),
    )(bar_start, bar_summary_token, own_grad, moving, parts)
    return grad_queries, grad_keys, grad_values


def solution(mesh):
    in_specs = (
        P("seq", "head"),
        P("seq", "head"),
        P("seq", "head"),
        P("seq", "head"),
        P("head", None),
        P("seq"),
        P("seq", None),
        P("seq"),
    )
    out_specs = (P("seq", "head"), P("seq", "head"), P("seq", "head"))
    return jax.shard_map(shards, mesh=mesh, in_specs=in_specs, out_specs=out_specs, check_vma=False)
```

```python
import math

import jax
import jax.numpy as jnp
from jax import lax
from jax.experimental import pallas as pl
from jax.experimental.pallas import tpu as pltpu
from jax.sharding import PartitionSpec as P

HD = 128
REACH = 4
TOK = 128
BARS_HERE = 8
HEADS_HERE = 4
FEAT = HD * HEADS_HERE
META = 16
ROWS = 2 * TOK + META
NZ = 8
NXY = 16
N_SEQ = NZ * NXY
OFFSETS = (1, 2, 4, 8, 12, 16, 24, 32)
SCALE = HD ** (-0.5)
LOG2E = math.log2(math.e)
EXP_SCALE = SCALE * LOG2E
LOWEST = -1e30

Z_GROUPS = [[j * NZ + z for z in range(NZ)] for j in range(NXY)]
XY_GROUPS = [[j * NZ + z for j in range(NXY)] for z in range(NZ)]
TO_NEXT = [(j * NZ + z, j * NZ + (z + 1) % NZ) for j in range(NXY) for z in range(NZ)]
TO_PREVIOUS = [(dst, src) for src, dst in TO_NEXT]
ROW_UP = [(i, i + NZ) for i in range(N_SEQ - NZ) if i % NZ >= NZ - REACH]
ROW_DOWN = [(dst, src) for src, dst in ROW_UP]

VMEM_LIMIT = 50 * 2**20
SMEM = pltpu.SMEM
VMEM = pltpu.VMEM
HBM = pltpu.HBM
NT = (((1,), (1,)), ((), ()))
TN = (((0,), (0,)), ((), ()))
BF16 = jnp.bfloat16
F32 = jnp.float32


def whole(space):
    return pl.BlockSpec(memory_space=space)


def shape(dims, dtype=BF16):
    return jax.ShapeDtypeStruct(dims, dtype)


def local_bar(starts, positions):
    count = jnp.zeros_like(positions)
    for b in range(1, BARS_HERE):
        count = count + (positions >= starts[b]).astype(jnp.int32)
    return count


def low(flags):
    return flags.astype(F32).astype(BF16)


def query_pack_kernel(starts, related, queries, grad_y, out_weight, packed):
    packed[0:TOK, :] = queries[...]
    grad_out = lax.dot_general(grad_y[...], out_weight[...], NT, preferred_element_type=F32)
    packed[TOK : 2 * TOK, :] = grad_out.astype(BF16)
    lane = lax.broadcasted_iota(jnp.int32, (META, TOK), 1)
    row = lax.broadcasted_iota(jnp.int32, (META, TOK), 0)
    bar = local_bar(starts, lane + starts[0])
    info = jnp.where(row == 0, bar, 0)
    for j in range(len(OFFSETS)):
        entry = jnp.zeros((META, TOK), jnp.int32)
        for b in range(BARS_HERE):
            has = (related[b, j] >= 0).astype(jnp.int32)
            entry = jnp.where(bar == b, has, entry)
        info = jnp.where(row == j + 1, entry, info)
    packed[2 * TOK :, :] = jnp.zeros((META, FEAT), BF16)
    packed[2 * TOK :, 0:TOK] = low(info)


def key_pack_kernel(starts, slots, keys, values, packed, sums):
    base = starts[0]
    packed[0:TOK, :] = keys[...]
    packed[TOK : 2 * TOK, :] = values[...]
    lane = lax.broadcasted_iota(jnp.int32, (META, TOK), 1)
    row = lax.broadcasted_iota(jnp.int32, (META, TOK), 0)
    packed[2 * TOK :, :] = jnp.zeros((META, FEAT), BF16)
    packed[2 * TOK :, 0:TOK] = low(local_bar(starts, lane + base))
    slot = jnp.full((META, TOK), -1, jnp.int32)
    for b in range(BARS_HERE):
        slot = jnp.where(row == b, slots[b] - base, slot)
    pick = low(lane == slot)
    for kind, source in ((0, keys), (1, values)):
        rows = jnp.dot(pick, source[...], preferred_element_type=F32)[0:BARS_HERE].astype(BF16)
        for h in range(HEADS_HERE):
            at = (2 * h + kind) * HD
            for j in range(NXY):
                sums[j, :, at : at + HD] = rows[:, h * HD : (h + 1) * HD]


def place_of(starts):
    rank = lax.shift_right_logical(starts[0], 7)
    return rank, jnp.bitwise_and(rank, NZ - 1)


def load_all(chunks, blocks, sums, packed, pairs, keys, sems):
    copies = [pltpu.make_async_copy(blocks[i], pairs.at[i], sems.at[i]) for i in range(2)]
    copies.append(pltpu.make_async_copy(sums, keys, sems.at[2]))
    copies += [
        pltpu.make_async_copy(chunks[o], packed.at[o], sems.at[3 + o]) for o in range(NZ)
    ]
    for copy in copies:
        copy.start()
    return copies


def build_bias(starts, packed, pairs, bias):
    rank, z = place_of(starts)
    own_local, previous_local = (
        jnp.transpose(
            jnp.broadcast_to(pairs[i, 2 * TOK :, 0:TOK].astype(F32)[0:1], (TOK, TOK))
        ).astype(jnp.int32)
        for i in range(2)
    )
    key_row = lax.broadcasted_iota(jnp.int32, (TOK, TOK), 0)
    token_col = lax.broadcasted_iota(jnp.int32, (TOK, TOK), 1)
    summary_bar = (
        lax.shift_right_logical(key_row, 3) * (NZ * BARS_HERE)
        + jnp.bitwise_and(key_row, BARS_HERE - 1)
        + z * BARS_HERE
    )
    for o in range(NZ):
        owner = rank - z + jnp.bitwise_and(z + o, NZ - 1)
        info = packed[o, 2 * TOK :, 0:TOK].astype(F32).astype(jnp.int32)
        token_bar = info[0:1] + owner * BARS_HERE
        rel = [
            jnp.where(info[j + 1 : j + 2] > 0, token_bar - OFFSETS[j], -1)
            for j in range(len(OFFSETS))
        ]
        if o <= REACH:
            key_owner = owner - o
            key_local = jnp.where(z + o >= NZ, previous_local, own_local)
            key_bar = jnp.where(key_owner >= 0, key_local + key_owner * BARS_HERE, -2)
            seen = key_bar == rel[0]
            for entry in rel[1:]:
                seen = seen | (key_bar == entry)
            if o == 0:
                seen = seen | ((key_bar == token_bar) & (key_row <= token_col))
            bias[o] = jnp.where(seen, 0.0, -jnp.inf)
        hidden = summary_bar >= token_bar
        for entry in rel:
            hidden = hidden | (summary_bar == entry)
        bias[REACH + 1 + o] = jnp.where(hidden, -jnp.inf, 0.0)


def products(starts, packed, pairs, keys, bias, h, o):
    _, z = place_of(starts)
    cols = slice(h * HD, (h + 1) * HD)
    at = 2 * h * HD
    query = packed[o, 0:TOK, cols]
    grad = packed[o, TOK : 2 * TOK, cols]
    key, value = keys[:, at : at + HD], keys[:, at + HD : at + 2 * HD]
    mask = bias[REACH + 1 + o]
    if o <= REACH:
        side = lax.shift_right_logical(z + o, 3)
        key = jnp.concatenate([pairs[side, 0:TOK, cols], key], axis=0)
        value = jnp.concatenate([pairs[side, TOK : 2 * TOK, cols], value], axis=0)
        mask = jnp.concatenate([bias[o], mask], axis=0)
    scores = lax.dot_general(key, query, NT, preferred_element_type=F32)
    dprobs = lax.dot_general(value, grad, NT, preferred_element_type=F32)
    return key, query, grad, scores, dprobs, mask


def stats_kernel(*refs):
    starts, *refs = refs
    chunks, (own, previous, sums, stats, bias_out), refs = refs[:NZ], refs[NZ : NZ + 5], refs[NZ + 5 :]
    packed, pairs, keys, bias, sems, bias_sem = refs
    copies = load_all(chunks, (own, previous), sums, packed, pairs, keys, sems)
    for copy in copies:
        copy.wait()
    build_bias(starts, packed, pairs, bias)
    bias_copy = pltpu.make_async_copy(bias, bias_out, bias_sem)
    bias_copy.start()
    _, z = place_of(starts)
    for o in range(NZ):
        chunk = jnp.bitwise_and(z + o, NZ - 1)
        log_sums, means = [], []
        for h in range(HEADS_HERE):
            _, _, _, scores, dprobs, mask = products(starts, packed, pairs, keys, bias, h, o)
            scores = scores + mask
            top = jnp.maximum(jnp.max(scores, axis=0, keepdims=True), LOWEST)
            weights = jnp.exp2((scores - top) * EXP_SCALE)
            total = jnp.sum(weights, axis=0, keepdims=True)
            weighted = jnp.sum(weights * dprobs, axis=0, keepdims=True)
            log_sums.append(top * EXP_SCALE + jnp.log(total) * LOG2E)
            means.append(jnp.where(total > 0.0, weighted / total, 0.0))
        merged = jnp.concatenate(log_sums + means, axis=0)
        for peer in range(NZ):
            stats[peer, chunk] = merged
    bias_copy.wait()


def grads_kernel(*refs):
    starts, *refs = refs
    chunks, (own, previous, sums, bias_in, stats), refs = refs[:NZ], refs[NZ : NZ + 5], refs[NZ + 5 :]
    query_grad, previous_grad, own_grad, sum_grad = refs[:4]
    packed, pairs, keys, bias, merged, sems, bias_sem = refs[4:]
    copies = load_all(chunks, (own, previous), sums, packed, pairs, keys, sems)
    copies.append(pltpu.make_async_copy(bias_in, bias, bias_sem))
    copies[-1].start()
    top = stats[0, :, 0:HEADS_HERE, :]
    for i in range(1, NZ):
        top = jnp.maximum(top, stats[i, :, 0:HEADS_HERE, :])
    total = jnp.zeros_like(top)
    mean = jnp.zeros_like(top)
    for i in range(NZ):
        weight = jnp.exp2(stats[i, :, 0:HEADS_HERE, :] - top)
        total = total + weight
        mean = mean + weight * stats[i, :, HEADS_HERE:, :]
    merged[:, 0:HEADS_HERE, :] = top + jnp.log(total) * LOG2E
    merged[:, HEADS_HERE:, :] = mean / total
    for copy in copies:
        copy.wait()
    _, z = place_of(starts)
    for h in range(HEADS_HERE):
        cols = slice(h * HD, (h + 1) * HD)
        at = 2 * h * HD
        own_key = jnp.zeros((TOK, HD), F32)
        own_value, previous_key, previous_value = own_key, own_key, own_key
        probs_parts, dscores_parts, queries, grads = [], [], [], []
        for o in range(NZ):
            chunk = jnp.bitwise_and(z + o, NZ - 1)
            key, query, grad, scores, dprobs, mask = products(
                starts, packed, pairs, keys, bias, h, o
            )
            log_sum = merged[chunk, h : h + 1, :]
            delta = merged[chunk, HEADS_HERE + h : HEADS_HERE + h + 1, :]
            probs = jnp.exp2(scores * EXP_SCALE - log_sum + mask)
            probs_low = probs.astype(BF16)
            dscores = (probs * (dprobs - delta)).astype(BF16)
            dquery = lax.dot_general(dscores, key, TN, preferred_element_type=F32)
            query_grad[chunk, :, cols] = (SCALE * dquery).astype(BF16)
            if o <= REACH:
                dkey = jnp.dot(dscores[0:TOK], query, preferred_element_type=F32)
                dvalue = jnp.dot(probs_low[0:TOK], grad, preferred_element_type=F32)
                wraps = (z + o >= NZ).astype(F32)
                own_key = own_key + dkey * (1.0 - wraps)
                own_value = own_value + dvalue * (1.0 - wraps)
                previous_key = previous_key + dkey * wraps
                previous_value = previous_value + dvalue * wraps
                dscores, probs_low = dscores[TOK:], probs_low[TOK:]
            probs_parts.append(probs_low)
            dscores_parts.append(dscores)
            queries.append(query)
            grads.append(grad)
        own_grad[0:TOK, cols] = own_key * SCALE
        own_grad[TOK : 2 * TOK, cols] = own_value
        previous_grad[0:TOK, cols] = (previous_key * SCALE).astype(BF16)
        previous_grad[TOK : 2 * TOK, cols] = previous_value.astype(BF16)
        dkey = jnp.dot(
            jnp.concatenate(dscores_parts, axis=1),
            jnp.concatenate(queries, axis=0),
            preferred_element_type=F32,
        )
        dvalue = jnp.dot(
            jnp.concatenate(probs_parts, axis=1),
            jnp.concatenate(grads, axis=0),
            preferred_element_type=F32,
        )
        sum_grad[:, at : at + HD] = (dkey * SCALE).astype(BF16)
        sum_grad[:, at + HD : at + 2 * HD] = dvalue.astype(BF16)


def finish_kernel(starts, slots, own_grad, arrived, parts, grad_keys, grad_values):
    base = starts[0]
    total = parts[0].astype(F32)
    for i in range(1, NXY):
        total = total + parts[i].astype(F32)
    row = lax.broadcasted_iota(jnp.int32, (TOK, HD), 0)
    for h in range(HEADS_HERE):
        cols = slice(h * HD, (h + 1) * HD)
        for kind, out in ((0, grad_keys), (1, grad_values)):
            rows = slice(kind * TOK, (kind + 1) * TOK)
            at = (2 * h + kind) * HD
            grad = own_grad[rows, cols] + arrived[rows, cols].astype(F32)
            for b in range(BARS_HERE):
                grad = grad + jnp.where(row == slots[b] - base, total[b : b + 1, at : at + HD], 0.0)
            out[:, cols] = grad.astype(BF16)


def query_sum_kernel(parts, grad_queries):
    total = parts[0].astype(F32)
    for i in range(1, NZ):
        total = total + parts[i].astype(F32)
    grad_queries[...] = total.astype(BF16)


def shards(queries, keys, values, grad_y, out_weight, bar_start, related, bar_summary_token):
    params = pltpu.CompilerParams(vmem_limit_bytes=VMEM_LIMIT)
    packed = pl.pallas_call(
        query_pack_kernel,
        out_shape=shape((ROWS, FEAT)),
        in_specs=[whole(SMEM)] * 2 + [whole(VMEM)] * 3,
        out_specs=whole(VMEM),
        compiler_params=params,
    )(bar_start, related, queries, lax.all_gather(grad_y, "head", axis=1, tiled=True), out_weight)

    after, before = [packed], [packed]
    after.append(lax.ppermute(after[-1], "seq", TO_PREVIOUS))
    before.append(lax.ppermute(before[-1], "seq", TO_NEXT))

    own, sums = pl.pallas_call(
        key_pack_kernel,
        out_shape=(shape((ROWS, FEAT)), shape((NXY, BARS_HERE, 2 * FEAT))),
        in_specs=[whole(SMEM)] * 2 + [whole(VMEM)] * 2,
        out_specs=(whole(VMEM),) * 2,
    )(bar_start, bar_summary_token, keys, values)
    previous = lax.ppermute(own, "seq", ROW_UP)
    all_sums = lax.all_to_all(sums, "seq", 0, 0, axis_index_groups=XY_GROUPS).reshape(
        NXY * BARS_HERE, 2 * FEAT
    )

    for _ in range(2):
        after.append(lax.ppermute(after[-1], "seq", TO_PREVIOUS))
        before.append(lax.ppermute(before[-1], "seq", TO_NEXT))
    after.append(lax.ppermute(after[-1], "seq", TO_PREVIOUS))
    chunks = after + before[:0:-1]

    held = [
        VMEM((NZ, ROWS, FEAT), BF16),
        VMEM((2, ROWS, FEAT), BF16),
        VMEM((NXY * BARS_HERE, 2 * FEAT), BF16),
        VMEM((REACH + 1 + NZ, TOK, TOK), F32),
    ]
    sems = [pltpu.SemaphoreType.DMA((NZ + 3,)), pltpu.SemaphoreType.DMA]
    stats, bias = pl.pallas_call(
        stats_kernel,
        out_shape=(
            shape((NZ, NZ, 2 * HEADS_HERE, TOK), F32),
            shape((REACH + 1 + NZ, TOK, TOK), F32),
        ),
        in_specs=[whole(SMEM)] + [whole(HBM)] * (NZ + 3),
        out_specs=(whole(VMEM), whole(HBM)),
        scratch_shapes=held + sems,
        compiler_params=params,
    )(bar_start, *chunks, own, previous, all_sums)

    stats = lax.all_to_all(stats, "seq", 0, 0, axis_index_groups=Z_GROUPS)

    query_grad, previous_grad, own_grad, sum_grad = pl.pallas_call(
        grads_kernel,
        out_shape=(
            shape((NZ, TOK, FEAT)),
            shape((2 * TOK, FEAT)),
            shape((2 * TOK, FEAT), F32),
            shape((NXY * BARS_HERE, 2 * FEAT)),
        ),
        in_specs=[whole(SMEM)] + [whole(HBM)] * (NZ + 4) + [whole(VMEM)],
        out_specs=(whole(VMEM),) * 4,
        scratch_shapes=held + [VMEM((NZ, 2 * HEADS_HERE, TOK), F32)] + sems,
        compiler_params=params,
    )(bar_start, *chunks, own, previous, all_sums, bias, stats)

    query_parts = lax.all_to_all(query_grad, "seq", 0, 0, axis_index_groups=Z_GROUPS)
    parts = lax.all_to_all(
        sum_grad.reshape(NXY, BARS_HERE, 2 * FEAT), "seq", 0, 0, axis_index_groups=XY_GROUPS
    )
    arrived = lax.ppermute(previous_grad, "seq", ROW_DOWN)

    grad_keys, grad_values = pl.pallas_call(
        finish_kernel,
        out_shape=(shape((TOK, FEAT)), shape((TOK, FEAT))),
        in_specs=[whole(SMEM)] * 2 + [whole(VMEM)] * 3,
        out_specs=(whole(VMEM),) * 2,
    )(bar_start, bar_summary_token, own_grad, arrived, parts)
    grad_queries = pl.pallas_call(
        query_sum_kernel,
        out_shape=shape((TOK, FEAT)),
        in_specs=[whole(VMEM)],
        out_specs=whole(VMEM),
    )(query_parts)
    return grad_queries, grad_keys, grad_values


def solution(mesh):
    in_specs = (
        P("seq", "head"),
        P("seq", "head"),
        P("seq", "head"),
        P("seq", "head"),
        P("head", None),
        P("seq"),
        P("seq", None),
        P("seq"),
    )
    out_specs = (P("seq", "head"), P("seq", "head"), P("seq", "head"))
    return jax.shard_map(shards, mesh=mesh, in_specs=in_specs, out_specs=out_specs, check_vma=False)
```

```python
import math

import jax
import jax.numpy as jnp
from jax import lax
from jax.experimental import pallas as pl
from jax.experimental.pallas import tpu as pltpu
from jax.sharding import PartitionSpec as P

HD = 128
REACH = 4
TOK = 128
BARS_HERE = 8
HEADS_HERE = 4
FEAT = HD * HEADS_HERE
META = 16
ROWS = 2 * TOK + META
NZ = 8
NY = 4
NX = 4
NXY = NY * NX
N_SEQ = NZ * NXY
OFFSETS = (1, 2, 4, 8, 12, 16, 24, 32)
SCALE = HD ** (-0.5)
LOG2E = math.log2(math.e)
EXP_SCALE = SCALE * LOG2E
LOWEST = -1e30

Z_GROUPS = [[j * NZ + z for z in range(NZ)] for j in range(NXY)]
XY_GROUPS = [[j * NZ + z for j in range(NXY)] for z in range(NZ)]


def route(dy, dx, dz):
    return [
        ((y * NX + x) * NZ + z, ((y + dy) % NY * NX + (x + dx) % NX) * NZ + (z + dz) % NZ)
        for y in range(NY)
        for x in range(NX)
        for z in range(NZ)
    ]


TO_NEXT = route(0, 0, 1)
TO_PREVIOUS = route(0, 0, -1)
ROW_UP = [(i, i + NZ) for i in range(N_SEQ - NZ) if i % NZ >= NZ - REACH]
ROW_DOWN = [(dst, src) for src, dst in ROW_UP]
EARLY = (0, 1, 7, 2, 6, 3, 5)
LATE = (4,)
ORDER = EARLY + LATE

VMEM_LIMIT = 50 * 2**20
SMEM = pltpu.SMEM
VMEM = pltpu.VMEM
HBM = pltpu.HBM
NT = (((1,), (1,)), ((), ()))
TN = (((0,), (0,)), ((), ()))
BF16 = jnp.bfloat16
F32 = jnp.float32


def whole(space):
    return pl.BlockSpec(memory_space=space)


def shape(dims, dtype=BF16):
    return jax.ShapeDtypeStruct(dims, dtype)


def pinned(*arrays):
    return [pltpu.with_memory_space_constraint(array, HBM) for array in arrays]


def local_bar(starts, positions):
    count = jnp.zeros_like(positions)
    for b in range(1, BARS_HERE):
        count = count + (positions >= starts[b]).astype(jnp.int32)
    return count


def low(flags):
    return flags.astype(F32).astype(BF16)


def pack_kernel(
    core, starts, related, slots, queries, keys, values, grad_own, out_weight,
    partial, query_pack, key_pack, sums, weight, grad, sems,
):
    half = grad_own.shape[1]
    copies = [pltpu.make_async_copy(grad_own, grad, sems.at[0])]
    cols = pl.ds(pl.multiple_of(core[0] * half, half), half)
    copies.append(pltpu.make_async_copy(out_weight.at[:, cols], weight, sems.at[1]))
    copies.append(pltpu.make_async_copy(queries, query_pack.at[pl.ds(0, TOK)], sems.at[3]))
    copies.append(pltpu.make_async_copy(keys, key_pack.at[pl.ds(0, TOK)], sems.at[4]))
    copies.append(pltpu.make_async_copy(values, key_pack.at[pl.ds(TOK, TOK)], sems.at[5]))
    for copy in copies:
        copy.start()
    base = starts[0]
    lane = lax.broadcasted_iota(jnp.int32, (META, TOK), 1)
    row = lax.broadcasted_iota(jnp.int32, (META, TOK), 0)
    bar = local_bar(starts, lane + base)
    info = jnp.where(row == 0, bar, 0)
    for j in range(len(OFFSETS)):
        entry = jnp.zeros((META, TOK), jnp.int32)
        for b in range(BARS_HERE):
            has = (related[b, j] >= 0).astype(jnp.int32)
            entry = jnp.where(bar == b, has, entry)
        info = jnp.where(row == j + 1, entry, info)
    query_pack[TOK:, :] = jnp.zeros((TOK + META, FEAT), BF16)
    query_pack[2 * TOK :, 0:TOK] = low(info)
    key_pack[2 * TOK :, :] = jnp.zeros((META, FEAT), BF16)
    key_pack[2 * TOK :, 0:TOK] = low(bar)
    slot = jnp.full((META, TOK), -1, jnp.int32)
    for b in range(BARS_HERE):
        slot = jnp.where(row == b, slots[b] - base, slot)
    pick = low(lane == slot)
    for copy in copies[2:]:
        copy.wait()
    for kind in range(2):
        source = key_pack[kind * TOK : (kind + 1) * TOK, :]
        rows = jnp.dot(pick, source, preferred_element_type=F32)[0:BARS_HERE].astype(BF16)
        for h in range(HEADS_HERE):
            at = (2 * h + kind) * HD
            for j in range(NXY):
                sums[j, :, at : at + HD] = rows[:, h * HD : (h + 1) * HD]
    for copy in copies[:2]:
        copy.wait()
    partial[...] = lax.dot_general(weight[...], grad[...], NT, preferred_element_type=F32)


def grad_pack_kernel(core, pack, partial, grad_other, out_weight, packed, weight, sem):
    half = grad_other.shape[1]
    cols = pl.ds(pl.multiple_of((1 - core[0]) * half, half), half)
    copy = pltpu.make_async_copy(out_weight.at[:, cols], weight, sem)
    copy.start()
    packed[0:TOK, :] = pack[0:TOK, :]
    packed[2 * TOK :, :] = pack[2 * TOK :, :]
    copy.wait()
    turned = partial[...] + lax.dot_general(
        weight[...], grad_other[...], NT, preferred_element_type=F32
    )
    for h in range(HEADS_HERE):
        cols = slice(h * HD, (h + 1) * HD)
        packed[TOK : 2 * TOK, cols] = jnp.transpose(turned[cols]).astype(BF16)


def place():
    rank = lax.axis_index("seq")
    return rank, jnp.bitwise_and(rank, NZ - 1)


def load_keys(own, previous, sums, pairs, keys, sems):
    copies = [
        pltpu.make_async_copy(own, pairs.at[0], sems.at[0]),
        pltpu.make_async_copy(previous, pairs.at[1], sems.at[1]),
        pltpu.make_async_copy(sums, keys, sems.at[2]),
    ]
    for copy in copies:
        copy.start()
    return copies


class Bias:
    def __init__(self, packed, pairs):
        rank, self.z = place()
        self.row_start = rank - self.z
        self.packed = packed
        self.local = [
            jnp.transpose(
                jnp.broadcast_to(pairs[i, 2 * TOK :, 0:TOK].astype(F32)[0:1], (TOK, TOK))
            ).astype(jnp.int32)
            for i in range(2)
        ]
        self.key_row = lax.broadcasted_iota(jnp.int32, (TOK, TOK), 0)
        self.token_col = lax.broadcasted_iota(jnp.int32, (TOK, TOK), 1)
        owner = lax.shift_right_logical(self.key_row, 3) * NZ + self.z
        self.summary_bar = owner * BARS_HERE + jnp.bitwise_and(self.key_row, BARS_HERE - 1)

    def build(self, o, bias):
        owner = self.row_start + jnp.bitwise_and(self.z + o, NZ - 1)
        info = self.packed[o, 2 * TOK :, 0:TOK].astype(F32).astype(jnp.int32)
        token_bar = info[0:1] + owner * BARS_HERE
        rel = [
            jnp.where(info[j + 1 : j + 2] > 0, token_bar - OFFSETS[j], -1)
            for j in range(len(OFFSETS))
        ]
        if o <= REACH:
            key_owner = owner - o
            key_local = jnp.where(self.z + o >= NZ, self.local[1], self.local[0])
            key_bar = jnp.where(key_owner >= 0, key_local + key_owner * BARS_HERE, -2)
            seen = key_bar == rel[0]
            for entry in rel[1:]:
                seen = seen | (key_bar == entry)
            if o == 0:
                seen = seen | ((key_bar == token_bar) & (self.key_row <= self.token_col))
            bias[o] = jnp.where(seen, 0.0, -jnp.inf)
        hidden = self.summary_bar >= token_bar
        for entry in rel:
            hidden = hidden | (self.summary_bar == entry)
        bias[REACH + 1 + o] = jnp.where(hidden, -jnp.inf, 0.0)


def bias_blocks(order):
    return [o for o in order if o <= REACH] + [REACH + 1 + o for o in order]


def products(packed, pairs, keys, bias, h, o):
    _, z = place()
    cols = slice(h * HD, (h + 1) * HD)
    at = 2 * h * HD
    query = packed[o, 0:TOK, cols]
    grad = packed[o, TOK : 2 * TOK, cols]
    key, value = keys[:, at : at + HD], keys[:, at + HD : at + 2 * HD]
    mask = bias[REACH + 1 + o]
    if o <= REACH:
        side = lax.shift_right_logical(z + o, 3)
        key = jnp.concatenate([pairs[side, 0:TOK, cols], key], axis=0)
        value = jnp.concatenate([pairs[side, TOK : 2 * TOK, cols], value], axis=0)
        mask = jnp.concatenate([bias[o], mask], axis=0)
    scores = lax.dot_general(key, query, NT, preferred_element_type=F32)
    dprobs = lax.dot_general(value, grad, NT, preferred_element_type=F32)
    return key, scores, dprobs, mask


def stats_kernel(order, *refs):
    chunks, (own, previous, sums), refs = refs[: len(order)], refs[len(order) : len(order) + 3], refs[len(order) + 3 :]
    earlier, refs = (refs[0], refs[1:]) if len(order) < REACH else (None, refs)
    stats, bias_out, packed, pairs, keys, bias, key_sems, chunk_sems, bias_sems = refs
    key_copies = load_keys(own, previous, sums, pairs, keys, key_sems)
    copies = [
        pltpu.make_async_copy(chunk, packed.at[o], chunk_sems.at[o])
        for o, chunk in zip(order, chunks)
    ]
    for copy in copies:
        copy.start()
    for copy in key_copies:
        copy.wait()
    masks = Bias(packed, pairs)
    writes = []
    for i, o in enumerate(order):
        copies[i].wait()
        masks.build(o, bias)
        for block in bias_blocks((o,)):
            place_out = bias_out.at[bias_blocks(order).index(block)]
            writes.append(pltpu.make_async_copy(bias.at[block], place_out, bias_sems.at[block]))
            writes[-1].start()
        chunk = jnp.bitwise_and(masks.z + o, NZ - 1)
        log_sums, means = [], []
        made = [products(packed, pairs, keys, bias, h, o) for h in range(HEADS_HERE)]
        for _, scores, dprobs, mask in made:
            scores = scores + mask
            top = jnp.maximum(jnp.max(scores, axis=0, keepdims=True), LOWEST)
            weights = jnp.exp2((scores - top) * EXP_SCALE)
            total = jnp.sum(weights, axis=0, keepdims=True)
            weighted = jnp.sum(weights * dprobs, axis=0, keepdims=True)
            log_sums.append(top * EXP_SCALE + jnp.log(total) * LOG2E)
            means.append(jnp.where(total > 0.0, weighted / total, 0.0))
        merged = jnp.concatenate(log_sums + means, axis=0)
        if earlier is None:
            stats[chunk] = merged
            continue
        for peer in range(NZ):
            stats[peer] = earlier[...]
            stats[peer, chunk] = merged
    for copy in writes:
        copy.wait()


def merge_stats(stats, merged):
    top = stats[0, :, 0:HEADS_HERE, :]
    for i in range(1, NZ):
        top = jnp.maximum(top, stats[i, :, 0:HEADS_HERE, :])
    total = jnp.zeros_like(top)
    mean = jnp.zeros_like(top)
    for i in range(NZ):
        weight = jnp.exp2(stats[i, :, 0:HEADS_HERE, :] - top)
        total = total + weight
        mean = mean + weight * stats[i, :, HEADS_HERE:, :]
    merged[:, 0:HEADS_HERE, :] = top + jnp.log(total) * LOG2E
    merged[:, HEADS_HERE:, :] = mean / total


def query_grad_kernel(*refs):
    order = ORDER
    near = [o for o in order if o <= REACH]
    chunks, refs = refs[:NZ], refs[NZ:]
    own, previous, sums, bias_most, bias_last, stats_in, *refs = refs
    query_grads, (coarse_out, window_out, previous_grad), refs = refs[:NZ], refs[NZ : NZ + 3], refs[NZ + 3 :]
    packed, pairs, keys, bias, stats, merged, coarse, window, *refs = refs
    key_sems, chunk_sems, bias_sems, stats_sem, out_sems = refs
    stats_copy = pltpu.make_async_copy(stats_in, stats, stats_sem)
    stats_copy.start()
    key_copies = load_keys(own, previous, sums, pairs, keys, key_sems)
    copies = []
    for i, o in enumerate(order):
        mine = [pltpu.make_async_copy(chunks[o], packed.at[o], chunk_sems.at[o])]
        for block in bias_blocks((o,)):
            source, among = (bias_most, EARLY) if o in EARLY else (bias_last, LATE)
            source = source.at[bias_blocks(among).index(block)]
            mine.append(pltpu.make_async_copy(source, bias.at[block], bias_sems.at[block]))
        for copy in mine:
            copy.start()
        copies.append(mine)
    stats_copy.wait()
    merge_stats(stats, merged)
    for copy in key_copies:
        copy.wait()
    _, z = place()
    keys_turned = [
        jnp.transpose(keys[:, 2 * h * HD : (2 * h + 1) * HD]) for h in range(HEADS_HERE)
    ]
    pairs_turned = [
        [jnp.transpose(pairs[i, 0:TOK, h * HD : (h + 1) * HD]) for i in range(2)]
        for h in range(HEADS_HERE)
    ]
    writes = []
    others = [[None, None] for _ in range(HEADS_HERE)]
    for i, o in enumerate(order):
        for copy in copies[i]:
            copy.wait()
        chunk = jnp.bitwise_and(z + o, NZ - 1)
        made = [products(packed, pairs, keys, bias, h, o) for h in range(HEADS_HERE)]
        low_parts = []
        for h, (_, scores, dprobs, mask) in enumerate(made):
            log_sum = merged[chunk, h : h + 1, :]
            delta = merged[chunk, HEADS_HERE + h : HEADS_HERE + h + 1, :]
            probs = jnp.exp2(scores * EXP_SCALE - log_sum + mask)
            low_parts.append(((probs * (dprobs - delta)).astype(BF16), probs.astype(BF16)))
        for h, (dscores, probs_low) in enumerate(low_parts):
            turned = keys_turned[h]
            if o <= REACH:
                side = pairs_turned[h][0]
                if o > 0:
                    side = jnp.where(z + o >= NZ, pairs_turned[h][1], side)
                turned = jnp.concatenate([side, turned], axis=1)
            dquery = jnp.dot(turned, dscores, preferred_element_type=F32)
            query_grads[o][h * HD : (h + 1) * HD, :] = (SCALE * dquery).astype(BF16)
        for h, (dscores, probs_low) in enumerate(low_parts):
            if o <= REACH:
                window[near.index(o), 0, h] = dscores[0:TOK]
                window[near.index(o), 1, h] = probs_low[0:TOK]
            if 0 < o <= REACH:
                wraps = (z + o >= NZ).astype(F32)
                cols = slice(h * HD, (h + 1) * HD)
                for kind, left in enumerate((dscores, probs_low)):
                    right = packed[o, kind * TOK : (kind + 1) * TOK, cols]
                    part = wraps * jnp.dot(left[0:TOK], right, preferred_element_type=F32)
                    old = others[h][kind]
                    others[h][kind] = part if old is None else old + part
            coarse[i, 0, h] = dscores[-TOK:]
            coarse[i, 1, h] = probs_low[-TOK:]
        writes.append(pltpu.make_async_copy(coarse.at[i], coarse_out.at[i], out_sems.at[0, o]))
        writes[-1].start()
        if o <= REACH:
            at = near.index(o)
            writes.append(
                pltpu.make_async_copy(window.at[at], window_out.at[at], out_sems.at[1, o])
            )
            writes[-1].start()
    for h in range(HEADS_HERE):
        cols = slice(h * HD, (h + 1) * HD)
        previous_grad[0:TOK, cols] = (others[h][0] * SCALE).astype(BF16)
        previous_grad[TOK : 2 * TOK, cols] = others[h][1].astype(BF16)
    for copy in writes:
        copy.wait()


def key_grad_kernel(*refs):
    order = ORDER
    near = [o for o in order if o <= REACH]
    chunks, (coarse_in, window_in), refs = refs[:NZ], refs[NZ : NZ + 2], refs[NZ + 2 :]
    own_grad, *sum_grads = refs[: 1 + NY]
    packed, coarse, window, sum_grad, sems = refs[1 + NY :]
    copies = [pltpu.make_async_copy(chunks[i], packed.at[i], sems.at[i]) for i in range(NZ)]
    copies.append(pltpu.make_async_copy(coarse_in, coarse, sems.at[NZ]))
    copies.append(pltpu.make_async_copy(window_in, window, sems.at[NZ + 1]))
    for copy in copies:
        copy.start()
    for copy in copies:
        copy.wait()
    _, z = place()
    for h in range(HEADS_HERE):
        cols = slice(h * HD, (h + 1) * HD)
        for kind in range(2):
            tokens = [packed[i, kind * TOK : (kind + 1) * TOK, cols] for i in range(NZ)]
            scale = SCALE if kind == 0 else 1.0
            at = (2 * h + kind) * HD
            rows = slice(kind * TOK, (kind + 1) * TOK)
            total = jnp.dot(
                jnp.concatenate([coarse[i, kind, h] for i in range(NZ)], axis=1),
                jnp.concatenate(tokens, axis=0),
                preferred_element_type=F32,
            )
            total = total * scale
            for j in range(NXY):
                part = total[j * BARS_HERE : (j + 1) * BARS_HERE]
                sum_grad[j, :, at : at + HD] = part
            mine = jnp.zeros((TOK, HD), F32)
            for i, o in enumerate(near):
                part = jnp.dot(
                    window[i, kind, h], tokens[order.index(o)], preferred_element_type=F32
                )
                mine = mine + part * (z + o < NZ).astype(F32)
            own_grad[rows, cols] = mine * scale
    rank, _ = place()
    y = lax.shift_right_logical(rank, 5)
    x = lax.shift_right_logical(rank, 3)
    for i in range(NY):
        for k in range(NX):
            j = jnp.bitwise_and(y - i, NY - 1) * NX + jnp.bitwise_and(x - k, NX - 1)
            rows = slice(k * BARS_HERE, (k + 1) * BARS_HERE)
            sum_grads[i][rows, :] = sum_grad[j].astype(BF16)


def finish_kernel(
    starts, slots, own_grad, arrived, part0, part1, part2, part3, here, from_before, from_after,
    grad_queries, grad_keys, grad_values
):
    base = starts[0]
    total = part0[0:BARS_HERE, :].astype(F32)
    for part in (part1, part2, part3):
        total = total + part[...].astype(F32)
    row = lax.broadcasted_iota(jnp.int32, (TOK, HD), 0)
    for h in range(HEADS_HERE):
        cols = slice(h * HD, (h + 1) * HD)
        for kind, out in ((0, grad_keys), (1, grad_values)):
            rows = slice(kind * TOK, (kind + 1) * TOK)
            at = (2 * h + kind) * HD
            grad = own_grad[rows, cols] + arrived[rows, cols].astype(F32)
            for b in range(BARS_HERE):
                grad = grad + jnp.where(row == slots[b] - base, total[b : b + 1, at : at + HD], 0.0)
            out[:, cols] = grad.astype(BF16)
    for h in range(HEADS_HERE):
        rows = slice(h * HD, (h + 1) * HD)
        total = here[rows, :].astype(F32) + from_before[rows, :].astype(F32)
        total = total + from_after[rows, :].astype(F32)
        grad_queries[:, rows] = jnp.transpose(total).astype(BF16)


def add_low(*parts):
    total = parts[0].astype(F32)
    for part in parts[1:]:
        total = total + part.astype(F32)
    return total.astype(BF16)


def shards(queries, keys, values, grad_y, out_weight, bar_start, related, bar_summary_token):
    params = pltpu.CompilerParams(vmem_limit_bytes=VMEM_LIMIT)
    dma = pltpu.SemaphoreType.DMA
    grad_other = lax.ppermute(grad_y, "head", [(0, 1), (1, 0)])
    half = grad_y.shape[1]
    core = jnp.reshape(lax.axis_index("head"), (1,))
    partial, query_pack, own, sums = pl.pallas_call(
        pack_kernel,
        out_shape=(
            shape((FEAT, TOK), F32),
            shape((ROWS, FEAT)),
            shape((ROWS, FEAT)),
            shape((NXY, BARS_HERE, 2 * FEAT)),
        ),
        in_specs=[whole(SMEM)] * 4 + [whole(HBM)] * 5,
        out_specs=(whole(VMEM),) * 4,
        scratch_shapes=[VMEM((FEAT, half), BF16), VMEM(grad_y.shape, BF16), dma((6,))],
        compiler_params=params,
    )(
        core,
        *pinned(bar_start, related, bar_summary_token),
        *pinned(queries, keys, values, grad_y, out_weight),
    )
    packed = pl.pallas_call(
        grad_pack_kernel,
        out_shape=shape((ROWS, FEAT)),
        in_specs=[whole(SMEM)] + [whole(VMEM)] * 3 + [whole(HBM)],
        out_specs=whole(VMEM),
        scratch_shapes=[VMEM((FEAT, half), BF16), dma],
        compiler_params=params,
    )(
        core,
        *[pltpu.with_memory_space_constraint(x, VMEM) for x in (query_pack, partial)],
        grad_other,
        *pinned(out_weight),
    )

    after, before = [packed], [packed]

    def ring_step():
        after.append(lax.ppermute(after[-1], "seq", TO_PREVIOUS))
        before.append(lax.ppermute(before[-1], "seq", TO_NEXT))

    ring_step()
    all_sums = lax.all_to_all(sums, "seq", 0, 0, axis_index_groups=XY_GROUPS)
    after[1], before[1], all_sums = lax.optimization_barrier((after[1], before[1], all_sums))
    all_sums = all_sums.reshape(NXY * BARS_HERE, 2 * FEAT)
    ring_step()
    previous = lax.ppermute(own, "seq", ROW_UP)
    after[2], before[2], previous = lax.optimization_barrier((after[2], before[2], previous))
    ring_step()
    after.append(lax.ppermute(after[-1], "seq", TO_PREVIOUS))
    chunks = after + before[:0:-1]

    bars = NXY * BARS_HERE
    bias_shape = (REACH + 1 + NZ, TOK, TOK)
    stats_shape = (NZ, NZ, 2 * HEADS_HERE, TOK)
    held = [
        VMEM((NZ, ROWS, FEAT), BF16),
        VMEM((2, ROWS, FEAT), BF16),
        VMEM((bars, 2 * FEAT), BF16),
        VMEM(bias_shape, F32),
    ]
    def stats_of(order, *earlier):
        out = (shape(stats_shape, F32),) if earlier else (shape(stats_shape[1:], F32),)
        blocks = (len(bias_blocks(order)),) + bias_shape[1:]
        return pl.pallas_call(
            lambda *refs: stats_kernel(order, *refs),
            out_shape=out + (shape(blocks, F32),),
            in_specs=[whole(HBM)] * (len(order) + 3) + [whole(VMEM)] * len(earlier),
            out_specs=(whole(VMEM), whole(HBM)),
            scratch_shapes=held + [dma((3,)), dma((NZ,)), dma(bias_shape[:1])],
            compiler_params=params,
        )(*[chunks[o] for o in order], own, previous, all_sums, *earlier)

    partial_stats, bias_most = stats_of(EARLY)
    stats, bias_last = stats_of(LATE, partial_stats)

    stats = lax.all_to_all(stats, "seq", 0, 0, axis_index_groups=Z_GROUPS)

    coarse_shape = (NZ, 2, HEADS_HERE, bars, TOK)
    window_shape = (REACH + 1, 2, HEADS_HERE, TOK, TOK)
    *grads, coarse, window, previous_grad = pl.pallas_call(
        query_grad_kernel,
        out_shape=(shape((FEAT, TOK)),) * NZ
        + (shape(coarse_shape), shape(window_shape), shape((2 * TOK, FEAT))),
        in_specs=[whole(HBM)] * (NZ + 6),
        out_specs=(whole(VMEM),) * NZ + (whole(HBM),) * 2 + (whole(VMEM),),
        scratch_shapes=held
        + [
            VMEM(stats_shape, F32),
            VMEM(stats_shape[1:], F32),
            VMEM(coarse_shape, BF16),
            VMEM(window_shape, BF16),
            dma((3,)),
            dma((NZ,)),
            dma(bias_shape[:1]),
            dma,
            dma((2, NZ)),
        ],
        compiler_params=params,
    )(*chunks, own, previous, all_sums, bias_most, bias_last, stats)

    def forward_step(array):
        return lax.ppermute(array, "seq", TO_NEXT)

    def backward_step(array):
        return lax.ppermute(array, "seq", TO_PREVIOUS)

    forward, backward = forward_step(grads[4]), backward_step(grads[5])
    arrived = lax.ppermute(previous_grad, "seq", ROW_DOWN)
    own_grad, *sum_grads = pl.pallas_call(
        key_grad_kernel,
        out_shape=(shape((2 * TOK, FEAT), F32),) + (shape((NX * BARS_HERE, 2 * FEAT)),) * NY,
        in_specs=[whole(HBM)] * (NZ + 2),
        out_specs=(whole(VMEM),) * (1 + NY),
        scratch_shapes=[
            VMEM((NZ, ROWS, FEAT), BF16),
            VMEM(coarse_shape, BF16),
            VMEM(window_shape, BF16),
            VMEM((NXY, BARS_HERE, 2 * FEAT), F32),
            dma((NZ + 2,)),
        ],
        compiler_params=params,
    )(*[chunks[o] for o in ORDER], coarse, window)

    move = lambda array, *by: lax.ppermute(array, "seq", route(*by))
    forward, backward = forward_step(add_low(forward, grads[3])), backward_step(add_low(backward, grads[6]))
    moved = [move(sum_grads[i], -i, 0, 0) for i in range(1, NY)]
    forward, backward, *moved = lax.optimization_barrier((forward, backward, *moved))
    forward, backward = forward_step(add_low(forward, grads[2])), backward_step(add_low(backward, grads[7]))
    row_grad = add_low(sum_grads[0], *moved)
    parts = [
        move(row_grad[k * BARS_HERE : (k + 1) * BARS_HERE], 0, -k, 0) for k in range(1, NX)
    ]
    forward, backward, *parts = lax.optimization_barrier((forward, backward, *parts))
    forward = forward_step(add_low(forward, grads[1]))

    grad_queries, grad_keys, grad_values = pl.pallas_call(
        finish_kernel,
        out_shape=(shape((TOK, FEAT)),) * 3,
        in_specs=[whole(SMEM)] * 2 + [whole(VMEM)] * 9,
        out_specs=(whole(VMEM),) * 3,
    )(
        *pinned(bar_start, bar_summary_token),
        own_grad,
        arrived,
        row_grad,
        *parts,
        grads[0],
        forward,
        backward,
    )
    return grad_queries, grad_keys, grad_values


def solution(mesh):
    in_specs = (
        P("seq", "head"),
        P("seq", "head"),
        P("seq", "head"),
        P("seq", "head"),
        P("head", None),
        P("seq"),
        P("seq", None),
        P("seq"),
    )
    out_specs = (P("seq", "head"), P("seq", "head"), P("seq", "head"))
    return jax.shard_map(shards, mesh=mesh, in_specs=in_specs, out_specs=out_specs, check_vma=False)
```

```python
import math

import jax
import jax.numpy as jnp
from jax import lax
from jax.experimental import pallas as pl
from jax.experimental.pallas import tpu as pltpu
from jax.sharding import PartitionSpec as P

HD = 128
REACH = 4
TOK = 128
BARS_HERE = 8
HEADS_HERE = 4
FEAT = HD * HEADS_HERE
META = 16
ROWS = 2 * TOK + META
NZ = 8
NY = 4
NX = 4
NXY = NY * NX
N_SEQ = NZ * NXY
OFFSETS = (1, 2, 4, 8, 12, 16, 24, 32)
SCALE = HD ** (-0.5)
LOG2E = math.log2(math.e)
EXP_SCALE = SCALE * LOG2E
LOWEST = -1e30

Z_GROUPS = [[j * NZ + z for z in range(NZ)] for j in range(NXY)]
XY_GROUPS = [[j * NZ + z for j in range(NXY)] for z in range(NZ)]


def route(dy, dx, dz):
    return [
        ((y * NX + x) * NZ + z, ((y + dy) % NY * NX + (x + dx) % NX) * NZ + (z + dz) % NZ)
        for y in range(NY)
        for x in range(NX)
        for z in range(NZ)
    ]


TO_NEXT = route(0, 0, 1)
TO_PREVIOUS = route(0, 0, -1)
ROW_UP = [(i, i + NZ) for i in range(N_SEQ - NZ) if i % NZ >= NZ - REACH]
ROW_DOWN = [(dst, src) for src, dst in ROW_UP]
EARLY = (0, 1, 7, 2, 6, 3, 5)
LATE = (4,)
ORDER = EARLY + LATE
TOGETHER = 2

VMEM_LIMIT = 50 * 2**20
SMEM = pltpu.SMEM
VMEM = pltpu.VMEM
HBM = pltpu.HBM
NT = (((1,), (1,)), ((), ()))
TN = (((0,), (0,)), ((), ()))
BF16 = jnp.bfloat16
F32 = jnp.float32


def whole(space):
    return pl.BlockSpec(memory_space=space)


def shape(dims, dtype=BF16):
    return jax.ShapeDtypeStruct(dims, dtype)


def pinned(*arrays):
    return [pltpu.with_memory_space_constraint(array, HBM) for array in arrays]


def local_bar(starts, positions):
    count = jnp.zeros_like(positions)
    for b in range(1, BARS_HERE):
        count = count + (positions >= starts[b]).astype(jnp.int32)
    return count


def low(flags):
    return flags.astype(F32).astype(BF16)


def pack_kernel(
    core, starts, related, slots, queries, keys, values, grad_own, out_weight,
    partial, query_pack, key_pack, sums, weight, grad, sems,
):
    half = grad_own.shape[1]
    copies = [pltpu.make_async_copy(grad_own, grad, sems.at[0])]
    cols = pl.ds(pl.multiple_of(core[0] * half, half), half)
    copies.append(pltpu.make_async_copy(out_weight.at[:, cols], weight, sems.at[1]))
    copies.append(pltpu.make_async_copy(queries, query_pack.at[pl.ds(0, TOK)], sems.at[3]))
    copies.append(pltpu.make_async_copy(keys, key_pack.at[pl.ds(0, TOK)], sems.at[4]))
    copies.append(pltpu.make_async_copy(values, key_pack.at[pl.ds(TOK, TOK)], sems.at[5]))
    for copy in copies:
        copy.start()
    base = starts[0]
    lane = lax.broadcasted_iota(jnp.int32, (META, TOK), 1)
    row = lax.broadcasted_iota(jnp.int32, (META, TOK), 0)
    bar = local_bar(starts, lane + base)
    info = jnp.where(row == 0, bar, 0)
    for j in range(len(OFFSETS)):
        entry = jnp.zeros((META, TOK), jnp.int32)
        for b in range(BARS_HERE):
            has = (related[b, j] >= 0).astype(jnp.int32)
            entry = jnp.where(bar == b, has, entry)
        info = jnp.where(row == j + 1, entry, info)
    query_pack[TOK:, :] = jnp.zeros((TOK + META, FEAT), BF16)
    query_pack[2 * TOK :, 0:TOK] = low(info)
    key_pack[2 * TOK :, :] = jnp.zeros((META, FEAT), BF16)
    key_pack[2 * TOK :, 0:TOK] = low(bar)
    slot = jnp.full((META, TOK), -1, jnp.int32)
    for b in range(BARS_HERE):
        slot = jnp.where(row == b, slots[b] - base, slot)
    pick = low(lane == slot)
    for copy in copies[2:]:
        copy.wait()
    for kind in range(2):
        source = key_pack[kind * TOK : (kind + 1) * TOK, :]
        rows = jnp.dot(pick, source, preferred_element_type=F32)[0:BARS_HERE].astype(BF16)
        for h in range(HEADS_HERE):
            at = (2 * h + kind) * HD
            for j in range(NXY):
                sums[j, :, at : at + HD] = rows[:, h * HD : (h + 1) * HD]
    for copy in copies[:2]:
        copy.wait()
    partial[...] = lax.dot_general(weight[...], grad[...], NT, preferred_element_type=F32)


def grad_pack_kernel(core, pack, partial, grad_other, out_weight, packed, weight, sem):
    half = grad_other.shape[1]
    cols = pl.ds(pl.multiple_of((1 - core[0]) * half, half), half)
    copy = pltpu.make_async_copy(out_weight.at[:, cols], weight, sem)
    copy.start()
    packed[0:TOK, :] = pack[0:TOK, :]
    packed[2 * TOK :, :] = pack[2 * TOK :, :]
    copy.wait()
    turned = partial[...] + lax.dot_general(
        weight[...], grad_other[...], NT, preferred_element_type=F32
    )
    for h in range(HEADS_HERE):
        cols = slice(h * HD, (h + 1) * HD)
        packed[TOK : 2 * TOK, cols] = jnp.transpose(turned[cols]).astype(BF16)


def place():
    rank = lax.axis_index("seq")
    return rank, jnp.bitwise_and(rank, NZ - 1)


def load_keys(own, previous, sums, pairs, keys, sems):
    copies = [
        pltpu.make_async_copy(own, pairs.at[0], sems.at[0]),
        pltpu.make_async_copy(previous, pairs.at[1], sems.at[1]),
        pltpu.make_async_copy(sums, keys, sems.at[2]),
    ]
    for copy in copies:
        copy.start()
    return copies


class Bias:
    def __init__(self, packed, pairs):
        rank, self.z = place()
        self.row_start = rank - self.z
        self.packed = packed
        self.local = [
            jnp.transpose(
                jnp.broadcast_to(pairs[i, 2 * TOK :, 0:TOK].astype(F32)[0:1], (TOK, TOK))
            ).astype(jnp.int32)
            for i in range(2)
        ]
        self.key_row = lax.broadcasted_iota(jnp.int32, (TOK, TOK), 0)
        self.token_col = lax.broadcasted_iota(jnp.int32, (TOK, TOK), 1)
        owner = lax.shift_right_logical(self.key_row, 3) * NZ + self.z
        self.summary_bar = owner * BARS_HERE + jnp.bitwise_and(self.key_row, BARS_HERE - 1)

    def build(self, o, bias):
        owner = self.row_start + jnp.bitwise_and(self.z + o, NZ - 1)
        info = self.packed[o, 2 * TOK :, 0:TOK].astype(F32).astype(jnp.int32)
        token_bar = info[0:1] + owner * BARS_HERE
        rel = [
            jnp.where(info[j + 1 : j + 2] > 0, token_bar - OFFSETS[j], -1)
            for j in range(len(OFFSETS))
        ]
        if o <= REACH:
            key_owner = owner - o
            key_local = jnp.where(self.z + o >= NZ, self.local[1], self.local[0])
            key_bar = jnp.where(key_owner >= 0, key_local + key_owner * BARS_HERE, -2)
            seen = key_bar == rel[0]
            for entry in rel[1:]:
                seen = seen | (key_bar == entry)
            if o == 0:
                seen = seen | ((key_bar == token_bar) & (self.key_row <= self.token_col))
            bias[o] = jnp.where(seen, 0.0, -jnp.inf)
        hidden = self.summary_bar >= token_bar
        for entry in rel:
            hidden = hidden | (self.summary_bar == entry)
        bias[REACH + 1 + o] = jnp.where(hidden, -jnp.inf, 0.0)


def bias_blocks(order):
    return [o for o in order if o <= REACH] + [REACH + 1 + o for o in order]


def products(packed, pairs, keys, bias, h, o):
    _, z = place()
    cols = slice(h * HD, (h + 1) * HD)
    at = 2 * h * HD
    query = packed[o, 0:TOK, cols]
    grad = packed[o, TOK : 2 * TOK, cols]
    key, value = keys[:, at : at + HD], keys[:, at + HD : at + 2 * HD]
    mask = bias[REACH + 1 + o]
    if o <= REACH:
        side = lax.shift_right_logical(z + o, 3)
        key = jnp.concatenate([pairs[side, 0:TOK, cols], key], axis=0)
        value = jnp.concatenate([pairs[side, TOK : 2 * TOK, cols], value], axis=0)
        mask = jnp.concatenate([bias[o], mask], axis=0)
    scores = lax.dot_general(key, query, NT, preferred_element_type=F32)
    dprobs = lax.dot_general(value, grad, NT, preferred_element_type=F32)
    return key, scores, dprobs, mask


def stats_kernel(order, *refs):
    chunks, (own, previous, sums), refs = refs[: len(order)], refs[len(order) : len(order) + 3], refs[len(order) + 3 :]
    earlier, refs = (refs[0], refs[1:]) if len(order) < REACH else (None, refs)
    stats, bias_out, packed, pairs, keys, bias, key_sems, chunk_sems, bias_sems = refs
    key_copies = load_keys(own, previous, sums, pairs, keys, key_sems)
    copies = [
        pltpu.make_async_copy(chunk, packed.at[o], chunk_sems.at[o])
        for o, chunk in zip(order, chunks)
    ]
    for copy in copies:
        copy.start()
    for copy in key_copies:
        copy.wait()
    masks = Bias(packed, pairs)
    writes = []
    for i, o in enumerate(order):
        copies[i].wait()
        masks.build(o, bias)
        for block in bias_blocks((o,)):
            place_out = bias_out.at[bias_blocks(order).index(block)]
            writes.append(pltpu.make_async_copy(bias.at[block], place_out, bias_sems.at[block]))
            writes[-1].start()
        chunk = jnp.bitwise_and(masks.z + o, NZ - 1)
        log_sums, means = [], []
        made = [products(packed, pairs, keys, bias, h, o) for h in range(HEADS_HERE)]
        for _, scores, dprobs, mask in made:
            scores = scores + mask
            top = jnp.maximum(jnp.max(scores, axis=0, keepdims=True), LOWEST)
            weights = jnp.exp2((scores - top) * EXP_SCALE)
            total = jnp.sum(weights, axis=0, keepdims=True)
            weighted = jnp.sum(weights * dprobs, axis=0, keepdims=True)
            log_sums.append(top * EXP_SCALE + jnp.log(total) * LOG2E)
            means.append(jnp.where(total > 0.0, weighted / total, 0.0))
        merged = jnp.concatenate(log_sums + means, axis=0)
        if earlier is None:
            stats[chunk] = merged
            continue
        for peer in range(NZ):
            stats[peer] = earlier[...]
            stats[peer, chunk] = merged
    for copy in writes:
        copy.wait()


def merge_stats(stats, merged):
    top = stats[0, :, 0:HEADS_HERE, :]
    for i in range(1, NZ):
        top = jnp.maximum(top, stats[i, :, 0:HEADS_HERE, :])
    total = jnp.zeros_like(top)
    mean = jnp.zeros_like(top)
    for i in range(NZ):
        weight = jnp.exp2(stats[i, :, 0:HEADS_HERE, :] - top)
        total = total + weight
        mean = mean + weight * stats[i, :, HEADS_HERE:, :]
    merged[:, 0:HEADS_HERE, :] = top + jnp.log(total) * LOG2E
    merged[:, HEADS_HERE:, :] = mean / total


def query_grad_kernel(*refs):
    order = ORDER
    near = [o for o in order if o <= REACH]
    chunks, refs = refs[:NZ], refs[NZ:]
    own, previous, sums, bias_most, bias_last, stats_in, *refs = refs
    query_grads, (coarse_out, window_out, previous_grad), refs = refs[:NZ], refs[NZ : NZ + 3], refs[NZ + 3 :]
    packed, pairs, keys, bias, stats, merged, coarse, window, *refs = refs
    key_sems, chunk_sems, bias_sems, stats_sem, out_sems = refs
    stats_copy = pltpu.make_async_copy(stats_in, stats, stats_sem)
    stats_copy.start()
    key_copies = load_keys(own, previous, sums, pairs, keys, key_sems)
    copies = []
    for i, o in enumerate(order):
        mine = [pltpu.make_async_copy(chunks[o], packed.at[o], chunk_sems.at[o])]
        for block in bias_blocks((o,)):
            source, among = (bias_most, EARLY) if o in EARLY else (bias_last, LATE)
            source = source.at[bias_blocks(among).index(block)]
            mine.append(pltpu.make_async_copy(source, bias.at[block], bias_sems.at[block]))
        for copy in mine:
            copy.start()
        copies.append(mine)
    stats_copy.wait()
    merge_stats(stats, merged)
    for copy in key_copies:
        copy.wait()
    _, z = place()
    keys_turned = [
        jnp.transpose(keys[:, 2 * h * HD : (2 * h + 1) * HD]) for h in range(HEADS_HERE)
    ]
    pairs_turned = [
        [jnp.transpose(pairs[i, 0:TOK, h * HD : (h + 1) * HD]) for i in range(2)]
        for h in range(HEADS_HERE)
    ]
    writes = []
    others = [[None, None] for _ in range(HEADS_HERE)]
    for first in range(0, NZ, TOGETHER):
        group = range(first, first + TOGETHER)
        for i in group:
            for copy in copies[i]:
                copy.wait()
        units = [(i, order[i], h) for i in group for h in range(HEADS_HERE)]
        made = [products(packed, pairs, keys, bias, h, o) for _, o, h in units]
        low_parts = []
        for (i, o, h), (_, scores, dprobs, mask) in zip(units, made):
            chunk = jnp.bitwise_and(z + o, NZ - 1)
            log_sum = merged[chunk, h : h + 1, :]
            delta = merged[chunk, HEADS_HERE + h : HEADS_HERE + h + 1, :]
            probs = jnp.exp2(scores * EXP_SCALE - log_sum + mask)
            low_parts.append(((probs * (dprobs - delta)).astype(BF16), probs.astype(BF16)))
        for (i, o, h), (dscores, probs_low) in zip(units, low_parts):
            turned = keys_turned[h]
            if o <= REACH:
                side = pairs_turned[h][0]
                if o > 0:
                    side = jnp.where(z + o >= NZ, pairs_turned[h][1], side)
                turned = jnp.concatenate([side, turned], axis=1)
            dquery = jnp.dot(turned, dscores, preferred_element_type=F32)
            turned = jnp.transpose(SCALE * dquery)
            query_grads[o][:, h * HD : (h + 1) * HD] = turned.astype(BF16)
        for (i, o, h), (dscores, probs_low) in zip(units, low_parts):
            if o <= REACH:
                window[near.index(o), 0, h] = dscores[0:TOK]
                window[near.index(o), 1, h] = probs_low[0:TOK]
            if 0 < o <= REACH:
                wraps = (z + o >= NZ).astype(F32)
                cols = slice(h * HD, (h + 1) * HD)
                for kind, left in enumerate((dscores, probs_low)):
                    right = packed[o, kind * TOK : (kind + 1) * TOK, cols]
                    part = wraps * jnp.dot(left[0:TOK], right, preferred_element_type=F32)
                    old = others[h][kind]
                    others[h][kind] = part if old is None else old + part
            coarse[i, 0, h] = dscores[-TOK:]
            coarse[i, 1, h] = probs_low[-TOK:]
        for i in group:
            o = order[i]
            writes.append(pltpu.make_async_copy(coarse.at[i], coarse_out.at[i], out_sems.at[0, o]))
            writes[-1].start()
            if o <= REACH:
                at = near.index(o)
                writes.append(
                    pltpu.make_async_copy(window.at[at], window_out.at[at], out_sems.at[1, o])
                )
                writes[-1].start()
    for h in range(HEADS_HERE):
        cols = slice(h * HD, (h + 1) * HD)
        previous_grad[0:TOK, cols] = (others[h][0] * SCALE).astype(BF16)
        previous_grad[TOK : 2 * TOK, cols] = others[h][1].astype(BF16)
    for copy in writes:
        copy.wait()


def key_grad_kernel(*refs):
    order = ORDER
    near = [o for o in order if o <= REACH]
    chunks, (coarse_in, window_in), refs = refs[:NZ], refs[NZ : NZ + 2], refs[NZ + 2 :]
    own_grad, sum_grad, packed, coarse, window, sems = refs
    copies = []
    for i, o in enumerate(order):
        mine = [pltpu.make_async_copy(chunks[i], packed.at[i], sems.at[0, i])]
        mine.append(pltpu.make_async_copy(coarse_in.at[i], coarse.at[i], sems.at[1, i]))
        if o in near:
            at = near.index(o)
            mine.append(pltpu.make_async_copy(window_in.at[at], window.at[at], sems.at[2, i]))
        for copy in mine:
            copy.start()
        copies.append(mine)
    _, z = place()
    units = [(h, kind) for h in range(HEADS_HERE) for kind in range(2)]
    totals, mine = [None] * len(units), [None] * len(units)
    half = NZ // 2
    for first in range(0, NZ, half):
        group = range(first, first + half)
        for i in group:
            for copy in copies[i]:
                copy.wait()
        for unit, (h, kind) in enumerate(units):
            cols = slice(h * HD, (h + 1) * HD)
            tokens = [packed[i, kind * TOK : (kind + 1) * TOK, cols] for i in group]
            part = jnp.dot(
                jnp.concatenate([coarse[i, kind, h] for i in group], axis=1),
                jnp.concatenate(tokens, axis=0),
                preferred_element_type=F32,
            )
            totals[unit] = part if first == 0 else totals[unit] + part
            for i in group:
                if order[i] in near:
                    part = jnp.dot(
                        window[near.index(order[i]), kind, h],
                        tokens[i - first],
                        preferred_element_type=F32,
                    )
                    part = part * (z + order[i] < NZ).astype(F32)
                    mine[unit] = part if mine[unit] is None else mine[unit] + part
    for unit, (h, kind) in enumerate(units):
        scale = SCALE if kind == 0 else 1.0
        at = (2 * h + kind) * HD
        own_grad[kind * TOK : (kind + 1) * TOK, h * HD : (h + 1) * HD] = mine[unit] * scale
        sum_grad[:, at : at + HD] = (totals[unit] * scale).astype(BF16)


def finish_kernel(starts, slots, own_grad, arrived, parts, grad_keys, grad_values):
    base = starts[0]
    total = parts[0].astype(F32)
    for i in range(1, NXY):
        total = total + parts[i].astype(F32)
    high = total.astype(BF16).astype(F32)
    halves = jnp.concatenate([high, total - high], axis=0).astype(BF16)
    lane = lax.broadcasted_iota(jnp.int32, (2 * BARS_HERE, TOK), 1)
    row = lax.broadcasted_iota(jnp.int32, (2 * BARS_HERE, TOK), 0)
    slot = jnp.full((2 * BARS_HERE, TOK), -1, jnp.int32)
    for b in range(BARS_HERE):
        slot = jnp.where(jnp.bitwise_and(row, BARS_HERE - 1) == b, slots[b] - base, slot)
    placed = lax.dot_general(low(lane == slot), halves, TN, preferred_element_type=F32)
    for h in range(HEADS_HERE):
        cols = slice(h * HD, (h + 1) * HD)
        for kind, out in ((0, grad_keys), (1, grad_values)):
            rows = slice(kind * TOK, (kind + 1) * TOK)
            at = (2 * h + kind) * HD
            grad = own_grad[rows, cols] + arrived[rows, cols].astype(F32)
            out[:, cols] = (grad + placed[:, at : at + HD]).astype(BF16)


def add_low(*parts):
    total = parts[0].astype(F32)
    for part in parts[1:]:
        total = total + part.astype(F32)
    return total.astype(BF16)


def shards(queries, keys, values, grad_y, out_weight, bar_start, related, bar_summary_token):
    params = pltpu.CompilerParams(vmem_limit_bytes=VMEM_LIMIT)
    dma = pltpu.SemaphoreType.DMA
    grad_other = lax.ppermute(grad_y, "head", [(0, 1), (1, 0)])
    half = grad_y.shape[1]
    core = jnp.reshape(lax.axis_index("head"), (1,))
    partial, query_pack, own, sums = pl.pallas_call(
        pack_kernel,
        out_shape=(
            shape((FEAT, TOK), F32),
            shape((ROWS, FEAT)),
            shape((ROWS, FEAT)),
            shape((NXY, BARS_HERE, 2 * FEAT)),
        ),
        in_specs=[whole(SMEM)] * 4 + [whole(HBM)] * 5,
        out_specs=(whole(VMEM),) * 4,
        scratch_shapes=[VMEM((FEAT, half), BF16), VMEM(grad_y.shape, BF16), dma((6,))],
        compiler_params=params,
    )(
        core,
        *pinned(bar_start, related, bar_summary_token),
        *pinned(queries, keys, values, grad_y, out_weight),
    )
    packed = pl.pallas_call(
        grad_pack_kernel,
        out_shape=shape((ROWS, FEAT)),
        in_specs=[whole(SMEM)] + [whole(VMEM)] * 3 + [whole(HBM)],
        out_specs=whole(VMEM),
        scratch_shapes=[VMEM((FEAT, half), BF16), dma],
        compiler_params=params,
    )(
        core,
        *[pltpu.with_memory_space_constraint(x, VMEM) for x in (query_pack, partial)],
        grad_other,
        *pinned(out_weight),
    )

    after, before = [packed], [packed]

    def ring_step():
        after.append(lax.ppermute(after[-1], "seq", TO_PREVIOUS))
        before.append(lax.ppermute(before[-1], "seq", TO_NEXT))

    ring_step()
    all_sums = lax.all_to_all(sums, "seq", 0, 0, axis_index_groups=XY_GROUPS)
    after[1], before[1], all_sums = lax.optimization_barrier((after[1], before[1], all_sums))
    all_sums = all_sums.reshape(NXY * BARS_HERE, 2 * FEAT)
    ring_step()
    previous = lax.ppermute(own, "seq", ROW_UP)
    after[2], before[2], previous = lax.optimization_barrier((after[2], before[2], previous))
    ring_step()
    after.append(lax.ppermute(after[-1], "seq", TO_PREVIOUS))
    chunks = after + before[:0:-1]

    bars = NXY * BARS_HERE
    bias_shape = (REACH + 1 + NZ, TOK, TOK)
    stats_shape = (NZ, NZ, 2 * HEADS_HERE, TOK)
    held = [
        VMEM((NZ, ROWS, FEAT), BF16),
        VMEM((2, ROWS, FEAT), BF16),
        VMEM((bars, 2 * FEAT), BF16),
        VMEM(bias_shape, F32),
    ]
    def stats_of(order, *earlier):
        out = (shape(stats_shape, F32),) if earlier else (shape(stats_shape[1:], F32),)
        blocks = (len(bias_blocks(order)),) + bias_shape[1:]
        return pl.pallas_call(
            lambda *refs: stats_kernel(order, *refs),
            out_shape=out + (shape(blocks, F32),),
            in_specs=[whole(HBM)] * (len(order) + 3) + [whole(VMEM)] * len(earlier),
            out_specs=(whole(VMEM), whole(HBM)),
            scratch_shapes=held + [dma((3,)), dma((NZ,)), dma(bias_shape[:1])],
            compiler_params=params,
        )(*[chunks[o] for o in order], own, previous, all_sums, *earlier)

    partial_stats, bias_most = stats_of(EARLY)
    stats, bias_last = stats_of(LATE, partial_stats)

    stats = lax.all_to_all(stats, "seq", 0, 0, axis_index_groups=Z_GROUPS)

    coarse_shape = (NZ, 2, HEADS_HERE, bars, TOK)
    window_shape = (REACH + 1, 2, HEADS_HERE, TOK, TOK)
    *grads, coarse, window, previous_grad = pl.pallas_call(
        query_grad_kernel,
        out_shape=(shape((TOK, FEAT)),) * NZ
        + (shape(coarse_shape), shape(window_shape), shape((2 * TOK, FEAT))),
        in_specs=[whole(HBM)] * (NZ + 6),
        out_specs=(whole(VMEM),) * NZ + (whole(HBM),) * 2 + (whole(VMEM),),
        scratch_shapes=held
        + [
            VMEM(stats_shape, F32),
            VMEM(stats_shape[1:], F32),
            VMEM(coarse_shape, BF16),
            VMEM(window_shape, BF16),
            dma((3,)),
            dma((NZ,)),
            dma(bias_shape[:1]),
            dma,
            dma((2, NZ)),
        ],
        compiler_params=params,
    )(*chunks, own, previous, all_sums, bias_most, bias_last, stats)

    def forward_step(array):
        return lax.ppermute(array, "seq", TO_NEXT)

    def backward_step(array):
        return lax.ppermute(array, "seq", TO_PREVIOUS)

    forward, backward = forward_step(grads[4]), backward_step(grads[5])
    arrived = lax.ppermute(previous_grad, "seq", ROW_DOWN)
    own_grad, sum_grad = pl.pallas_call(
        key_grad_kernel,
        out_shape=(shape((2 * TOK, FEAT), F32), shape((bars, 2 * FEAT))),
        in_specs=[whole(HBM)] * (NZ + 2),
        out_specs=(whole(VMEM),) * 2,
        scratch_shapes=[
            VMEM((NZ, ROWS, FEAT), BF16),
            VMEM(coarse_shape, BF16),
            VMEM(window_shape, BF16),
            dma((3, NZ)),
        ],
        compiler_params=params,
    )(*[chunks[o] for o in ORDER], coarse, window)

    forward, backward, sum_grad = lax.optimization_barrier((forward, backward, sum_grad))
    forward, backward = forward_step(add_low(forward, grads[3])), backward_step(add_low(backward, grads[6]))
    parts = lax.all_to_all(
        sum_grad.reshape(NXY, BARS_HERE, 2 * FEAT), "seq", 0, 0, axis_index_groups=XY_GROUPS
    )
    forward, backward, parts = lax.optimization_barrier((forward, backward, parts))
    forward, backward = forward_step(add_low(forward, grads[2])), backward_step(add_low(backward, grads[7]))
    forward = forward_step(add_low(forward, grads[1]))

    grad_keys, grad_values = pl.pallas_call(
        finish_kernel,
        out_shape=(shape((TOK, FEAT)),) * 2,
        in_specs=[whole(SMEM)] * 2 + [whole(VMEM)] * 3,
        out_specs=(whole(VMEM),) * 2,
    )(*pinned(bar_start, bar_summary_token), own_grad, arrived, parts)
    grad_queries = add_low(grads[0], forward, backward)
    return grad_queries, grad_keys, grad_values


def solution(mesh):
    in_specs = (
        P("seq", "head"),
        P("seq", "head"),
        P("seq", "head"),
        P("seq", "head"),
        P("head", None),
        P("seq"),
        P("seq", None),
        P("seq"),
    )
    out_specs = (P("seq", "head"), P("seq", "head"), P("seq", "head"))
    return jax.shard_map(shards, mesh=mesh, in_specs=in_specs, out_specs=out_specs, check_vma=False)
```

```python
import math

import jax
import jax.numpy as jnp
from jax import lax
from jax.experimental import pallas as pl
from jax.experimental.pallas import tpu as pltpu
from jax.sharding import PartitionSpec as P

HD = 128
REACH = 4
TOK = 128
BARS_HERE = 8
HEADS_HERE = 4
FEAT = HD * HEADS_HERE
META = 16
ROWS = 2 * TOK + META
NZ = 8
NY = 4
NX = 4
NXY = NY * NX
N_SEQ = NZ * NXY
OFFSETS = (1, 2, 4, 8, 12, 16, 24, 32)
SCALE = HD ** (-0.5)
LOG2E = math.log2(math.e)
EXP_SCALE = SCALE * LOG2E
LOWEST = -1e30

Z_GROUPS = [[j * NZ + z for z in range(NZ)] for j in range(NXY)]
XY_GROUPS = [[j * NZ + z for j in range(NXY)] for z in range(NZ)]


def route(dy, dx, dz):
    return [
        ((y * NX + x) * NZ + z, ((y + dy) % NY * NX + (x + dx) % NX) * NZ + (z + dz) % NZ)
        for y in range(NY)
        for x in range(NX)
        for z in range(NZ)
    ]


TO_NEXT = route(0, 0, 1)
TO_PREVIOUS = route(0, 0, -1)
ROW_UP = [(i, i + NZ) for i in range(N_SEQ - NZ) if i % NZ >= NZ - REACH]
ROW_DOWN = [(dst, src) for src, dst in ROW_UP]
EARLY = (0, 1, 7, 2, 6, 3, 5)
LATE = (4,)
LEADING = (4, 5)
TRAILING = (3, 6, 2, 7, 1, 0)
ORDER = LEADING + TRAILING
TOGETHER = 2

VMEM_LIMIT = 50 * 2**20
SMEM = pltpu.SMEM
VMEM = pltpu.VMEM
HBM = pltpu.HBM
NT = (((1,), (1,)), ((), ()))
TN = (((0,), (0,)), ((), ()))
BF16 = jnp.bfloat16
F32 = jnp.float32


def whole(space):
    return pl.BlockSpec(memory_space=space)


def shape(dims, dtype=BF16):
    return jax.ShapeDtypeStruct(dims, dtype)


def pinned(*arrays):
    return [pltpu.with_memory_space_constraint(array, HBM) for array in arrays]


def local_bar(starts, positions):
    count = jnp.zeros_like(positions)
    for b in range(1, BARS_HERE):
        count = count + (positions >= starts[b]).astype(jnp.int32)
    return count


def low(flags):
    return flags.astype(F32).astype(BF16)


def pack_kernel(
    core, starts, related, slots, queries, keys, values, grad_own, out_weight,
    partial, query_pack, key_pack, sums, weight, grad, sems,
):
    half = grad_own.shape[1]
    copies = [pltpu.make_async_copy(grad_own, grad, sems.at[0])]
    cols = pl.ds(pl.multiple_of(core[0] * half, half), half)
    copies.append(pltpu.make_async_copy(out_weight.at[:, cols], weight, sems.at[1]))
    copies.append(pltpu.make_async_copy(queries, query_pack.at[pl.ds(0, TOK)], sems.at[3]))
    copies.append(pltpu.make_async_copy(keys, key_pack.at[pl.ds(0, TOK)], sems.at[4]))
    copies.append(pltpu.make_async_copy(values, key_pack.at[pl.ds(TOK, TOK)], sems.at[5]))
    for copy in copies:
        copy.start()
    base = starts[0]
    lane = lax.broadcasted_iota(jnp.int32, (META, TOK), 1)
    row = lax.broadcasted_iota(jnp.int32, (META, TOK), 0)
    bar = local_bar(starts, lane + base)
    info = jnp.where(row == 0, bar, 0)
    for j in range(len(OFFSETS)):
        entry = jnp.zeros((META, TOK), jnp.int32)
        for b in range(BARS_HERE):
            has = (related[b, j] >= 0).astype(jnp.int32)
            entry = jnp.where(bar == b, has, entry)
        info = jnp.where(row == j + 1, entry, info)
    query_pack[TOK:, :] = jnp.zeros((TOK + META, FEAT), BF16)
    query_pack[2 * TOK :, 0:TOK] = low(info)
    key_pack[2 * TOK :, :] = jnp.zeros((META, FEAT), BF16)
    key_pack[2 * TOK :, 0:TOK] = low(bar)
    slot = jnp.full((META, TOK), -1, jnp.int32)
    for b in range(BARS_HERE):
        slot = jnp.where(row == b, slots[b] - base, slot)
    pick = low(lane == slot)
    for copy in copies[2:]:
        copy.wait()
    for kind in range(2):
        source = key_pack[kind * TOK : (kind + 1) * TOK, :]
        rows = jnp.dot(pick, source, preferred_element_type=F32)[0:BARS_HERE].astype(BF16)
        for h in range(HEADS_HERE):
            at = (2 * h + kind) * HD
            for j in range(NXY):
                sums[j, :, at : at + HD] = rows[:, h * HD : (h + 1) * HD]
    for copy in copies[:2]:
        copy.wait()
    partial[...] = lax.dot_general(weight[...], grad[...], NT, preferred_element_type=F32)


def grad_pack_kernel(core, pack, partial, grad_other, out_weight, packed, weight, sem):
    half = grad_other.shape[1]
    cols = pl.ds(pl.multiple_of((1 - core[0]) * half, half), half)
    copy = pltpu.make_async_copy(out_weight.at[:, cols], weight, sem)
    copy.start()
    packed[0:TOK, :] = pack[0:TOK, :]
    packed[2 * TOK :, :] = pack[2 * TOK :, :]
    copy.wait()
    turned = partial[...] + lax.dot_general(
        weight[...], grad_other[...], NT, preferred_element_type=F32
    )
    for h in range(HEADS_HERE):
        cols = slice(h * HD, (h + 1) * HD)
        packed[TOK : 2 * TOK, cols] = jnp.transpose(turned[cols]).astype(BF16)


def place():
    rank = lax.axis_index("seq")
    return rank, jnp.bitwise_and(rank, NZ - 1)


def load_keys(own, previous, sums, pairs, keys, sems):
    copies = [
        pltpu.make_async_copy(own, pairs.at[0], sems.at[0]),
        pltpu.make_async_copy(previous, pairs.at[1], sems.at[1]),
        pltpu.make_async_copy(sums, keys, sems.at[2]),
    ]
    for copy in copies:
        copy.start()
    return copies


class Bias:
    def __init__(self, packed, pairs):
        rank, self.z = place()
        self.row_start = rank - self.z
        self.packed = packed
        self.local = [
            jnp.transpose(
                jnp.broadcast_to(pairs[i, 2 * TOK :, 0:TOK].astype(F32)[0:1], (TOK, TOK))
            ).astype(jnp.int32)
            for i in range(2)
        ]
        self.key_row = lax.broadcasted_iota(jnp.int32, (TOK, TOK), 0)
        self.token_col = lax.broadcasted_iota(jnp.int32, (TOK, TOK), 1)
        owner = lax.shift_right_logical(self.key_row, 3) * NZ + self.z
        self.summary_bar = owner * BARS_HERE + jnp.bitwise_and(self.key_row, BARS_HERE - 1)

    def build(self, o, bias):
        owner = self.row_start + jnp.bitwise_and(self.z + o, NZ - 1)
        info = self.packed[o, 2 * TOK :, 0:TOK].astype(F32).astype(jnp.int32)
        token_bar = info[0:1] + owner * BARS_HERE
        rel = [
            jnp.where(info[j + 1 : j + 2] > 0, token_bar - OFFSETS[j], -1)
            for j in range(len(OFFSETS))
        ]
        if o <= REACH:
            key_owner = owner - o
            key_local = jnp.where(self.z + o >= NZ, self.local[1], self.local[0])
            key_bar = jnp.where(key_owner >= 0, key_local + key_owner * BARS_HERE, -2)
            seen = key_bar == rel[0]
            for entry in rel[1:]:
                seen = seen | (key_bar == entry)
            if o == 0:
                seen = seen | ((key_bar == token_bar) & (self.key_row <= self.token_col))
            bias[o] = jnp.where(seen, 0.0, -jnp.inf)
        hidden = self.summary_bar >= token_bar
        for entry in rel:
            hidden = hidden | (self.summary_bar == entry)
        bias[REACH + 1 + o] = jnp.where(hidden, -jnp.inf, 0.0)


def bias_blocks(order):
    return [o for o in order if o <= REACH] + [REACH + 1 + o for o in order]


def products(packed, pairs, keys, bias, h, o):
    _, z = place()
    cols = slice(h * HD, (h + 1) * HD)
    at = 2 * h * HD
    query = packed[o, 0:TOK, cols]
    grad = packed[o, TOK : 2 * TOK, cols]
    key, value = keys[:, at : at + HD], keys[:, at + HD : at + 2 * HD]
    mask = bias[REACH + 1 + o]
    if o <= REACH:
        side = lax.shift_right_logical(z + o, 3)
        key = jnp.concatenate([pairs[side, 0:TOK, cols], key], axis=0)
        value = jnp.concatenate([pairs[side, TOK : 2 * TOK, cols], value], axis=0)
        mask = jnp.concatenate([bias[o], mask], axis=0)
    scores = lax.dot_general(key, query, NT, preferred_element_type=F32)
    dprobs = lax.dot_general(value, grad, NT, preferred_element_type=F32)
    return key, scores, dprobs, mask


def stats_kernel(order, *refs):
    chunks, (own, previous, sums), refs = refs[: len(order)], refs[len(order) : len(order) + 3], refs[len(order) + 3 :]
    earlier, refs = (refs[0], refs[1:]) if len(order) < REACH else (None, refs)
    stats, bias_out, packed, pairs, keys, bias, key_sems, chunk_sems, bias_sems = refs
    key_copies = load_keys(own, previous, sums, pairs, keys, key_sems)
    copies = [
        pltpu.make_async_copy(chunk, packed.at[o], chunk_sems.at[o])
        for o, chunk in zip(order, chunks)
    ]
    for copy in copies:
        copy.start()
    for copy in key_copies:
        copy.wait()
    masks = Bias(packed, pairs)
    writes = []
    for i, o in enumerate(order):
        copies[i].wait()
        masks.build(o, bias)
        for block in bias_blocks((o,)):
            place_out = bias_out.at[bias_blocks(order).index(block)]
            writes.append(pltpu.make_async_copy(bias.at[block], place_out, bias_sems.at[block]))
            writes[-1].start()
        chunk = jnp.bitwise_and(masks.z + o, NZ - 1)
        log_sums, means = [], []
        made = [products(packed, pairs, keys, bias, h, o) for h in range(HEADS_HERE)]
        for _, scores, dprobs, mask in made:
            scores = scores + mask
            top = jnp.maximum(jnp.max(scores, axis=0, keepdims=True), LOWEST)
            weights = jnp.exp2((scores - top) * EXP_SCALE)
            total = jnp.sum(weights, axis=0, keepdims=True)
            weighted = jnp.sum(weights * dprobs, axis=0, keepdims=True)
            log_sums.append(top * EXP_SCALE + jnp.log(total) * LOG2E)
            means.append(jnp.where(total > 0.0, weighted / total, 0.0))
        merged = jnp.concatenate(log_sums + means, axis=0)
        if earlier is None:
            stats[chunk] = merged
            continue
        for peer in range(NZ):
            stats[peer] = earlier[...]
            stats[peer, chunk] = merged
    for copy in writes:
        copy.wait()


def merge_stats(stats, merged):
    top = stats[0, :, 0:HEADS_HERE, :]
    for i in range(1, NZ):
        top = jnp.maximum(top, stats[i, :, 0:HEADS_HERE, :])
    total = jnp.zeros_like(top)
    mean = jnp.zeros_like(top)
    for i in range(NZ):
        weight = jnp.exp2(stats[i, :, 0:HEADS_HERE, :] - top)
        total = total + weight
        mean = mean + weight * stats[i, :, HEADS_HERE:, :]
    merged[:, 0:HEADS_HERE, :] = top + jnp.log(total) * LOG2E
    merged[:, HEADS_HERE:, :] = mean / total


def query_grad_kernel(order, *refs):
    count = len(order)
    merging = order is LEADING
    near = [o for o in order if o <= REACH]
    chunks, (own, previous, sums, bias_most, bias_last, stats_in), refs = refs[:count], refs[count : count + 6], refs[count + 6 :]
    query_grads, (coarse_out, window_out), refs = refs[:count], refs[count : count + 2], refs[count + 2 :]
    merged_out, refs = (refs[0], refs[1:]) if merging else (None, refs)
    packed, pairs, keys, bias, stats, merged, coarse, window, *refs = refs
    key_sems, chunk_sems, bias_sems, stats_sem, out_sems = refs
    stats_copy = pltpu.make_async_copy(stats_in, stats, stats_sem)
    stats_copy.start()
    key_copies = load_keys(own, previous, sums, pairs, keys, key_sems)
    copies = []
    for i, o in enumerate(order):
        mine = [pltpu.make_async_copy(chunks[i], packed.at[o], chunk_sems.at[o])]
        for block in bias_blocks((o,)):
            source, among = (bias_most, EARLY) if o in EARLY else (bias_last, LATE)
            source = source.at[bias_blocks(among).index(block)]
            mine.append(pltpu.make_async_copy(source, bias.at[block], bias_sems.at[block]))
        for copy in mine:
            copy.start()
        copies.append(mine)
    stats_copy.wait()
    if merging:
        merge_stats(stats, merged)
        merged_out[...] = merged[...]
    else:
        merged = stats
    for copy in key_copies:
        copy.wait()
    _, z = place()
    keys_turned = [
        jnp.transpose(keys[:, 2 * h * HD : (2 * h + 1) * HD]) for h in range(HEADS_HERE)
    ]
    pairs_turned = [
        [jnp.transpose(pairs[i, 0:TOK, h * HD : (h + 1) * HD]) for i in range(2)]
        for h in range(HEADS_HERE)
    ]
    writes = []
    for first in range(0, count, TOGETHER):
        group = range(first, first + TOGETHER)
        for i in group:
            for copy in copies[i]:
                copy.wait()
        units = [(i, order[i], h) for i in group for h in range(HEADS_HERE)]
        made = [products(packed, pairs, keys, bias, h, o) for _, o, h in units]
        low_parts = []
        for (i, o, h), (_, scores, dprobs, mask) in zip(units, made):
            chunk = jnp.bitwise_and(z + o, NZ - 1)
            log_sum = merged[chunk, h : h + 1, :]
            delta = merged[chunk, HEADS_HERE + h : HEADS_HERE + h + 1, :]
            probs = jnp.exp2(scores * EXP_SCALE - log_sum + mask)
            low_parts.append(((probs * (dprobs - delta)).astype(BF16), probs.astype(BF16)))
        for (i, o, h), (dscores, probs_low) in zip(units, low_parts):
            turned = keys_turned[h]
            if o <= REACH:
                side = pairs_turned[h][0]
                if o > 0:
                    side = jnp.where(z + o >= NZ, pairs_turned[h][1], side)
                turned = jnp.concatenate([side, turned], axis=1)
            dquery = jnp.dot(turned, dscores, preferred_element_type=F32)
            turned = jnp.transpose(SCALE * dquery)
            query_grads[i][:, h * HD : (h + 1) * HD] = turned.astype(BF16)
        for (i, o, h), (dscores, probs_low) in zip(units, low_parts):
            if o <= REACH:
                window[near.index(o), 0, h] = dscores[0:TOK]
                window[near.index(o), 1, h] = probs_low[0:TOK]
            coarse[i, 0, h] = dscores[-TOK:]
            coarse[i, 1, h] = probs_low[-TOK:]
        for i in group:
            o = order[i]
            writes.append(pltpu.make_async_copy(coarse.at[i], coarse_out.at[i], out_sems.at[0, o]))
            writes[-1].start()
            if o <= REACH:
                at = near.index(o)
                writes.append(
                    pltpu.make_async_copy(window.at[at], window_out.at[at], out_sems.at[1, o])
                )
                writes[-1].start()
    for copy in writes:
        copy.wait()


def key_grad_kernel(*refs):
    order = ORDER
    near = [o for o in order if o <= REACH]
    chunks, coarse_in, window_in, refs = refs[:NZ], refs[NZ : NZ + 2], refs[NZ + 2 : NZ + 4], refs[NZ + 4 :]
    previous_grad, own_grad, sum_grad, packed, coarse, window, sems = refs
    copies = []
    for i, o in enumerate(order):
        part, group = (0, LEADING) if o in LEADING else (1, TRAILING)
        mine = [pltpu.make_async_copy(chunks[i], packed.at[i], sems.at[0, i])]
        source = coarse_in[part].at[group.index(o)]
        mine.append(pltpu.make_async_copy(source, coarse.at[i], sems.at[1, i]))
        if o in near:
            source = window_in[part].at[[n for n in group if n <= REACH].index(o)]
            target = window.at[near.index(o)]
            mine.append(pltpu.make_async_copy(source, target, sems.at[2, i]))
        for copy in mine:
            copy.start()
        copies.append(mine)
    _, z = place()
    units = [(h, kind) for h in range(HEADS_HERE) for kind in range(2)]
    zero = jnp.zeros((TOK, HD), F32)
    totals, mine, others = [None] * len(units), [zero] * len(units), [zero] * len(units)
    half = NZ // 2
    for first in range(0, NZ, half):
        group = range(first, first + half)
        for i in group:
            for copy in copies[i]:
                copy.wait()
        for unit, (h, kind) in enumerate(units):
            cols = slice(h * HD, (h + 1) * HD)
            tokens = [packed[i, kind * TOK : (kind + 1) * TOK, cols] for i in group]
            part = jnp.dot(
                jnp.concatenate([coarse[i, kind, h] for i in group], axis=1),
                jnp.concatenate(tokens, axis=0),
                preferred_element_type=F32,
            )
            totals[unit] = part if first == 0 else totals[unit] + part
            for i in group:
                if order[i] in near:
                    part = jnp.dot(
                        window[near.index(order[i]), kind, h],
                        tokens[i - first],
                        preferred_element_type=F32,
                    )
                    wraps = (z + order[i] >= NZ).astype(F32)
                    mine[unit] = mine[unit] + part * (1.0 - wraps)
                    if order[i] > 0:
                        others[unit] = others[unit] + part * wraps
    for unit, (h, kind) in enumerate(units):
        scale = SCALE if kind == 0 else 1.0
        at = (2 * h + kind) * HD
        here = (slice(kind * TOK, (kind + 1) * TOK), slice(h * HD, (h + 1) * HD))
        own_grad[here] = mine[unit] * scale
        previous_grad[here] = (others[unit] * scale).astype(BF16)
        sum_grad[:, at : at + HD] = (totals[unit] * scale).astype(BF16)


def finish_kernel(starts, slots, own_grad, arrived, parts, grad_keys, grad_values):
    base = starts[0]
    total = parts[0].astype(F32)
    for i in range(1, NXY):
        total = total + parts[i].astype(F32)
    high = total.astype(BF16).astype(F32)
    halves = jnp.concatenate([high, total - high], axis=0).astype(BF16)
    lane = lax.broadcasted_iota(jnp.int32, (2 * BARS_HERE, TOK), 1)
    row = lax.broadcasted_iota(jnp.int32, (2 * BARS_HERE, TOK), 0)
    slot = jnp.full((2 * BARS_HERE, TOK), -1, jnp.int32)
    for b in range(BARS_HERE):
        slot = jnp.where(jnp.bitwise_and(row, BARS_HERE - 1) == b, slots[b] - base, slot)
    placed = lax.dot_general(low(lane == slot), halves, TN, preferred_element_type=F32)
    for h in range(HEADS_HERE):
        cols = slice(h * HD, (h + 1) * HD)
        for kind, out in ((0, grad_keys), (1, grad_values)):
            rows = slice(kind * TOK, (kind + 1) * TOK)
            at = (2 * h + kind) * HD
            grad = own_grad[rows, cols] + arrived[rows, cols].astype(F32)
            out[:, cols] = (grad + placed[:, at : at + HD]).astype(BF16)


def add_low(*parts):
    total = parts[0].astype(F32)
    for part in parts[1:]:
        total = total + part.astype(F32)
    return total.astype(BF16)


def shards(queries, keys, values, grad_y, out_weight, bar_start, related, bar_summary_token):
    params = pltpu.CompilerParams(vmem_limit_bytes=VMEM_LIMIT)
    dma = pltpu.SemaphoreType.DMA
    grad_other = lax.ppermute(grad_y, "head", [(0, 1), (1, 0)])
    half = grad_y.shape[1]
    core = jnp.reshape(lax.axis_index("head"), (1,))
    partial, query_pack, own, sums = pl.pallas_call(
        pack_kernel,
        out_shape=(
            shape((FEAT, TOK), F32),
            shape((ROWS, FEAT)),
            shape((ROWS, FEAT)),
            shape((NXY, BARS_HERE, 2 * FEAT)),
        ),
        in_specs=[whole(SMEM)] * 4 + [whole(HBM)] * 5,
        out_specs=(whole(VMEM),) * 4,
        scratch_shapes=[VMEM((FEAT, half), BF16), VMEM(grad_y.shape, BF16), dma((6,))],
        compiler_params=params,
    )(
        core,
        *pinned(bar_start, related, bar_summary_token),
        *pinned(queries, keys, values, grad_y, out_weight),
    )
    packed = pl.pallas_call(
        grad_pack_kernel,
        out_shape=shape((ROWS, FEAT)),
        in_specs=[whole(SMEM)] + [whole(VMEM)] * 3 + [whole(HBM)],
        out_specs=whole(VMEM),
        scratch_shapes=[VMEM((FEAT, half), BF16), dma],
        compiler_params=params,
    )(
        core,
        *[pltpu.with_memory_space_constraint(x, VMEM) for x in (query_pack, partial)],
        grad_other,
        *pinned(out_weight),
    )

    after, before = [packed], [packed]

    def ring_step():
        after.append(lax.ppermute(after[-1], "seq", TO_PREVIOUS))
        before.append(lax.ppermute(before[-1], "seq", TO_NEXT))

    ring_step()
    all_sums = lax.all_to_all(sums, "seq", 0, 0, axis_index_groups=XY_GROUPS)
    after[1], before[1], all_sums = lax.optimization_barrier((after[1], before[1], all_sums))
    all_sums = all_sums.reshape(NXY * BARS_HERE, 2 * FEAT)
    ring_step()
    previous = lax.ppermute(own, "seq", ROW_UP)
    after[2], before[2], previous = lax.optimization_barrier((after[2], before[2], previous))
    ring_step()
    after.append(lax.ppermute(after[-1], "seq", TO_PREVIOUS))
    chunks = after + before[:0:-1]

    bars = NXY * BARS_HERE
    bias_shape = (REACH + 1 + NZ, TOK, TOK)
    stats_shape = (NZ, NZ, 2 * HEADS_HERE, TOK)
    held = [
        VMEM((NZ, ROWS, FEAT), BF16),
        VMEM((2, ROWS, FEAT), BF16),
        VMEM((bars, 2 * FEAT), BF16),
        VMEM(bias_shape, F32),
    ]
    def stats_of(order, *earlier):
        out = (shape(stats_shape, F32),) if earlier else (shape(stats_shape[1:], F32),)
        blocks = (len(bias_blocks(order)),) + bias_shape[1:]
        return pl.pallas_call(
            lambda *refs: stats_kernel(order, *refs),
            out_shape=out + (shape(blocks, F32),),
            in_specs=[whole(HBM)] * (len(order) + 3) + [whole(VMEM)] * len(earlier),
            out_specs=(whole(VMEM), whole(HBM)),
            scratch_shapes=held + [dma((3,)), dma((NZ,)), dma(bias_shape[:1])],
            compiler_params=params,
        )(*[chunks[o] for o in order], own, previous, all_sums, *earlier)

    partial_stats, bias_most = stats_of(EARLY)
    stats, bias_last = stats_of(LATE, partial_stats)

    stats = lax.all_to_all(stats, "seq", 0, 0, axis_index_groups=Z_GROUPS)

    def query_grads(order, stats):
        merging = order is LEADING
        near = sum(o <= REACH for o in order)
        coarse_shape = (len(order), 2, HEADS_HERE, bars, TOK)
        window_shape = (near, 2, HEADS_HERE, TOK, TOK)
        made = pl.pallas_call(
            lambda *refs: query_grad_kernel(order, *refs),
            out_shape=(shape((TOK, FEAT)),) * len(order)
            + (shape(coarse_shape), shape(window_shape))
            + (shape(stats_shape[1:], F32),) * merging,
            in_specs=[whole(HBM)] * (len(order) + 6),
            out_specs=(whole(VMEM),) * len(order) + (whole(HBM),) * 2 + (whole(VMEM),) * merging,
            scratch_shapes=held
            + [
                VMEM(stats.shape, F32),
                VMEM(stats_shape[1:], F32),
                VMEM(coarse_shape, BF16),
                VMEM(window_shape, BF16),
                dma((3,)),
                dma((NZ,)),
                dma(bias_shape[:1]),
                dma,
                dma((2, NZ)),
            ],
            compiler_params=params,
        )(*[chunks[o] for o in order], own, previous, all_sums, bias_most, bias_last, stats)
        *grads, coarse, window, merged = made if merging else (*made, None)
        return dict(zip(order, grads)), coarse, window, merged

    def forward_step(array):
        return lax.ppermute(array, "seq", TO_NEXT)

    def backward_step(array):
        return lax.ppermute(array, "seq", TO_PREVIOUS)

    grads, coarse_a, window_a, merged = query_grads(LEADING, stats)
    forward, backward = forward_step(grads[4]), backward_step(grads[5])
    more, coarse_b, window_b, _ = query_grads(TRAILING, merged)
    grads.update(more)
    forward, backward, coarse_b = lax.optimization_barrier((forward, backward, coarse_b))
    forward, backward = forward_step(add_low(forward, grads[3])), backward_step(add_low(backward, grads[6]))
    previous_grad, own_grad, sum_grad = pl.pallas_call(
        key_grad_kernel,
        out_shape=(
            shape((2 * TOK, FEAT)),
            shape((2 * TOK, FEAT), F32),
            shape((bars, 2 * FEAT)),
        ),
        in_specs=[whole(HBM)] * (NZ + 4),
        out_specs=(whole(VMEM),) * 3,
        scratch_shapes=[
            VMEM((NZ, ROWS, FEAT), BF16),
            VMEM((NZ, 2, HEADS_HERE, bars, TOK), BF16),
            VMEM((REACH + 1, 2, HEADS_HERE, TOK, TOK), BF16),
            dma((3, NZ)),
        ],
        compiler_params=params,
    )(*[chunks[o] for o in ORDER], coarse_a, coarse_b, window_a, window_b)
    forward, backward, sum_grad = lax.optimization_barrier((forward, backward, sum_grad))
    forward = forward_step(forward.astype(F32) + grads[2].astype(F32))
    backward = backward_step(backward.astype(F32) + grads[7].astype(F32))
    arrived = lax.ppermute(previous_grad, "seq", ROW_DOWN)
    parts = lax.all_to_all(
        sum_grad.reshape(NXY, BARS_HERE, 2 * FEAT), "seq", 0, 0, axis_index_groups=XY_GROUPS
    )
    forward = forward_step(add_low(forward, grads[1]))

    grad_keys, grad_values = pl.pallas_call(
        finish_kernel,
        out_shape=(shape((TOK, FEAT)),) * 2,
        in_specs=[whole(SMEM)] * 2 + [whole(VMEM)] * 3,
        out_specs=(whole(VMEM),) * 2,
    )(*pinned(bar_start, bar_summary_token), own_grad, arrived, parts)
    grad_queries = add_low(grads[0], forward, backward)
    return grad_queries, grad_keys, grad_values


def solution(mesh):
    in_specs = (
        P("seq", "head"),
        P("seq", "head"),
        P("seq", "head"),
        P("seq", "head"),
        P("head", None),
        P("seq"),
        P("seq", None),
        P("seq"),
    )
    out_specs = (P("seq", "head"), P("seq", "head"), P("seq", "head"))
    return jax.shard_map(shards, mesh=mesh, in_specs=in_specs, out_specs=out_specs, check_vma=False)
```

```python
import math

import jax
import jax.numpy as jnp
from jax import lax
from jax.experimental import pallas as pl
from jax.experimental.pallas import tpu as pltpu
from jax.sharding import PartitionSpec as P

HD = 128
REACH = 4
TOK = 128
BARS_HERE = 8
HEADS_HERE = 4
FEAT = HD * HEADS_HERE
META = 16
ROWS = 2 * TOK + META
NZ = 8
NY = 4
NX = 4
NXY = NY * NX
N_SEQ = NZ * NXY
OFFSETS = (1, 2, 4, 8, 12, 16, 24, 32)
SCALE = HD ** (-0.5)
LOG2E = math.log2(math.e)
EXP_SCALE = SCALE * LOG2E
LOWEST = -1e30

Z_GROUPS = [[j * NZ + z for z in range(NZ)] for j in range(NXY)]
XY_GROUPS = [[j * NZ + z for j in range(NXY)] for z in range(NZ)]


def route(dy, dx, dz):
    return [
        ((y * NX + x) * NZ + z, ((y + dy) % NY * NX + (x + dx) % NX) * NZ + (z + dz) % NZ)
        for y in range(NY)
        for x in range(NX)
        for z in range(NZ)
    ]


TO_NEXT = route(0, 0, 1)
TO_PREVIOUS = route(0, 0, -1)
ROW_UP = [(i, i + NZ) for i in range(N_SEQ - NZ) if i % NZ >= NZ - REACH]
ROW_DOWN = [(dst, src) for src, dst in ROW_UP]
EARLY = (0, 1, 7, 2, 6, 3, 5)
LATE = (4,)
LEADING = (4, 5)
TRAILING = (3, 6, 2, 7, 1, 0)
ORDER = LEADING + TRAILING
TOGETHER = 2

VMEM_LIMIT = 50 * 2**20
SMEM = pltpu.SMEM
VMEM = pltpu.VMEM
HBM = pltpu.HBM
NT = (((1,), (1,)), ((), ()))
TN = (((0,), (0,)), ((), ()))
BF16 = jnp.bfloat16
F32 = jnp.float32


def whole(space):
    return pl.BlockSpec(memory_space=space)


def shape(dims, dtype=BF16):
    return jax.ShapeDtypeStruct(dims, dtype)


def pinned(*arrays):
    return [pltpu.with_memory_space_constraint(array, HBM) for array in arrays]


def local_bar(starts, positions):
    count = jnp.zeros_like(positions)
    for b in range(1, BARS_HERE):
        count = count + (positions >= starts[b]).astype(jnp.int32)
    return count


def low(flags):
    return flags.astype(F32).astype(BF16)


def pack_kernel(
    core, starts, related, slots, queries, keys, values, grad_own, out_weight,
    partial, query_pack, key_pack, sums, weight, grad, sems,
):
    half = grad_own.shape[1]
    copies = [pltpu.make_async_copy(grad_own, grad, sems.at[0])]
    cols = pl.ds(pl.multiple_of(core[0] * half, half), half)
    copies.append(pltpu.make_async_copy(out_weight.at[:, cols], weight, sems.at[1]))
    copies.append(pltpu.make_async_copy(queries, query_pack.at[pl.ds(0, TOK)], sems.at[3]))
    copies.append(pltpu.make_async_copy(keys, key_pack.at[pl.ds(0, TOK)], sems.at[4]))
    copies.append(pltpu.make_async_copy(values, key_pack.at[pl.ds(TOK, TOK)], sems.at[5]))
    for copy in copies:
        copy.start()
    base = starts[0]
    lane = lax.broadcasted_iota(jnp.int32, (META, TOK), 1)
    row = lax.broadcasted_iota(jnp.int32, (META, TOK), 0)
    bar = local_bar(starts, lane + base)
    info = jnp.where(row == 0, bar, 0)
    for j in range(len(OFFSETS)):
        entry = jnp.zeros((META, TOK), jnp.int32)
        for b in range(BARS_HERE):
            has = (related[b, j] >= 0).astype(jnp.int32)
            entry = jnp.where(bar == b, has, entry)
        info = jnp.where(row == j + 1, entry, info)
    query_pack[TOK:, :] = jnp.zeros((TOK + META, FEAT), BF16)
    query_pack[2 * TOK :, 0:TOK] = low(info)
    key_pack[2 * TOK :, :] = jnp.zeros((META, FEAT), BF16)
    key_pack[2 * TOK :, 0:TOK] = low(bar)
    slot = jnp.full((META, TOK), -1, jnp.int32)
    for b in range(BARS_HERE):
        slot = jnp.where(row == b, slots[b] - base, slot)
    pick = low(lane == slot)
    for copy in copies[2:]:
        copy.wait()
    for kind in range(2):
        source = key_pack[kind * TOK : (kind + 1) * TOK, :]
        rows = jnp.dot(pick, source, preferred_element_type=F32)[0:BARS_HERE].astype(BF16)
        for h in range(HEADS_HERE):
            at = (2 * h + kind) * HD
            for j in range(NXY):
                sums[j, :, at : at + HD] = rows[:, h * HD : (h + 1) * HD]
    for copy in copies[:2]:
        copy.wait()
    partial[...] = lax.dot_general(weight[...], grad[...], NT, preferred_element_type=F32)


def grad_pack_kernel(core, pack, partial, grad_other, out_weight, packed, weight, sem):
    half = grad_other.shape[1]
    cols = pl.ds(pl.multiple_of((1 - core[0]) * half, half), half)
    copy = pltpu.make_async_copy(out_weight.at[:, cols], weight, sem)
    copy.start()
    packed[0:TOK, :] = pack[0:TOK, :]
    packed[2 * TOK :, :] = pack[2 * TOK :, :]
    copy.wait()
    turned = partial[...] + lax.dot_general(
        weight[...], grad_other[...], NT, preferred_element_type=F32
    )
    for h in range(HEADS_HERE):
        cols = slice(h * HD, (h + 1) * HD)
        packed[TOK : 2 * TOK, cols] = jnp.transpose(turned[cols]).astype(BF16)


def place():
    rank = lax.axis_index("seq")
    return rank, jnp.bitwise_and(rank, NZ - 1)


def load_keys(own, previous, sums, pairs, keys, sems):
    copies = [
        pltpu.make_async_copy(own, pairs.at[0], sems.at[0]),
        pltpu.make_async_copy(previous, pairs.at[1], sems.at[1]),
        pltpu.make_async_copy(sums, keys, sems.at[2]),
    ]
    for copy in copies:
        copy.start()
    return copies


class Bias:
    def __init__(self, packed, pairs):
        rank, self.z = place()
        self.row_start = rank - self.z
        self.packed = packed
        self.local = [
            jnp.transpose(
                jnp.broadcast_to(pairs[i, 2 * TOK :, 0:TOK].astype(F32)[0:1], (TOK, TOK))
            ).astype(jnp.int32)
            for i in range(2)
        ]
        self.key_row = lax.broadcasted_iota(jnp.int32, (TOK, TOK), 0)
        self.token_col = lax.broadcasted_iota(jnp.int32, (TOK, TOK), 1)
        owner = lax.shift_right_logical(self.key_row, 3) * NZ + self.z
        self.summary_bar = owner * BARS_HERE + jnp.bitwise_and(self.key_row, BARS_HERE - 1)

    def build(self, o, bias):
        owner = self.row_start + jnp.bitwise_and(self.z + o, NZ - 1)
        info = self.packed[o, 2 * TOK :, 0:TOK].astype(F32).astype(jnp.int32)
        token_bar = info[0:1] + owner * BARS_HERE
        rel = [
            jnp.where(info[j + 1 : j + 2] > 0, token_bar - OFFSETS[j], -1)
            for j in range(len(OFFSETS))
        ]
        if o <= REACH:
            key_owner = owner - o
            key_local = jnp.where(self.z + o >= NZ, self.local[1], self.local[0])
            key_bar = jnp.where(key_owner >= 0, key_local + key_owner * BARS_HERE, -2)
            seen = key_bar == rel[0]
            for entry in rel[1:]:
                seen = seen | (key_bar == entry)
            if o == 0:
                seen = seen | ((key_bar == token_bar) & (self.key_row <= self.token_col))
            bias[o] = jnp.where(seen, 0.0, -jnp.inf)
        hidden = self.summary_bar >= token_bar
        for entry in rel:
            hidden = hidden | (self.summary_bar == entry)
        bias[REACH + 1 + o] = jnp.where(hidden, -jnp.inf, 0.0)


def bias_blocks(order):
    return [o for o in order if o <= REACH] + [REACH + 1 + o for o in order]


def products(packed, pairs, keys, bias, h, o):
    _, z = place()
    cols = slice(h * HD, (h + 1) * HD)
    at = 2 * h * HD
    query = packed[o, 0:TOK, cols]
    grad = packed[o, TOK : 2 * TOK, cols]
    key, value = keys[:, at : at + HD], keys[:, at + HD : at + 2 * HD]
    mask = bias[REACH + 1 + o]
    if o <= REACH:
        side = lax.shift_right_logical(z + o, 3)
        key = jnp.concatenate([pairs[side, 0:TOK, cols], key], axis=0)
        value = jnp.concatenate([pairs[side, TOK : 2 * TOK, cols], value], axis=0)
        mask = jnp.concatenate([bias[o], mask], axis=0)
    scores = lax.dot_general(key, query, NT, preferred_element_type=F32)
    dprobs = lax.dot_general(value, grad, NT, preferred_element_type=F32)
    return key, scores, dprobs, mask


def stats_kernel(order, *refs):
    chunks, (own, previous, sums), refs = refs[: len(order)], refs[len(order) : len(order) + 3], refs[len(order) + 3 :]
    earlier, refs = (refs[0], refs[1:]) if len(order) < REACH else (None, refs)
    stats, bias_out, packed, pairs, keys, bias, key_sems, chunk_sems, bias_sems = refs
    key_copies = load_keys(own, previous, sums, pairs, keys, key_sems)
    copies = [
        pltpu.make_async_copy(chunk, packed.at[o], chunk_sems.at[o])
        for o, chunk in zip(order, chunks)
    ]
    for copy in copies:
        copy.start()
    for copy in key_copies:
        copy.wait()
    masks = Bias(packed, pairs)
    writes = []
    for i, o in enumerate(order):
        copies[i].wait()
        masks.build(o, bias)
        for block in bias_blocks((o,)):
            place_out = bias_out.at[bias_blocks(order).index(block)]
            writes.append(pltpu.make_async_copy(bias.at[block], place_out, bias_sems.at[block]))
            writes[-1].start()
        chunk = jnp.bitwise_and(masks.z + o, NZ - 1)
        log_sums, means = [], []
        made = [products(packed, pairs, keys, bias, h, o) for h in range(HEADS_HERE)]
        for _, scores, dprobs, mask in made:
            scores = scores + mask
            top = jnp.maximum(jnp.max(scores, axis=0, keepdims=True), LOWEST)
            weights = jnp.exp2((scores - top) * EXP_SCALE)
            total = jnp.sum(weights, axis=0, keepdims=True)
            weighted = jnp.sum(weights * dprobs, axis=0, keepdims=True)
            log_sums.append(top * EXP_SCALE + jnp.log(total) * LOG2E)
            means.append(jnp.where(total > 0.0, weighted / total, 0.0))
        merged = jnp.concatenate(log_sums + means, axis=0)
        if earlier is None:
            stats[chunk] = merged
            continue
        for peer in range(NZ):
            stats[peer] = earlier[...]
            stats[peer, chunk] = merged
    for copy in writes:
        copy.wait()


def merge_stats(stats, merged):
    top = stats[0, :, 0:HEADS_HERE, :]
    for i in range(1, NZ):
        top = jnp.maximum(top, stats[i, :, 0:HEADS_HERE, :])
    total = jnp.zeros_like(top)
    mean = jnp.zeros_like(top)
    for i in range(NZ):
        weight = jnp.exp2(stats[i, :, 0:HEADS_HERE, :] - top)
        total = total + weight
        mean = mean + weight * stats[i, :, HEADS_HERE:, :]
    merged[:, 0:HEADS_HERE, :] = top + jnp.log(total) * LOG2E
    merged[:, HEADS_HERE:, :] = mean / total


def query_grad_kernel(order, *refs):
    count = len(order)
    merging = order is LEADING
    near = [o for o in order if o <= REACH]
    chunks, (own, previous, sums, bias_most, bias_last, stats_in), refs = refs[:count], refs[count : count + 6], refs[count + 6 :]
    query_grads, (coarse, window), refs = refs[:count], refs[count : count + 2], refs[count + 2 :]
    merged_out, refs = (refs[0], refs[1:]) if merging else (None, refs)
    packed, pairs, keys, bias, stats, merged, key_sems, chunk_sems, bias_sems, stats_sem = refs
    stats_copy = pltpu.make_async_copy(stats_in, stats, stats_sem)
    stats_copy.start()
    key_copies = load_keys(own, previous, sums, pairs, keys, key_sems)
    copies = []
    for i, o in enumerate(order):
        mine = [pltpu.make_async_copy(chunks[i], packed.at[o], chunk_sems.at[o])]
        for block in bias_blocks((o,)):
            source, among = (bias_most, EARLY) if o in EARLY else (bias_last, LATE)
            source = source.at[bias_blocks(among).index(block)]
            mine.append(pltpu.make_async_copy(source, bias.at[block], bias_sems.at[block]))
        for copy in mine:
            copy.start()
        copies.append(mine)
    stats_copy.wait()
    if merging:
        merge_stats(stats, merged)
        merged_out[...] = merged[...]
    else:
        merged = stats
    for copy in key_copies:
        copy.wait()
    _, z = place()
    keys_turned = [
        jnp.transpose(keys[:, 2 * h * HD : (2 * h + 1) * HD]) for h in range(HEADS_HERE)
    ]
    pairs_turned = [
        [jnp.transpose(pairs[i, 0:TOK, h * HD : (h + 1) * HD]) for i in range(2)]
        for h in range(HEADS_HERE)
    ]
    for first in range(0, count, TOGETHER):
        group = range(first, first + TOGETHER)
        for i in group:
            for copy in copies[i]:
                copy.wait()
        units = [(i, order[i], h) for i in group for h in range(HEADS_HERE)]
        made = [products(packed, pairs, keys, bias, h, o) for _, o, h in units]
        low_parts = []
        for (i, o, h), (_, scores, dprobs, mask) in zip(units, made):
            chunk = jnp.bitwise_and(z + o, NZ - 1)
            log_sum = merged[chunk, h : h + 1, :]
            delta = merged[chunk, HEADS_HERE + h : HEADS_HERE + h + 1, :]
            probs = jnp.exp2(scores * EXP_SCALE - log_sum + mask)
            low_parts.append(((probs * (dprobs - delta)).astype(BF16), probs.astype(BF16)))
        for (i, o, h), (dscores, probs_low) in zip(units, low_parts):
            turned = keys_turned[h]
            if o <= REACH:
                side = pairs_turned[h][0]
                if o > 0:
                    side = jnp.where(z + o >= NZ, pairs_turned[h][1], side)
                turned = jnp.concatenate([side, turned], axis=1)
            dquery = jnp.dot(turned, dscores, preferred_element_type=F32)
            turned = jnp.transpose(SCALE * dquery)
            query_grads[i][:, h * HD : (h + 1) * HD] = turned.astype(BF16)
        for (i, o, h), (dscores, probs_low) in zip(units, low_parts):
            if o <= REACH:
                window[near.index(o), 0, h] = dscores[0:TOK]
                window[near.index(o), 1, h] = probs_low[0:TOK]
            coarse[i, 0, h] = dscores[-TOK:]
            coarse[i, 1, h] = probs_low[-TOK:]


def key_grad_kernel(*refs):
    order = ORDER
    near = [o for o in order if o <= REACH]
    chunks, coarse_in, window_in, refs = refs[:NZ], refs[NZ : NZ + 2], refs[NZ + 2 : NZ + 4], refs[NZ + 4 :]
    previous_grad, own_grad, sum_grad, packed, sems = refs
    copies, coarse, window = [], [], {}
    for i, o in enumerate(order):
        part, group = (0, LEADING) if o in LEADING else (1, TRAILING)
        coarse.append(coarse_in[part].at[group.index(o)])
        if o in near:
            window[o] = window_in[part].at[[n for n in group if n <= REACH].index(o)]
        copies.append(pltpu.make_async_copy(chunks[i], packed.at[i], sems.at[i]))
        copies[-1].start()
    _, z = place()
    units = [(h, kind) for h in range(HEADS_HERE) for kind in range(2)]
    zero = jnp.zeros((TOK, HD), F32)
    totals, mine, others = [None] * len(units), [zero] * len(units), [zero] * len(units)
    half = NZ // 2
    for first in range(0, NZ, half):
        group = range(first, first + half)
        for i in group:
            copies[i].wait()
        for unit, (h, kind) in enumerate(units):
            cols = slice(h * HD, (h + 1) * HD)
            tokens = [packed[i, kind * TOK : (kind + 1) * TOK, cols] for i in group]
            part = jnp.dot(
                jnp.concatenate([coarse[i][kind, h] for i in group], axis=1),
                jnp.concatenate(tokens, axis=0),
                preferred_element_type=F32,
            )
            totals[unit] = part if first == 0 else totals[unit] + part
            for i in group:
                if order[i] in near:
                    part = jnp.dot(
                        window[order[i]][kind, h],
                        tokens[i - first],
                        preferred_element_type=F32,
                    )
                    wraps = (z + order[i] >= NZ).astype(F32)
                    mine[unit] = mine[unit] + part * (1.0 - wraps)
                    if order[i] > 0:
                        others[unit] = others[unit] + part * wraps
    for unit, (h, kind) in enumerate(units):
        scale = SCALE if kind == 0 else 1.0
        at = (2 * h + kind) * HD
        here = (slice(kind * TOK, (kind + 1) * TOK), slice(h * HD, (h + 1) * HD))
        own_grad[here] = mine[unit] * scale
        previous_grad[here] = (others[unit] * scale).astype(BF16)
        sum_grad[:, at : at + HD] = (totals[unit] * scale).astype(BF16)


def finish_kernel(starts, slots, own_grad, arrived, parts, grad_keys, grad_values):
    base = starts[0]
    total = parts[0].astype(F32)
    for i in range(1, NXY):
        total = total + parts[i].astype(F32)
    high = total.astype(BF16).astype(F32)
    halves = jnp.concatenate([high, total - high], axis=0).astype(BF16)
    lane = lax.broadcasted_iota(jnp.int32, (2 * BARS_HERE, TOK), 1)
    row = lax.broadcasted_iota(jnp.int32, (2 * BARS_HERE, TOK), 0)
    slot = jnp.full((2 * BARS_HERE, TOK), -1, jnp.int32)
    for b in range(BARS_HERE):
        slot = jnp.where(jnp.bitwise_and(row, BARS_HERE - 1) == b, slots[b] - base, slot)
    placed = lax.dot_general(low(lane == slot), halves, TN, preferred_element_type=F32)
    for h in range(HEADS_HERE):
        cols = slice(h * HD, (h + 1) * HD)
        for kind, out in ((0, grad_keys), (1, grad_values)):
            rows = slice(kind * TOK, (kind + 1) * TOK)
            at = (2 * h + kind) * HD
            grad = own_grad[rows, cols] + arrived[rows, cols].astype(F32)
            out[:, cols] = (grad + placed[:, at : at + HD]).astype(BF16)


def add_low(*parts):
    total = parts[0].astype(F32)
    for part in parts[1:]:
        total = total + part.astype(F32)
    return total.astype(BF16)


def shards(queries, keys, values, grad_y, out_weight, bar_start, related, bar_summary_token):
    params = pltpu.CompilerParams(vmem_limit_bytes=VMEM_LIMIT)
    dma = pltpu.SemaphoreType.DMA
    grad_other = lax.ppermute(grad_y, "head", [(0, 1), (1, 0)])
    half = grad_y.shape[1]
    core = jnp.reshape(lax.axis_index("head"), (1,))
    partial, query_pack, own, sums = pl.pallas_call(
        pack_kernel,
        out_shape=(
            shape((FEAT, TOK), F32),
            shape((ROWS, FEAT)),
            shape((ROWS, FEAT)),
            shape((NXY, BARS_HERE, 2 * FEAT)),
        ),
        in_specs=[whole(SMEM)] * 4 + [whole(HBM)] * 5,
        out_specs=(whole(VMEM),) * 4,
        scratch_shapes=[VMEM((FEAT, half), BF16), VMEM(grad_y.shape, BF16), dma((6,))],
        compiler_params=params,
    )(
        core,
        *pinned(bar_start, related, bar_summary_token),
        *pinned(queries, keys, values, grad_y, out_weight),
    )
    packed = pl.pallas_call(
        grad_pack_kernel,
        out_shape=shape((ROWS, FEAT)),
        in_specs=[whole(SMEM)] + [whole(VMEM)] * 3 + [whole(HBM)],
        out_specs=whole(VMEM),
        scratch_shapes=[VMEM((FEAT, half), BF16), dma],
        compiler_params=params,
    )(
        core,
        *[pltpu.with_memory_space_constraint(x, VMEM) for x in (query_pack, partial)],
        grad_other,
        *pinned(out_weight),
    )

    after, before = [packed], [packed]

    def ring_step():
        after.append(lax.ppermute(after[-1], "seq", TO_PREVIOUS))
        before.append(lax.ppermute(before[-1], "seq", TO_NEXT))

    ring_step()
    all_sums = lax.all_to_all(sums, "seq", 0, 0, axis_index_groups=XY_GROUPS)
    after[1], before[1], all_sums = lax.optimization_barrier((after[1], before[1], all_sums))
    all_sums = all_sums.reshape(NXY * BARS_HERE, 2 * FEAT)
    ring_step()
    previous = lax.ppermute(own, "seq", ROW_UP)
    after[2], before[2], previous = lax.optimization_barrier((after[2], before[2], previous))
    ring_step()
    after.append(lax.ppermute(after[-1], "seq", TO_PREVIOUS))
    chunks = after + before[:0:-1]

    bars = NXY * BARS_HERE
    bias_shape = (REACH + 1 + NZ, TOK, TOK)
    stats_shape = (NZ, NZ, 2 * HEADS_HERE, TOK)
    held = [
        VMEM((NZ, ROWS, FEAT), BF16),
        VMEM((2, ROWS, FEAT), BF16),
        VMEM((bars, 2 * FEAT), BF16),
        VMEM(bias_shape, F32),
    ]
    def stats_of(order, *earlier):
        out = (shape(stats_shape, F32),) if earlier else (shape(stats_shape[1:], F32),)
        blocks = (len(bias_blocks(order)),) + bias_shape[1:]
        return pl.pallas_call(
            lambda *refs: stats_kernel(order, *refs),
            out_shape=out + (shape(blocks, F32),),
            in_specs=[whole(HBM)] * (len(order) + 3) + [whole(VMEM)] * len(earlier),
            out_specs=(whole(VMEM), whole(HBM)),
            scratch_shapes=held + [dma((3,)), dma((NZ,)), dma(bias_shape[:1])],
            compiler_params=params,
        )(*[chunks[o] for o in order], own, previous, all_sums, *earlier)

    partial_stats, bias_most = stats_of(EARLY)
    stats, bias_last = stats_of(LATE, partial_stats)

    stats = lax.all_to_all(stats, "seq", 0, 0, axis_index_groups=Z_GROUPS)

    def query_grads(order, stats):
        merging = order is LEADING
        near = sum(o <= REACH for o in order)
        coarse_shape = (len(order), 2, HEADS_HERE, bars, TOK)
        window_shape = (near, 2, HEADS_HERE, TOK, TOK)
        made = pl.pallas_call(
            lambda *refs: query_grad_kernel(order, *refs),
            out_shape=(shape((TOK, FEAT)),) * len(order)
            + (VMEM(coarse_shape, BF16), VMEM(window_shape, BF16))
            + (shape(stats_shape[1:], F32),) * merging,
            in_specs=[whole(HBM)] * (len(order) + 6),
            out_specs=(whole(VMEM),) * (len(order) + 2 + merging),
            scratch_shapes=held
            + [
                VMEM(stats.shape, F32),
                VMEM(stats_shape[1:], F32),
                dma((3,)),
                dma((NZ,)),
                dma(bias_shape[:1]),
                dma,
            ],
            compiler_params=params,
        )(*[chunks[o] for o in order], own, previous, all_sums, bias_most, bias_last, stats)
        *grads, coarse, window, merged = made if merging else (*made, None)
        return dict(zip(order, grads)), coarse, window, merged

    def forward_step(array):
        return lax.ppermute(array, "seq", TO_NEXT)

    def backward_step(array):
        return lax.ppermute(array, "seq", TO_PREVIOUS)

    grads, coarse_a, window_a, merged = query_grads(LEADING, stats)
    forward, backward = forward_step(grads[4]), backward_step(grads[5])
    more, coarse_b, window_b, _ = query_grads(TRAILING, merged)
    grads.update(more)
    forward, backward, coarse_b = lax.optimization_barrier((forward, backward, coarse_b))
    forward, backward = forward_step(add_low(forward, grads[3])), backward_step(add_low(backward, grads[6]))
    previous_grad, own_grad, sum_grad = pl.pallas_call(
        key_grad_kernel,
        out_shape=(
            shape((2 * TOK, FEAT)),
            shape((2 * TOK, FEAT), F32),
            shape((bars, 2 * FEAT)),
        ),
        in_specs=[whole(HBM)] * NZ + [whole(VMEM)] * 4,
        out_specs=(whole(VMEM),) * 3,
        scratch_shapes=[VMEM((NZ, ROWS, FEAT), BF16), dma((NZ,))],
        compiler_params=params,
    )(
        *[chunks[o] for o in ORDER],
        *[
            pltpu.with_memory_space_constraint(x, VMEM)
            for x in (coarse_a, coarse_b, window_a, window_b)
        ],
    )
    forward, backward, sum_grad = lax.optimization_barrier((forward, backward, sum_grad))
    forward = forward_step(forward.astype(F32) + grads[2].astype(F32))
    backward = backward_step(backward.astype(F32) + grads[7].astype(F32))
    arrived = lax.ppermute(previous_grad, "seq", ROW_DOWN)
    parts = lax.all_to_all(
        sum_grad.reshape(NXY, BARS_HERE, 2 * FEAT), "seq", 0, 0, axis_index_groups=XY_GROUPS
    )
    forward = forward_step(add_low(forward, grads[1]))

    grad_keys, grad_values = pl.pallas_call(
        finish_kernel,
        out_shape=(shape((TOK, FEAT)),) * 2,
        in_specs=[whole(SMEM)] * 2 + [whole(VMEM)] * 3,
        out_specs=(whole(VMEM),) * 2,
    )(*pinned(bar_start, bar_summary_token), own_grad, arrived, parts)
    grad_queries = add_low(grads[0], forward, backward)
    return grad_queries, grad_keys, grad_values


def solution(mesh):
    in_specs = (
        P("seq", "head"),
        P("seq", "head"),
        P("seq", "head"),
        P("seq", "head"),
        P("head", None),
        P("seq"),
        P("seq", None),
        P("seq"),
    )
    out_specs = (P("seq", "head"), P("seq", "head"), P("seq", "head"))
    return jax.shard_map(shards, mesh=mesh, in_specs=in_specs, out_specs=out_specs, check_vma=False)
```

```python
import math

import jax
import jax.numpy as jnp
from jax import lax
from jax.experimental import pallas as pl
from jax.experimental.pallas import tpu as pltpu
from jax.sharding import PartitionSpec as P

HD = 128
REACH = 4
TOK = 128
BARS_HERE = 8
HEADS_HERE = 4
FEAT = HD * HEADS_HERE
META = 16
ROWS = 2 * TOK + META
NZ = 8
NY = 4
NX = 4
NXY = NY * NX
N_SEQ = NZ * NXY
OFFSETS = (1, 2, 4, 8, 12, 16, 24, 32)
SCALE = HD ** (-0.5)
LOG2E = math.log2(math.e)
EXP_SCALE = SCALE * LOG2E
LOWEST = -1e30

Z_GROUPS = [[j * NZ + z for z in range(NZ)] for j in range(NXY)]
XY_GROUPS = [[j * NZ + z for j in range(NXY)] for z in range(NZ)]


def route(dy, dx, dz):
    return [
        ((y * NX + x) * NZ + z, ((y + dy) % NY * NX + (x + dx) % NX) * NZ + (z + dz) % NZ)
        for y in range(NY)
        for x in range(NX)
        for z in range(NZ)
    ]


TO_NEXT = route(0, 0, 1)
TO_PREVIOUS = route(0, 0, -1)
ROW_UP = [(i, i + NZ) for i in range(N_SEQ - NZ) if i % NZ >= NZ - REACH]
ROW_DOWN = [(dst, src) for src, dst in ROW_UP]
EARLY = (0, 1, 7, 2, 6, 3, 5)
LATE = (4,)
LEADING = (4, 5)
TRAILING = (3, 6, 2, 7, 1, 0)
ORDER = LEADING + TRAILING
TOGETHER = 2

VMEM_LIMIT = 50 * 2**20
SMEM = pltpu.SMEM
VMEM = pltpu.VMEM
HBM = pltpu.HBM
NT = (((1,), (1,)), ((), ()))
TN = (((0,), (0,)), ((), ()))
BF16 = jnp.bfloat16
F32 = jnp.float32


def whole(space):
    return pl.BlockSpec(memory_space=space)


def shape(dims, dtype=BF16):
    return jax.ShapeDtypeStruct(dims, dtype)


def pinned(*arrays):
    return [pltpu.with_memory_space_constraint(array, HBM) for array in arrays]


def local_bar(starts, positions):
    count = jnp.zeros_like(positions)
    for b in range(1, BARS_HERE):
        count = count + (positions >= starts[b]).astype(jnp.int32)
    return count


def low(flags):
    return flags.astype(F32).astype(BF16)


def pack_kernel(
    core, starts, related, slots, queries, keys, values, grad_own, out_weight,
    partial, query_pack, key_pack, sums, weight, grad, sems,
):
    half = grad_own.shape[1]
    copies = [pltpu.make_async_copy(grad_own, grad, sems.at[0])]
    cols = pl.ds(pl.multiple_of(core[0] * half, half), half)
    copies.append(pltpu.make_async_copy(out_weight.at[:, cols], weight, sems.at[1]))
    copies.append(pltpu.make_async_copy(queries, query_pack.at[pl.ds(0, TOK)], sems.at[3]))
    copies.append(pltpu.make_async_copy(keys, key_pack.at[pl.ds(0, TOK)], sems.at[4]))
    copies.append(pltpu.make_async_copy(values, key_pack.at[pl.ds(TOK, TOK)], sems.at[5]))
    for copy in copies:
        copy.start()
    base = starts[0]
    lane = lax.broadcasted_iota(jnp.int32, (META, TOK), 1)
    row = lax.broadcasted_iota(jnp.int32, (META, TOK), 0)
    bar = local_bar(starts, lane + base)
    info = jnp.where(row == 0, bar, 0)
    for j in range(len(OFFSETS)):
        entry = jnp.zeros((META, TOK), jnp.int32)
        for b in range(BARS_HERE):
            has = (related[b, j] >= 0).astype(jnp.int32)
            entry = jnp.where(bar == b, has, entry)
        info = jnp.where(row == j + 1, entry, info)
    query_pack[TOK:, :] = jnp.zeros((TOK + META, FEAT), BF16)
    query_pack[2 * TOK :, 0:TOK] = low(info)
    key_pack[2 * TOK :, :] = jnp.zeros((META, FEAT), BF16)
    key_pack[2 * TOK :, 0:TOK] = low(bar)
    slot = jnp.full((META, TOK), -1, jnp.int32)
    for b in range(BARS_HERE):
        slot = jnp.where(row == b, slots[b] - base, slot)
    pick = low(lane == slot)
    for copy in copies[2:]:
        copy.wait()
    for kind in range(2):
        source = key_pack[kind * TOK : (kind + 1) * TOK, :]
        rows = jnp.dot(pick, source, preferred_element_type=F32)[0:BARS_HERE].astype(BF16)
        for h in range(HEADS_HERE):
            at = (2 * h + kind) * HD
            for j in range(NXY):
                sums[j, :, at : at + HD] = rows[:, h * HD : (h + 1) * HD]
    for copy in copies[:2]:
        copy.wait()
    partial[...] = lax.dot_general(weight[...], grad[...], NT, preferred_element_type=F32)


def grad_pack_kernel(core, pack, partial, grad_other, out_weight, packed, weight, sem):
    half = grad_other.shape[1]
    cols = pl.ds(pl.multiple_of((1 - core[0]) * half, half), half)
    copy = pltpu.make_async_copy(out_weight.at[:, cols], weight, sem)
    copy.start()
    packed[0:TOK, :] = pack[0:TOK, :]
    packed[2 * TOK :, :] = pack[2 * TOK :, :]
    copy.wait()
    turned = partial[...] + lax.dot_general(
        weight[...], grad_other[...], NT, preferred_element_type=F32
    )
    for h in range(HEADS_HERE):
        cols = slice(h * HD, (h + 1) * HD)
        packed[TOK : 2 * TOK, cols] = jnp.transpose(turned[cols]).astype(BF16)


def place():
    rank = lax.axis_index("seq")
    return rank, jnp.bitwise_and(rank, NZ - 1)


def load_keys(own, previous, sums, pairs, keys, sems):
    copies = [
        pltpu.make_async_copy(own, pairs.at[0], sems.at[0]),
        pltpu.make_async_copy(previous, pairs.at[1], sems.at[1]),
        pltpu.make_async_copy(sums, keys, sems.at[2]),
    ]
    for copy in copies:
        copy.start()
    return copies


class Bias:
    def __init__(self, packed, pairs):
        rank, self.z = place()
        self.row_start = rank - self.z
        self.packed = packed
        self.local = [
            jnp.transpose(
                jnp.broadcast_to(pairs[i, 2 * TOK :, 0:TOK].astype(F32)[0:1], (TOK, TOK))
            ).astype(jnp.int32)
            for i in range(2)
        ]
        self.key_row = lax.broadcasted_iota(jnp.int32, (TOK, TOK), 0)
        self.token_col = lax.broadcasted_iota(jnp.int32, (TOK, TOK), 1)
        owner = lax.shift_right_logical(self.key_row, 3) * NZ + self.z
        self.summary_bar = owner * BARS_HERE + jnp.bitwise_and(self.key_row, BARS_HERE - 1)

    def build(self, o, bias):
        owner = self.row_start + jnp.bitwise_and(self.z + o, NZ - 1)
        info = self.packed[o, 2 * TOK :, 0:TOK].astype(F32).astype(jnp.int32)
        token_bar = info[0:1] + owner * BARS_HERE
        rel = [
            jnp.where(info[j + 1 : j + 2] > 0, token_bar - OFFSETS[j], -1)
            for j in range(len(OFFSETS))
        ]
        if o <= REACH:
            key_owner = owner - o
            key_local = jnp.where(self.z + o >= NZ, self.local[1], self.local[0])
            key_bar = jnp.where(key_owner >= 0, key_local + key_owner * BARS_HERE, -2)
            seen = key_bar == rel[0]
            for entry in rel[1:]:
                seen = seen | (key_bar == entry)
            if o == 0:
                seen = seen | ((key_bar == token_bar) & (self.key_row <= self.token_col))
            bias[o] = jnp.where(seen, 0.0, -jnp.inf)
        hidden = self.summary_bar >= token_bar
        for entry in rel:
            hidden = hidden | (self.summary_bar == entry)
        bias[REACH + 1 + o] = jnp.where(hidden, -jnp.inf, 0.0)


def bias_blocks(order):
    return [o for o in order if o <= REACH] + [REACH + 1 + o for o in order]


class BiasBlocks:
    def __init__(self, *groups):
        self.where = {
            block: (ref, i) for order, ref in groups for i, block in enumerate(bias_blocks(order))
        }

    def __getitem__(self, block):
        ref, i = self.where[block]
        return ref[i]

    def __setitem__(self, block, value):
        ref, i = self.where[block]
        ref[i] = value


def products(packed, pairs, keys, bias, h, o):
    _, z = place()
    cols = slice(h * HD, (h + 1) * HD)
    at = 2 * h * HD
    query = packed[o, 0:TOK, cols]
    grad = packed[o, TOK : 2 * TOK, cols]
    key, value = keys[:, at : at + HD], keys[:, at + HD : at + 2 * HD]
    mask = bias[REACH + 1 + o]
    if o <= REACH:
        side = lax.shift_right_logical(z + o, 3)
        key = jnp.concatenate([pairs[side, 0:TOK, cols], key], axis=0)
        value = jnp.concatenate([pairs[side, TOK : 2 * TOK, cols], value], axis=0)
        mask = jnp.concatenate([bias[o], mask], axis=0)
    scores = lax.dot_general(key, query, NT, preferred_element_type=F32)
    dprobs = lax.dot_general(value, grad, NT, preferred_element_type=F32)
    return key, scores, dprobs, mask


def stats_kernel(order, *refs):
    chunks, (own, previous, sums), refs = refs[: len(order)], refs[len(order) : len(order) + 3], refs[len(order) + 3 :]
    earlier, refs = (refs[0], refs[1:]) if len(order) < REACH else (None, refs)
    stats, bias_out, packed, pairs, keys, key_sems, chunk_sems = refs
    bias = BiasBlocks((order, bias_out))
    key_copies = load_keys(own, previous, sums, pairs, keys, key_sems)
    copies = [
        pltpu.make_async_copy(chunk, packed.at[o], chunk_sems.at[o])
        for o, chunk in zip(order, chunks)
    ]
    for copy in copies:
        copy.start()
    for copy in key_copies:
        copy.wait()
    masks = Bias(packed, pairs)
    for i, o in enumerate(order):
        copies[i].wait()
        masks.build(o, bias)
        chunk = jnp.bitwise_and(masks.z + o, NZ - 1)
        log_sums, means = [], []
        made = [products(packed, pairs, keys, bias, h, o) for h in range(HEADS_HERE)]
        for _, scores, dprobs, mask in made:
            scores = scores + mask
            top = jnp.maximum(jnp.max(scores, axis=0, keepdims=True), LOWEST)
            weights = jnp.exp2((scores - top) * EXP_SCALE)
            total = jnp.sum(weights, axis=0, keepdims=True)
            weighted = jnp.sum(weights * dprobs, axis=0, keepdims=True)
            log_sums.append(top * EXP_SCALE + jnp.log(total) * LOG2E)
            means.append(jnp.where(total > 0.0, weighted / total, 0.0))
        merged = jnp.concatenate(log_sums + means, axis=0)
        if earlier is None:
            stats[chunk] = merged
            continue
        for peer in range(NZ):
            stats[peer] = earlier[...]
            stats[peer, chunk] = merged


def merge_stats(stats, merged):
    top = stats[0, :, 0:HEADS_HERE, :]
    for i in range(1, NZ):
        top = jnp.maximum(top, stats[i, :, 0:HEADS_HERE, :])
    total = jnp.zeros_like(top)
    mean = jnp.zeros_like(top)
    for i in range(NZ):
        weight = jnp.exp2(stats[i, :, 0:HEADS_HERE, :] - top)
        total = total + weight
        mean = mean + weight * stats[i, :, HEADS_HERE:, :]
    merged[:, 0:HEADS_HERE, :] = top + jnp.log(total) * LOG2E
    merged[:, HEADS_HERE:, :] = mean / total


def query_grad_kernel(order, *refs):
    count = len(order)
    merging = order is LEADING
    near = [o for o in order if o <= REACH]
    chunks, (own, previous, sums, bias_most, bias_last, stats_in), refs = refs[:count], refs[count : count + 6], refs[count + 6 :]
    query_grads, (coarse, window), refs = refs[:count], refs[count : count + 2], refs[count + 2 :]
    merged_out, refs = (refs[0], refs[1:]) if merging else (None, refs)
    packed, pairs, keys, stats, merged, key_sems, chunk_sems, stats_sem = refs
    bias = BiasBlocks((EARLY, bias_most), (LATE, bias_last))
    stats_copy = pltpu.make_async_copy(stats_in, stats, stats_sem)
    stats_copy.start()
    key_copies = load_keys(own, previous, sums, pairs, keys, key_sems)
    copies = []
    for i, o in enumerate(order):
        mine = [pltpu.make_async_copy(chunks[i], packed.at[o], chunk_sems.at[o])]
        for copy in mine:
            copy.start()
        copies.append(mine)
    stats_copy.wait()
    if merging:
        merge_stats(stats, merged)
        merged_out[...] = merged[...]
    else:
        merged = stats
    for copy in key_copies:
        copy.wait()
    _, z = place()
    keys_turned = [
        jnp.transpose(keys[:, 2 * h * HD : (2 * h + 1) * HD]) for h in range(HEADS_HERE)
    ]
    pairs_turned = [
        [jnp.transpose(pairs[i, 0:TOK, h * HD : (h + 1) * HD]) for i in range(2)]
        for h in range(HEADS_HERE)
    ]
    for first in range(0, count, TOGETHER):
        group = range(first, first + TOGETHER)
        for i in group:
            for copy in copies[i]:
                copy.wait()
        units = [(i, order[i], h) for i in group for h in range(HEADS_HERE)]
        made = [products(packed, pairs, keys, bias, h, o) for _, o, h in units]
        low_parts = []
        for (i, o, h), (_, scores, dprobs, mask) in zip(units, made):
            chunk = jnp.bitwise_and(z + o, NZ - 1)
            log_sum = merged[chunk, h : h + 1, :]
            delta = merged[chunk, HEADS_HERE + h : HEADS_HERE + h + 1, :]
            probs = jnp.exp2(scores * EXP_SCALE - log_sum + mask)
            low_parts.append(((probs * (dprobs - delta)).astype(BF16), probs.astype(BF16)))
        for (i, o, h), (dscores, probs_low) in zip(units, low_parts):
            turned = keys_turned[h]
            if o <= REACH:
                side = pairs_turned[h][0]
                if o > 0:
                    side = jnp.where(z + o >= NZ, pairs_turned[h][1], side)
                turned = jnp.concatenate([side, turned], axis=1)
            dquery = jnp.dot(turned, dscores, preferred_element_type=F32)
            turned = jnp.transpose(SCALE * dquery)
            query_grads[i][:, h * HD : (h + 1) * HD] = turned.astype(BF16)
        for (i, o, h), (dscores, probs_low) in zip(units, low_parts):
            if o <= REACH:
                window[near.index(o), 0, h] = dscores[0:TOK]
                window[near.index(o), 1, h] = probs_low[0:TOK]
            coarse[i, 0, h] = dscores[-TOK:]
            coarse[i, 1, h] = probs_low[-TOK:]


def key_grad_kernel(*refs):
    order = ORDER
    near = [o for o in order if o <= REACH]
    chunks, coarse_in, window_in, refs = refs[:NZ], refs[NZ : NZ + 2], refs[NZ + 2 : NZ + 4], refs[NZ + 4 :]
    previous_grad, own_grad, sum_grad, packed, sems = refs
    copies, coarse, window = [], [], {}
    for i, o in enumerate(order):
        part, group = (0, LEADING) if o in LEADING else (1, TRAILING)
        coarse.append(coarse_in[part].at[group.index(o)])
        if o in near:
            window[o] = window_in[part].at[[n for n in group if n <= REACH].index(o)]
        copies.append(pltpu.make_async_copy(chunks[i], packed.at[i], sems.at[i]))
        copies[-1].start()
    _, z = place()
    units = [(h, kind) for h in range(HEADS_HERE) for kind in range(2)]
    zero = jnp.zeros((TOK, HD), F32)
    totals, mine, others = [None] * len(units), [zero] * len(units), [zero] * len(units)
    half = NZ // 2
    for first in range(0, NZ, half):
        group = range(first, first + half)
        for i in group:
            copies[i].wait()
        for unit, (h, kind) in enumerate(units):
            cols = slice(h * HD, (h + 1) * HD)
            tokens = [packed[i, kind * TOK : (kind + 1) * TOK, cols] for i in group]
            part = jnp.dot(
                jnp.concatenate([coarse[i][kind, h] for i in group], axis=1),
                jnp.concatenate(tokens, axis=0),
                preferred_element_type=F32,
            )
            totals[unit] = part if first == 0 else totals[unit] + part
            for i in group:
                if order[i] in near:
                    part = jnp.dot(
                        window[order[i]][kind, h],
                        tokens[i - first],
                        preferred_element_type=F32,
                    )
                    wraps = (z + order[i] >= NZ).astype(F32)
                    mine[unit] = mine[unit] + part * (1.0 - wraps)
                    if order[i] > 0:
                        others[unit] = others[unit] + part * wraps
    for unit, (h, kind) in enumerate(units):
        scale = SCALE if kind == 0 else 1.0
        at = (2 * h + kind) * HD
        here = (slice(kind * TOK, (kind + 1) * TOK), slice(h * HD, (h + 1) * HD))
        own_grad[here] = mine[unit] * scale
        previous_grad[here] = (others[unit] * scale).astype(BF16)
        sum_grad[:, at : at + HD] = (totals[unit] * scale).astype(BF16)


def finish_kernel(starts, slots, own_grad, arrived, parts, grad_keys, grad_values):
    base = starts[0]
    total = parts[0].astype(F32)
    for i in range(1, NXY):
        total = total + parts[i].astype(F32)
    high = total.astype(BF16).astype(F32)
    halves = jnp.concatenate([high, total - high], axis=0).astype(BF16)
    lane = lax.broadcasted_iota(jnp.int32, (2 * BARS_HERE, TOK), 1)
    row = lax.broadcasted_iota(jnp.int32, (2 * BARS_HERE, TOK), 0)
    slot = jnp.full((2 * BARS_HERE, TOK), -1, jnp.int32)
    for b in range(BARS_HERE):
        slot = jnp.where(jnp.bitwise_and(row, BARS_HERE - 1) == b, slots[b] - base, slot)
    placed = lax.dot_general(low(lane == slot), halves, TN, preferred_element_type=F32)
    for h in range(HEADS_HERE):
        cols = slice(h * HD, (h + 1) * HD)
        for kind, out in ((0, grad_keys), (1, grad_values)):
            rows = slice(kind * TOK, (kind + 1) * TOK)
            at = (2 * h + kind) * HD
            grad = own_grad[rows, cols] + arrived[rows, cols].astype(F32)
            out[:, cols] = (grad + placed[:, at : at + HD]).astype(BF16)


def add_low(*parts):
    total = parts[0].astype(F32)
    for part in parts[1:]:
        total = total + part.astype(F32)
    return total.astype(BF16)


def shards(queries, keys, values, grad_y, out_weight, bar_start, related, bar_summary_token):
    params = pltpu.CompilerParams(vmem_limit_bytes=VMEM_LIMIT)
    dma = pltpu.SemaphoreType.DMA
    grad_other = lax.ppermute(grad_y, "head", [(0, 1), (1, 0)])
    half = grad_y.shape[1]
    core = jnp.reshape(lax.axis_index("head"), (1,))
    partial, query_pack, own, sums = pl.pallas_call(
        pack_kernel,
        out_shape=(
            shape((FEAT, TOK), F32),
            shape((ROWS, FEAT)),
            shape((ROWS, FEAT)),
            shape((NXY, BARS_HERE, 2 * FEAT)),
        ),
        in_specs=[whole(SMEM)] * 4 + [whole(HBM)] * 5,
        out_specs=(whole(VMEM),) * 4,
        scratch_shapes=[VMEM((FEAT, half), BF16), VMEM(grad_y.shape, BF16), dma((6,))],
        compiler_params=params,
    )(
        core,
        *pinned(bar_start, related, bar_summary_token),
        *pinned(queries, keys, values, grad_y, out_weight),
    )
    packed = pl.pallas_call(
        grad_pack_kernel,
        out_shape=shape((ROWS, FEAT)),
        in_specs=[whole(SMEM)] + [whole(VMEM)] * 3 + [whole(HBM)],
        out_specs=whole(VMEM),
        scratch_shapes=[VMEM((FEAT, half), BF16), dma],
        compiler_params=params,
    )(
        core,
        *[pltpu.with_memory_space_constraint(x, VMEM) for x in (query_pack, partial)],
        grad_other,
        *pinned(out_weight),
    )

    after, before = [packed], [packed]

    def ring_step():
        after.append(lax.ppermute(after[-1], "seq", TO_PREVIOUS))
        before.append(lax.ppermute(before[-1], "seq", TO_NEXT))

    ring_step()
    all_sums = lax.all_to_all(sums, "seq", 0, 0, axis_index_groups=XY_GROUPS)
    after[1], before[1], all_sums = lax.optimization_barrier((after[1], before[1], all_sums))
    all_sums = all_sums.reshape(NXY * BARS_HERE, 2 * FEAT)
    ring_step()
    previous = lax.ppermute(own, "seq", ROW_UP)
    after[2], before[2], previous = lax.optimization_barrier((after[2], before[2], previous))
    ring_step()
    after.append(lax.ppermute(after[-1], "seq", TO_PREVIOUS))
    chunks = after + before[:0:-1]

    bars = NXY * BARS_HERE
    bias_shape = (REACH + 1 + NZ, TOK, TOK)
    stats_shape = (NZ, NZ, 2 * HEADS_HERE, TOK)
    held = [
        VMEM((NZ, ROWS, FEAT), BF16),
        VMEM((2, ROWS, FEAT), BF16),
        VMEM((bars, 2 * FEAT), BF16),
    ]
    def stats_of(order, *earlier):
        out = (shape(stats_shape, F32),) if earlier else (shape(stats_shape[1:], F32),)
        blocks = (len(bias_blocks(order)),) + bias_shape[1:]
        return pl.pallas_call(
            lambda *refs: stats_kernel(order, *refs),
            out_shape=out + (VMEM(blocks, F32),),
            in_specs=[whole(HBM)] * (len(order) + 3) + [whole(VMEM)] * len(earlier),
            out_specs=(whole(VMEM),) * 2,
            scratch_shapes=held + [dma((3,)), dma((NZ,))],
            compiler_params=params,
        )(*[chunks[o] for o in order], own, previous, all_sums, *earlier)

    partial_stats, bias_most = stats_of(EARLY)
    stats, bias_last = stats_of(LATE, partial_stats)
    bias_most, bias_last = (
        pltpu.with_memory_space_constraint(array, VMEM) for array in (bias_most, bias_last)
    )

    stats = lax.all_to_all(stats, "seq", 0, 0, axis_index_groups=Z_GROUPS)

    def query_grads(order, stats):
        merging = order is LEADING
        near = sum(o <= REACH for o in order)
        coarse_shape = (len(order), 2, HEADS_HERE, bars, TOK)
        window_shape = (near, 2, HEADS_HERE, TOK, TOK)
        made = pl.pallas_call(
            lambda *refs: query_grad_kernel(order, *refs),
            out_shape=(shape((TOK, FEAT)),) * len(order)
            + (VMEM(coarse_shape, BF16), VMEM(window_shape, BF16))
            + (shape(stats_shape[1:], F32),) * merging,
            in_specs=[whole(HBM)] * (len(order) + 3) + [whole(VMEM)] * 2 + [whole(HBM)],
            out_specs=(whole(VMEM),) * (len(order) + 2 + merging),
            scratch_shapes=held
            + [
                VMEM(stats.shape, F32),
                VMEM(stats_shape[1:], F32),
                dma((3,)),
                dma((NZ,)),
                dma,
            ],
            compiler_params=params,
        )(*[chunks[o] for o in order], own, previous, all_sums, bias_most, bias_last, stats)
        *grads, coarse, window, merged = made if merging else (*made, None)
        return dict(zip(order, grads)), coarse, window, merged

    def forward_step(array):
        return lax.ppermute(array, "seq", TO_NEXT)

    def backward_step(array):
        return lax.ppermute(array, "seq", TO_PREVIOUS)

    grads, coarse_a, window_a, merged = query_grads(LEADING, stats)
    forward, backward = forward_step(grads[4]), backward_step(grads[5])
    more, coarse_b, window_b, _ = query_grads(TRAILING, merged)
    grads.update(more)
    forward, backward, coarse_b = lax.optimization_barrier((forward, backward, coarse_b))
    forward, backward = forward_step(add_low(forward, grads[3])), backward_step(add_low(backward, grads[6]))
    previous_grad, own_grad, sum_grad = pl.pallas_call(
        key_grad_kernel,
        out_shape=(
            shape((2 * TOK, FEAT)),
            shape((2 * TOK, FEAT), F32),
            shape((bars, 2 * FEAT)),
        ),
        in_specs=[whole(HBM)] * NZ + [whole(VMEM)] * 4,
        out_specs=(whole(VMEM),) * 3,
        scratch_shapes=[VMEM((NZ, ROWS, FEAT), BF16), dma((NZ,))],
        compiler_params=params,
    )(
        *[chunks[o] for o in ORDER],
        *[
            pltpu.with_memory_space_constraint(x, VMEM)
            for x in (coarse_a, coarse_b, window_a, window_b)
        ],
    )
    forward, backward, sum_grad = lax.optimization_barrier((forward, backward, sum_grad))
    forward = forward_step(forward.astype(F32) + grads[2].astype(F32))
    backward = backward_step(backward.astype(F32) + grads[7].astype(F32))
    arrived = lax.ppermute(previous_grad, "seq", ROW_DOWN)
    parts = lax.all_to_all(
        sum_grad.reshape(NXY, BARS_HERE, 2 * FEAT), "seq", 0, 0, axis_index_groups=XY_GROUPS
    )
    forward = forward_step(add_low(forward, grads[1]))

    grad_keys, grad_values = pl.pallas_call(
        finish_kernel,
        out_shape=(shape((TOK, FEAT)),) * 2,
        in_specs=[whole(SMEM)] * 2 + [whole(VMEM)] * 3,
        out_specs=(whole(VMEM),) * 2,
    )(*pinned(bar_start, bar_summary_token), own_grad, arrived, parts)
    grad_queries = add_low(grads[0], forward, backward)
    return grad_queries, grad_keys, grad_values


def solution(mesh):
    in_specs = (
        P("seq", "head"),
        P("seq", "head"),
        P("seq", "head"),
        P("seq", "head"),
        P("head", None),
        P("seq"),
        P("seq", None),
        P("seq"),
    )
    out_specs = (P("seq", "head"), P("seq", "head"), P("seq", "head"))
    return jax.shard_map(shards, mesh=mesh, in_specs=in_specs, out_specs=out_specs, check_vma=False)
```

```python
import math

import jax
import jax.numpy as jnp
from jax import lax
from jax.experimental import pallas as pl
from jax.experimental.pallas import tpu as pltpu
from jax.sharding import PartitionSpec as P

HD = 128
REACH = 4
TOK = 128
BARS_HERE = 8
HEADS_HERE = 4
FEAT = HD * HEADS_HERE
META = 16
ROWS = 2 * TOK + META
NZ = 8
NY = 4
NX = 4
NXY = NY * NX
N_SEQ = NZ * NXY
OFFSETS = (1, 2, 4, 8, 12, 16, 24, 32)
SCALE = HD ** (-0.5)
LOG2E = math.log2(math.e)
EXP_SCALE = SCALE * LOG2E
LOWEST = -1e30

Z_GROUPS = [[j * NZ + z for z in range(NZ)] for j in range(NXY)]
XY_GROUPS = [[j * NZ + z for j in range(NXY)] for z in range(NZ)]


def route(dy, dx, dz):
    return [
        ((y * NX + x) * NZ + z, ((y + dy) % NY * NX + (x + dx) % NX) * NZ + (z + dz) % NZ)
        for y in range(NY)
        for x in range(NX)
        for z in range(NZ)
    ]


TO_NEXT = route(0, 0, 1)
TO_PREVIOUS = route(0, 0, -1)
ROW_UP = [(i, i + NZ) for i in range(N_SEQ - NZ) if i % NZ >= NZ - REACH]
ROW_DOWN = [(dst, src) for src, dst in ROW_UP]
EARLY = (0, 1, 7, 2, 6, 3, 5)
LATE = (4,)
LEADING = (4, 5)
TRAILING = (3, 6, 2, 7, 1, 0)
ORDER = LEADING + TRAILING
TOGETHER = 3

VMEM_LIMIT = 50 * 2**20
SMEM = pltpu.SMEM
VMEM = pltpu.VMEM
HBM = pltpu.HBM
NT = (((1,), (1,)), ((), ()))
TN = (((0,), (0,)), ((), ()))
BF16 = jnp.bfloat16
F32 = jnp.float32


def whole(space):
    return pl.BlockSpec(memory_space=space)


def shape(dims, dtype=BF16):
    return jax.ShapeDtypeStruct(dims, dtype)


def pinned(*arrays):
    return [pltpu.with_memory_space_constraint(array, HBM) for array in arrays]


def local_bar(starts, positions):
    count = jnp.zeros_like(positions)
    for b in range(1, BARS_HERE):
        count = count + (positions >= starts[b]).astype(jnp.int32)
    return count


def low(flags):
    return flags.astype(F32).astype(BF16)


def pack_kernel(
    core, starts, related, slots, queries, keys, values, grad_own, out_weight,
    partial, query_pack, key_pack, sums, weight, grad, sems,
):
    half = grad_own.shape[1]
    copies = [pltpu.make_async_copy(grad_own, grad, sems.at[0])]
    cols = pl.ds(pl.multiple_of(core[0] * half, half), half)
    copies.append(pltpu.make_async_copy(out_weight.at[:, cols], weight, sems.at[1]))
    copies.append(pltpu.make_async_copy(queries, query_pack.at[pl.ds(0, TOK)], sems.at[3]))
    copies.append(pltpu.make_async_copy(keys, key_pack.at[pl.ds(0, TOK)], sems.at[4]))
    copies.append(pltpu.make_async_copy(values, key_pack.at[pl.ds(TOK, TOK)], sems.at[5]))
    for copy in copies:
        copy.start()
    base = starts[0]
    lane = lax.broadcasted_iota(jnp.int32, (META, TOK), 1)
    row = lax.broadcasted_iota(jnp.int32, (META, TOK), 0)
    bar = local_bar(starts, lane + base)
    info = jnp.where(row == 0, bar, 0)
    for j in range(len(OFFSETS)):
        entry = jnp.zeros((META, TOK), jnp.int32)
        for b in range(BARS_HERE):
            has = (related[b, j] >= 0).astype(jnp.int32)
            entry = jnp.where(bar == b, has, entry)
        info = jnp.where(row == j + 1, entry, info)
    query_pack[TOK:, :] = jnp.zeros((TOK + META, FEAT), BF16)
    query_pack[2 * TOK :, 0:TOK] = low(info)
    key_pack[2 * TOK :, :] = jnp.zeros((META, FEAT), BF16)
    key_pack[2 * TOK :, 0:TOK] = low(bar)
    slot = jnp.full((META, TOK), -1, jnp.int32)
    for b in range(BARS_HERE):
        slot = jnp.where(row == b, slots[b] - base, slot)
    pick = low(lane == slot)
    for copy in copies[2:]:
        copy.wait()
    for kind in range(2):
        source = key_pack[kind * TOK : (kind + 1) * TOK, :]
        rows = jnp.dot(pick, source, preferred_element_type=F32)[0:BARS_HERE].astype(BF16)
        for h in range(HEADS_HERE):
            at = (2 * h + kind) * HD
            for j in range(NXY):
                sums[j, :, at : at + HD] = rows[:, h * HD : (h + 1) * HD]
    for copy in copies[:2]:
        copy.wait()
    partial[...] = lax.dot_general(weight[...], grad[...], NT, preferred_element_type=F32)


def grad_pack_kernel(core, pack, partial, grad_other, out_weight, packed, weight, sem):
    half = grad_other.shape[1]
    cols = pl.ds(pl.multiple_of((1 - core[0]) * half, half), half)
    copy = pltpu.make_async_copy(out_weight.at[:, cols], weight, sem)
    copy.start()
    packed[0:TOK, :] = pack[0:TOK, :]
    packed[2 * TOK :, :] = pack[2 * TOK :, :]
    copy.wait()
    turned = partial[...] + lax.dot_general(
        weight[...], grad_other[...], NT, preferred_element_type=F32
    )
    for h in range(HEADS_HERE):
        cols = slice(h * HD, (h + 1) * HD)
        packed[TOK : 2 * TOK, cols] = jnp.transpose(turned[cols]).astype(BF16)


def place():
    rank = lax.axis_index("seq")
    return rank, jnp.bitwise_and(rank, NZ - 1)


def load_keys(own, previous, sums, pairs, keys, sems):
    copies = [
        pltpu.make_async_copy(own, pairs.at[0], sems.at[0]),
        pltpu.make_async_copy(previous, pairs.at[1], sems.at[1]),
        pltpu.make_async_copy(sums, keys, sems.at[2]),
    ]
    for copy in copies:
        copy.start()
    return copies


class Bias:
    def __init__(self, packed, pairs):
        rank, self.z = place()
        self.row_start = rank - self.z
        self.packed = packed
        self.local = [
            jnp.transpose(
                jnp.broadcast_to(pairs[i, 2 * TOK :, 0:TOK].astype(F32)[0:1], (TOK, TOK))
            ).astype(jnp.int32)
            for i in range(2)
        ]
        self.key_row = lax.broadcasted_iota(jnp.int32, (TOK, TOK), 0)
        self.token_col = lax.broadcasted_iota(jnp.int32, (TOK, TOK), 1)
        owner = lax.shift_right_logical(self.key_row, 3) * NZ + self.z
        self.summary_bar = owner * BARS_HERE + jnp.bitwise_and(self.key_row, BARS_HERE - 1)

    def build(self, o, bias):
        owner = self.row_start + jnp.bitwise_and(self.z + o, NZ - 1)
        info = self.packed[o, 2 * TOK :, 0:TOK].astype(F32).astype(jnp.int32)
        token_bar = info[0:1] + owner * BARS_HERE
        rel = [
            jnp.where(info[j + 1 : j + 2] > 0, token_bar - OFFSETS[j], -1)
            for j in range(len(OFFSETS))
        ]
        if o <= REACH:
            key_owner = owner - o
            key_local = jnp.where(self.z + o >= NZ, self.local[1], self.local[0])
            key_bar = jnp.where(key_owner >= 0, key_local + key_owner * BARS_HERE, -2)
            seen = key_bar == rel[0]
            for entry in rel[1:]:
                seen = seen | (key_bar == entry)
            if o == 0:
                seen = seen | ((key_bar == token_bar) & (self.key_row <= self.token_col))
            bias[o] = jnp.where(seen, 0.0, -jnp.inf)
        hidden = self.summary_bar >= token_bar
        for entry in rel:
            hidden = hidden | (self.summary_bar == entry)
        bias[REACH + 1 + o] = jnp.where(hidden, -jnp.inf, 0.0)


def bias_blocks(order):
    return [o for o in order if o <= REACH] + [REACH + 1 + o for o in order]


def products(packed, pairs, keys, bias, h, o):
    _, z = place()
    cols = slice(h * HD, (h + 1) * HD)
    at = 2 * h * HD
    query = packed[o, 0:TOK, cols]
    grad = packed[o, TOK : 2 * TOK, cols]
    key, value = keys[:, at : at + HD], keys[:, at + HD : at + 2 * HD]
    mask = bias[REACH + 1 + o]
    if o <= REACH:
        side = lax.shift_right_logical(z + o, 3)
        key = jnp.concatenate([pairs[side, 0:TOK, cols], key], axis=0)
        value = jnp.concatenate([pairs[side, TOK : 2 * TOK, cols], value], axis=0)
        mask = jnp.concatenate([bias[o], mask], axis=0)
    scores = lax.dot_general(key, query, NT, preferred_element_type=F32)
    dprobs = lax.dot_general(value, grad, NT, preferred_element_type=F32)
    return key, scores, dprobs, mask


def stats_kernel(order, *refs):
    chunks, (own, previous, sums), refs = refs[: len(order)], refs[len(order) : len(order) + 3], refs[len(order) + 3 :]
    earlier, refs = (refs[0], refs[1:]) if len(order) < REACH else (None, refs)
    stats, bias_out, packed, pairs, keys, bias, key_sems, chunk_sems, bias_sems = refs
    key_copies = load_keys(own, previous, sums, pairs, keys, key_sems)
    copies = [
        pltpu.make_async_copy(chunk, packed.at[o], chunk_sems.at[o])
        for o, chunk in zip(order, chunks)
    ]
    for copy in copies:
        copy.start()
    for copy in key_copies:
        copy.wait()
    masks = Bias(packed, pairs)
    writes = []
    for i, o in enumerate(order):
        copies[i].wait()
        masks.build(o, bias)
        for block in bias_blocks((o,)):
            place_out = bias_out.at[bias_blocks(order).index(block)]
            writes.append(pltpu.make_async_copy(bias.at[block], place_out, bias_sems.at[block]))
            writes[-1].start()
        chunk = jnp.bitwise_and(masks.z + o, NZ - 1)
        log_sums, means = [], []
        made = [products(packed, pairs, keys, bias, h, o) for h in range(HEADS_HERE)]
        for _, scores, dprobs, mask in made:
            scores = scores + mask
            top = jnp.maximum(jnp.max(scores, axis=0, keepdims=True), LOWEST)
            weights = jnp.exp2((scores - top) * EXP_SCALE)
            total = jnp.sum(weights, axis=0, keepdims=True)
            weighted = jnp.sum(weights * dprobs, axis=0, keepdims=True)
            log_sums.append(top * EXP_SCALE + jnp.log(total) * LOG2E)
            means.append(jnp.where(total > 0.0, weighted / total, 0.0))
        merged = jnp.concatenate(log_sums + means, axis=0)
        if earlier is None:
            stats[chunk] = merged
            continue
        for peer in range(NZ):
            stats[peer] = earlier[...]
            stats[peer, chunk] = merged
    for copy in writes:
        copy.wait()


def merge_stats(stats, merged):
    top = stats[0, :, 0:HEADS_HERE, :]
    for i in range(1, NZ):
        top = jnp.maximum(top, stats[i, :, 0:HEADS_HERE, :])
    total = jnp.zeros_like(top)
    mean = jnp.zeros_like(top)
    for i in range(NZ):
        weight = jnp.exp2(stats[i, :, 0:HEADS_HERE, :] - top)
        total = total + weight
        mean = mean + weight * stats[i, :, HEADS_HERE:, :]
    merged[:, 0:HEADS_HERE, :] = top + jnp.log(total) * LOG2E
    merged[:, HEADS_HERE:, :] = mean / total


def query_grad_kernel(order, *refs):
    count = len(order)
    merging = order is LEADING
    near = [o for o in order if o <= REACH]
    chunks, (own, previous, sums, bias_most, bias_last, stats_in), refs = refs[:count], refs[count : count + 6], refs[count + 6 :]
    query_grads, (coarse, window), refs = refs[:count], refs[count : count + 2], refs[count + 2 :]
    merged_out, refs = (refs[0], refs[1:]) if merging else (None, refs)
    packed, pairs, keys, bias, stats, merged, key_sems, chunk_sems, bias_sems, stats_sem = refs
    stats_copy = pltpu.make_async_copy(stats_in, stats, stats_sem)
    stats_copy.start()
    key_copies = load_keys(own, previous, sums, pairs, keys, key_sems)
    copies = []
    for i, o in enumerate(order):
        mine = [pltpu.make_async_copy(chunks[i], packed.at[o], chunk_sems.at[o])]
        for block in bias_blocks((o,)):
            source, among = (bias_most, EARLY) if o in EARLY else (bias_last, LATE)
            source = source.at[bias_blocks(among).index(block)]
            mine.append(pltpu.make_async_copy(source, bias.at[block], bias_sems.at[block]))
        for copy in mine:
            copy.start()
        copies.append(mine)
    stats_copy.wait()
    if merging:
        merge_stats(stats, merged)
        merged_out[...] = merged[...]
    else:
        merged = stats
    for copy in key_copies:
        copy.wait()
    _, z = place()
    keys_turned = [
        jnp.transpose(keys[:, 2 * h * HD : (2 * h + 1) * HD]) for h in range(HEADS_HERE)
    ]
    pairs_turned = [
        [jnp.transpose(pairs[i, 0:TOK, h * HD : (h + 1) * HD]) for i in range(2)]
        for h in range(HEADS_HERE)
    ]
    for first in range(0, count, TOGETHER):
        group = range(first, min(first + TOGETHER, count))
        for i in group:
            for copy in copies[i]:
                copy.wait()
        units = [(i, order[i], h) for i in group for h in range(HEADS_HERE)]
        made = [products(packed, pairs, keys, bias, h, o) for _, o, h in units]
        low_parts = []
        for (i, o, h), (_, scores, dprobs, mask) in zip(units, made):
            chunk = jnp.bitwise_and(z + o, NZ - 1)
            log_sum = merged[chunk, h : h + 1, :]
            delta = merged[chunk, HEADS_HERE + h : HEADS_HERE + h + 1, :]
            probs = jnp.exp2(scores * EXP_SCALE - log_sum + mask)
            low_parts.append(((probs * (dprobs - delta)).astype(BF16), probs.astype(BF16)))
        for (i, o, h), (dscores, probs_low) in zip(units, low_parts):
            turned = keys_turned[h]
            if o <= REACH:
                side = pairs_turned[h][0]
                if o > 0:
                    side = jnp.where(z + o >= NZ, pairs_turned[h][1], side)
                turned = jnp.concatenate([side, turned], axis=1)
            dquery = jnp.dot(turned, dscores, preferred_element_type=F32)
            turned = jnp.transpose(SCALE * dquery)
            query_grads[i][:, h * HD : (h + 1) * HD] = turned.astype(BF16)
        for (i, o, h), (dscores, probs_low) in zip(units, low_parts):
            if o <= REACH:
                window[near.index(o), 0, h] = dscores[0:TOK]
                window[near.index(o), 1, h] = probs_low[0:TOK]
            coarse[i, 0, h] = dscores[-TOK:]
            coarse[i, 1, h] = probs_low[-TOK:]


def key_grad_kernel(*refs):
    order = ORDER
    near = [o for o in order if o <= REACH]
    chunks, coarse_in, window_in, refs = refs[:NZ], refs[NZ : NZ + 2], refs[NZ + 2 : NZ + 4], refs[NZ + 4 :]
    previous_grad, own_grad, sum_grad, packed, sems = refs
    copies, coarse, window = [], [], {}
    for i, o in enumerate(order):
        part, group = (0, LEADING) if o in LEADING else (1, TRAILING)
        coarse.append(coarse_in[part].at[group.index(o)])
        if o in near:
            window[o] = window_in[part].at[[n for n in group if n <= REACH].index(o)]
        copies.append(pltpu.make_async_copy(chunks[i], packed.at[i], sems.at[i]))
        copies[-1].start()
    _, z = place()
    units = [(h, kind) for h in range(HEADS_HERE) for kind in range(2)]
    zero = jnp.zeros((TOK, HD), F32)
    totals, mine, others = [None] * len(units), [zero] * len(units), [zero] * len(units)
    half = NZ // 2
    for first in range(0, NZ, half):
        group = range(first, first + half)
        for i in group:
            copies[i].wait()
        for unit, (h, kind) in enumerate(units):
            cols = slice(h * HD, (h + 1) * HD)
            tokens = [packed[i, kind * TOK : (kind + 1) * TOK, cols] for i in group]
            part = jnp.dot(
                jnp.concatenate([coarse[i][kind, h] for i in group], axis=1),
                jnp.concatenate(tokens, axis=0),
                preferred_element_type=F32,
            )
            totals[unit] = part if first == 0 else totals[unit] + part
            for i in group:
                if order[i] in near:
                    part = jnp.dot(
                        window[order[i]][kind, h],
                        tokens[i - first],
                        preferred_element_type=F32,
                    )
                    wraps = (z + order[i] >= NZ).astype(F32)
                    mine[unit] = mine[unit] + part * (1.0 - wraps)
                    if order[i] > 0:
                        others[unit] = others[unit] + part * wraps
    for unit, (h, kind) in enumerate(units):
        scale = SCALE if kind == 0 else 1.0
        at = (2 * h + kind) * HD
        here = (slice(kind * TOK, (kind + 1) * TOK), slice(h * HD, (h + 1) * HD))
        own_grad[here] = mine[unit] * scale
        previous_grad[here] = (others[unit] * scale).astype(BF16)
        sum_grad[:, at : at + HD] = (totals[unit] * scale).astype(BF16)


def finish_kernel(starts, slots, own_grad, arrived, parts, grad_keys, grad_values):
    base = starts[0]
    total = parts[0].astype(F32)
    for i in range(1, NXY):
        total = total + parts[i].astype(F32)
    high = total.astype(BF16).astype(F32)
    halves = jnp.concatenate([high, total - high], axis=0).astype(BF16)
    lane = lax.broadcasted_iota(jnp.int32, (2 * BARS_HERE, TOK), 1)
    row = lax.broadcasted_iota(jnp.int32, (2 * BARS_HERE, TOK), 0)
    slot = jnp.full((2 * BARS_HERE, TOK), -1, jnp.int32)
    for b in range(BARS_HERE):
        slot = jnp.where(jnp.bitwise_and(row, BARS_HERE - 1) == b, slots[b] - base, slot)
    placed = lax.dot_general(low(lane == slot), halves, TN, preferred_element_type=F32)
    for h in range(HEADS_HERE):
        cols = slice(h * HD, (h + 1) * HD)
        for kind, out in ((0, grad_keys), (1, grad_values)):
            rows = slice(kind * TOK, (kind + 1) * TOK)
            at = (2 * h + kind) * HD
            grad = own_grad[rows, cols] + arrived[rows, cols].astype(F32)
            out[:, cols] = (grad + placed[:, at : at + HD]).astype(BF16)


def add_low(*parts):
    total = parts[0].astype(F32)
    for part in parts[1:]:
        total = total + part.astype(F32)
    return total.astype(BF16)


def shards(queries, keys, values, grad_y, out_weight, bar_start, related, bar_summary_token):
    params = pltpu.CompilerParams(vmem_limit_bytes=VMEM_LIMIT)
    dma = pltpu.SemaphoreType.DMA
    grad_other = lax.ppermute(grad_y, "head", [(0, 1), (1, 0)])
    half = grad_y.shape[1]
    core = jnp.reshape(lax.axis_index("head"), (1,))
    partial, query_pack, own, sums = pl.pallas_call(
        pack_kernel,
        out_shape=(
            shape((FEAT, TOK), F32),
            shape((ROWS, FEAT)),
            shape((ROWS, FEAT)),
            shape((NXY, BARS_HERE, 2 * FEAT)),
        ),
        in_specs=[whole(SMEM)] * 4 + [whole(HBM)] * 5,
        out_specs=(whole(VMEM),) * 4,
        scratch_shapes=[VMEM((FEAT, half), BF16), VMEM(grad_y.shape, BF16), dma((6,))],
        compiler_params=params,
    )(
        core,
        *pinned(bar_start, related, bar_summary_token),
        *pinned(queries, keys, values, grad_y, out_weight),
    )
    packed = pl.pallas_call(
        grad_pack_kernel,
        out_shape=shape((ROWS, FEAT)),
        in_specs=[whole(SMEM)] + [whole(VMEM)] * 3 + [whole(HBM)],
        out_specs=whole(VMEM),
        scratch_shapes=[VMEM((FEAT, half), BF16), dma],
        compiler_params=params,
    )(
        core,
        *[pltpu.with_memory_space_constraint(x, VMEM) for x in (query_pack, partial)],
        grad_other,
        *pinned(out_weight),
    )

    after, before = [packed], [packed]

    def ring_step():
        after.append(lax.ppermute(after[-1], "seq", TO_PREVIOUS))
        before.append(lax.ppermute(before[-1], "seq", TO_NEXT))

    ring_step()
    all_sums = lax.all_to_all(sums, "seq", 0, 0, axis_index_groups=XY_GROUPS)
    after[1], before[1], all_sums = lax.optimization_barrier((after[1], before[1], all_sums))
    all_sums = all_sums.reshape(NXY * BARS_HERE, 2 * FEAT)
    ring_step()
    previous = lax.ppermute(own, "seq", ROW_UP)
    after[2], before[2], previous = lax.optimization_barrier((after[2], before[2], previous))
    ring_step()
    after.append(lax.ppermute(after[-1], "seq", TO_PREVIOUS))
    chunks = after + before[:0:-1]

    bars = NXY * BARS_HERE
    bias_shape = (REACH + 1 + NZ, TOK, TOK)
    stats_shape = (NZ, NZ, 2 * HEADS_HERE, TOK)
    held = [
        VMEM((NZ, ROWS, FEAT), BF16),
        VMEM((2, ROWS, FEAT), BF16),
        VMEM((bars, 2 * FEAT), BF16),
        VMEM(bias_shape, F32),
    ]
    def stats_of(order, *earlier):
        out = (shape(stats_shape, F32),) if earlier else (shape(stats_shape[1:], F32),)
        blocks = (len(bias_blocks(order)),) + bias_shape[1:]
        return pl.pallas_call(
            lambda *refs: stats_kernel(order, *refs),
            out_shape=out + (shape(blocks, F32),),
            in_specs=[whole(HBM)] * (len(order) + 3) + [whole(VMEM)] * len(earlier),
            out_specs=(whole(VMEM), whole(HBM)),
            scratch_shapes=held + [dma((3,)), dma((NZ,)), dma(bias_shape[:1])],
            compiler_params=params,
        )(*[chunks[o] for o in order], own, previous, all_sums, *earlier)

    partial_stats, bias_most = stats_of(EARLY)
    stats, bias_last = stats_of(LATE, partial_stats)

    stats = lax.all_to_all(stats, "seq", 0, 0, axis_index_groups=Z_GROUPS)

    def query_grads(order, stats):
        merging = order is LEADING
        near = sum(o <= REACH for o in order)
        coarse_shape = (len(order), 2, HEADS_HERE, bars, TOK)
        window_shape = (near, 2, HEADS_HERE, TOK, TOK)
        made = pl.pallas_call(
            lambda *refs: query_grad_kernel(order, *refs),
            out_shape=(shape((TOK, FEAT)),) * len(order)
            + (VMEM(coarse_shape, BF16), VMEM(window_shape, BF16))
            + (shape(stats_shape[1:], F32),) * merging,
            in_specs=[whole(HBM)] * (len(order) + 6),
            out_specs=(whole(VMEM),) * (len(order) + 2 + merging),
            scratch_shapes=held
            + [
                VMEM(stats.shape, F32),
                VMEM(stats_shape[1:], F32),
                dma((3,)),
                dma((NZ,)),
                dma(bias_shape[:1]),
                dma,
            ],
            compiler_params=params,
        )(*[chunks[o] for o in order], own, previous, all_sums, bias_most, bias_last, stats)
        *grads, coarse, window, merged = made if merging else (*made, None)
        return dict(zip(order, grads)), coarse, window, merged

    def forward_step(array):
        return lax.ppermute(array, "seq", TO_NEXT)

    def backward_step(array):
        return lax.ppermute(array, "seq", TO_PREVIOUS)

    grads, coarse_a, window_a, merged = query_grads(LEADING, stats)
    forward, backward = forward_step(grads[4]), backward_step(grads[5])
    more, coarse_b, window_b, _ = query_grads(TRAILING, merged)
    grads.update(more)
    forward, backward, coarse_b = lax.optimization_barrier((forward, backward, coarse_b))
    forward, backward = forward_step(add_low(forward, grads[3])), backward_step(add_low(backward, grads[6]))
    previous_grad, own_grad, sum_grad = pl.pallas_call(
        key_grad_kernel,
        out_shape=(
            shape((2 * TOK, FEAT)),
            shape((2 * TOK, FEAT), F32),
            shape((bars, 2 * FEAT)),
        ),
        in_specs=[whole(HBM)] * NZ + [whole(VMEM)] * 4,
        out_specs=(whole(VMEM),) * 3,
        scratch_shapes=[VMEM((NZ, ROWS, FEAT), BF16), dma((NZ,))],
        compiler_params=params,
    )(
        *[chunks[o] for o in ORDER],
        *[
            pltpu.with_memory_space_constraint(x, VMEM)
            for x in (coarse_a, coarse_b, window_a, window_b)
        ],
    )
    forward, backward, sum_grad = lax.optimization_barrier((forward, backward, sum_grad))
    forward = forward_step(forward.astype(F32) + grads[2].astype(F32))
    backward = backward_step(backward.astype(F32) + grads[7].astype(F32))
    arrived = lax.ppermute(previous_grad, "seq", ROW_DOWN)
    parts = lax.all_to_all(
        sum_grad.reshape(NXY, BARS_HERE, 2 * FEAT), "seq", 0, 0, axis_index_groups=XY_GROUPS
    )
    forward = forward_step(add_low(forward, grads[1]))

    grad_keys, grad_values = pl.pallas_call(
        finish_kernel,
        out_shape=(shape((TOK, FEAT)),) * 2,
        in_specs=[whole(SMEM)] * 2 + [whole(VMEM)] * 3,
        out_specs=(whole(VMEM),) * 2,
    )(*pinned(bar_start, bar_summary_token), own_grad, arrived, parts)
    grad_queries = add_low(grads[0], forward, backward)
    return grad_queries, grad_keys, grad_values


def solution(mesh):
    in_specs = (
        P("seq", "head"),
        P("seq", "head"),
        P("seq", "head"),
        P("seq", "head"),
        P("head", None),
        P("seq"),
        P("seq", None),
        P("seq"),
    )
    out_specs = (P("seq", "head"), P("seq", "head"), P("seq", "head"))
    return jax.shard_map(shards, mesh=mesh, in_specs=in_specs, out_specs=out_specs, check_vma=False)
```
